512 devices in a mesh: src: 16 (over z), tgt: 32 (over x, y, core).
Axes of the slice: x: 4, y: 4, z: 16, core: 2. Of those that a mesh axis runs over, the one named last changes fastest.
Arguments:
- source_embed: bfloat16 [32768, 256], P('src'), may hold values from -0.375 to 0.375
- target_embed: bfloat16 [32768, 256], P('tgt'), may hold values from -0.375 to 0.375
- target_feat: bfloat16 [32768, 128], P('tgt'), may hold values from -6 to 6
- source_mass: float32 [32768], P('src'), may hold values from 0.05 to 20
- target_mass: float32 [32768], P('tgt'), may hold values from 0.05 to 20
Outputs:
- source_potential: float32 [32768], P('src')
- target_potential: float32 [32768], P('tgt')
- projected: float32 [32768, 128], P(('src', 'tgt'))
The draws below stay inside these ranges and needn't reach their ends.
All inputs are finite; a program needn't handle non-finite values.
Results may differ from the reference program's by a relative error of at most 0.001.
Values sent between devices are 32-bit elements; how exact they have to be, the bound alone decides.
No kernel may reach another device: no remote copies, remote signals or barrier semaphores. Data moves between devices by JAX's collectives and lax.ppermute only.
A program may use at most 192 MiB of HBM per device.

```python
import math
import jax
import jax.numpy as jnp
from jax import lax

S_DEV = 2048
T_DEV = 1024
DIM = 256
FEAT = 128
ITERS = 2
NS = 32768
NT = 32768
N_TGT = 32


def draw_source_embed(key, part):
    key = jax.random.fold_in(key, 3)
    first = jax.random.fold_in(key, 0)
    values = jnp.clip(jax.random.normal(first, (NS, DIM), jnp.float32) * 0.0625, -0.375, 0.375)
    return values.astype(jnp.bfloat16)


def block_scale(rng, dims, cuts, low, largest):
    level, own = 1.0, jax.random.fold_in(rng, 6)
    for position, parts in cuts:
        steps = jnp.exp(jax.random.uniform(jax.random.fold_in(own, position), (parts,), jnp.float32, low / len(cuts), largest / len(cuts)))
        level = level * jnp.repeat(steps, dims[position] // parts).reshape([-1 if axis == position else 1 for axis in range(len(dims))])
    return level


def noise(stream_key, dims, scale, reach, cuts=(), held_as=jnp.bfloat16):
    drawn = scale * jax.random.normal(stream_key, dims, jnp.float32)
    if cuts:
        drawn = drawn * block_scale(stream_key, dims, cuts, -0.22, 0.18)
    return jnp.clip(drawn, -reach, reach).astype(held_as)


def setup_inputs(seed: int = 0) -> dict:
    key_list = jax.random.split(jax.random.key(seed), 6)
    return {
        "source_embed": draw_source_embed(jax.random.fold_in(key_list[5], 71), 0),
        "target_embed": noise(key_list[1], (NT, DIM), 0.0625, 0.375, ((0, 32),)),
        "target_feat": noise(key_list[2], (NT, FEAT), 1.0, 6.0, ((0, 32),)),
        "source_mass": jnp.clip(jnp.exp(math.log(20.0) - 5.9914645 * jax.random.uniform(key_list[3], (NS,), jnp.float32) ** block_scale(key_list[3], (NS,), ((0, 16),), -0.2, 0.2)), 0.05, 20.0),
        "target_mass": jnp.clip(jnp.exp(math.log(20.0) - 5.9914645 * jax.random.uniform(key_list[4], (NT,), jnp.float32) ** block_scale(key_list[4], (NT,), ((0, 32),), -0.2, 0.2)), 0.05, 20.0),
    }


ENTROPY = 0.05


def reference(source_embed, target_embed, target_feat, source_mass, target_mass):
    blocks = NS // S_DEV
    src_blocks = source_embed.reshape(blocks, S_DEV, DIM)
    mass_blocks = source_mass.reshape(blocks, S_DEV)
    tgt = target_embed.astype(jnp.float32)
    sq_tgt = jnp.sum(tgt * tgt, axis=1)
    log_tgt = ENTROPY * jnp.log(target_mass)
    feat_blocks = target_feat.reshape(N_TGT, T_DEV, FEAT)

    def block_cost(block):
        xb = block.astype(jnp.float32)
        sq_src = jnp.sum(xb * xb, axis=1)
        cross = jnp.dot(xb, tgt.T, precision=lax.Precision.HIGHEST)
        return sq_src[:, None] + sq_tgt[None, :] - 2.0 * cross

    def column_pass(pot):
        pot_blocks = pot.reshape(blocks, S_DEV)

        def step(carry, item):
            top, total = carry
            block, part = item
            scores = (part[:, None] - block_cost(block)) / ENTROPY
            newtop = jnp.maximum(top, jnp.max(scores, axis=0))
            total = total * jnp.exp(top - newtop) + jnp.sum(jnp.exp(scores - newtop[None, :]), axis=0)
            return (newtop, total), None

        init = (jnp.full((NT,), -1e30, jnp.float32), jnp.zeros((NT,), jnp.float32))
        (top, total), _ = lax.scan(step, init, (src_blocks, pot_blocks))
        return log_tgt - ENTROPY * (top + jnp.log(total))

    def row_pass(target_pot, project):
        def one_block(item):
            block, mass = item
            cost = block_cost(block)
            scores = (target_pot[None, :] - cost) / ENTROPY
            top = jnp.max(scores, axis=1)
            total = jnp.sum(jnp.exp(scores - top[:, None]), axis=1)
            pot = ENTROPY * jnp.log(mass) - ENTROPY * (top + jnp.log(total))
            if project:
                split = scores.reshape(S_DEV, N_TGT, T_DEV)
                block_top = jnp.max(split, axis=2)
                weights = jnp.exp(split - block_top[:, :, None]).astype(jnp.bfloat16)
                numer = jnp.einsum("ibj,bjf->ibf", weights.astype(jnp.float32), feat_blocks.astype(jnp.float32))
                scale = jnp.exp(block_top - top[:, None])
                summed = jnp.sum(numer * scale[:, :, None], axis=1)
                return pot, summed / total[:, None]
            return pot, jnp.zeros((S_DEV, 1), jnp.float32)

        pots, projs = lax.map(one_block, (src_blocks, mass_blocks))
        return pots.reshape(NS), projs

    source_pot = jnp.zeros((NS,), jnp.float32)
    target_pot = jnp.zeros((NT,), jnp.float32)
    projected = None
    for step_index in range(ITERS):
        target_pot = column_pass(source_pot)
        last = step_index == ITERS - 1
        source_pot, projs = row_pass(target_pot, last)
        if last:
            projected = projs.reshape(NS, FEAT)
    return source_pot, target_pot, projected
```

```python
import jax
import jax.numpy as jnp
from jax import lax
from jax.sharding import PartitionSpec as P

ITERS = 2
ENTROPY = 0.05


def tile_cost(source_embed, target_embed):
    sq_src = jnp.sum(jnp.square(source_embed.astype(jnp.float32)), axis=1)
    sq_tgt = jnp.sum(jnp.square(target_embed.astype(jnp.float32)), axis=1)
    cross = lax.dot_general(
        source_embed, target_embed, (((1,), (1,)), ((), ())), preferred_element_type=jnp.float32
    )
    return sq_src[:, None] + sq_tgt[None, :] - 2.0 * cross


def merge_blocks(parts):
    top = jnp.max(parts, axis=0)
    return top + jnp.log(jnp.sum(jnp.exp(parts - top[None, :]), axis=0))


def merge_pair(a, b):
    return jnp.maximum(a, b) + jnp.log1p(jnp.exp(-jnp.abs(a - b)))


def swap(value, axis, mask):
    n = lax.axis_size(axis)
    return lax.ppermute(value, axis, [(i, i ^ mask) for i in range(n)])


def gather_all(value, axis):
    return lax.all_gather(value, axis)


def gather_exchange(value, axis):
    n = lax.axis_size(axis)
    return lax.all_to_all(jnp.broadcast_to(value[None], (n,) + value.shape), axis, 0, 0)


def merge_direct(value, axis):
    parts = [value] + [swap(value, axis, k) for k in range(1, lax.axis_size(axis))]
    top = parts[0]
    for part in parts[1:]:
        top = jnp.maximum(top, part)
    sums = [jnp.exp(part - top) for part in parts]
    while len(sums) > 1:
        sums = [a + b for a, b in zip(sums[::2], sums[1::2])]
    return top + jnp.log(sums[0])


def merge_doubling(value, axis, masks):
    for mask in masks:
        value = merge_pair(value, swap(value, axis, mask))
    return value


def local(source_embed, target_embed, target_feat, source_mass, target_mass):
    cost = tile_cost(source_embed, target_embed)
    log_src = ENTROPY * jnp.log(source_mass)
    log_tgt = ENTROPY * jnp.log(target_mass)
    n_tgt = lax.axis_size("tgt")
    share = source_mass.shape[0] // n_tgt

    def columns(pot):
        scores = (pot[:, None] - cost) / ENTROPY
        top = jnp.max(scores, axis=0)
        return top + jnp.log(jnp.sum(jnp.exp(scores - top[None, :]), axis=0))

    def rows(pot):
        scores = (pot[None, :] - cost) / ENTROPY
        top = jnp.max(scores, axis=1)
        expo = jnp.exp(scores - top[:, None])
        total = jnp.sum(expo, axis=1)
        return top + jnp.log(total), expo, total

    lse = merge_blocks(gather_all(columns(jnp.zeros_like(source_mass)), "src"))
    target_pot = log_tgt - ENTROPY * lse
    part, _, _ = rows(target_pot)
    lse = merge_blocks(gather_exchange(part, "tgt"))
    source_pot = log_src - ENTROPY * lse

    lse = merge_direct(columns(source_pot), "src")
    target_pot = log_tgt - ENTROPY * lse
    part, expo, total = rows(target_pot)
    numer = jnp.dot(expo.astype(jnp.bfloat16), target_feat, preferred_element_type=jnp.float32)
    mean = (numer / total[:, None]).reshape(n_tgt, share, -1)
    whole = merge_doubling(part, "tgt", (1, 2, 6, 8, 24))
    source_pot = log_src - ENTROPY * whole
    scale = jnp.exp(part - whole).reshape(n_tgt, share)
    projected = jnp.sum(lax.all_to_all(mean * scale[:, :, None], "tgt", 0, 0), axis=0)
    return (source_pot, target_pot, projected)


def solution(mesh):
    placed = (P("src", None), P("tgt", None), P("tgt", None), P("src"), P("tgt"))
    return jax.shard_map(
        local,
        mesh=mesh,
        in_specs=placed,
        out_specs=(P("src"), P("tgt"), P(("src", "tgt"), None)),
        check_vma=False,
    )
```

```python
import jax
import jax.numpy as jnp
from jax import lax
from jax.sharding import PartitionSpec as P

ITERS = 2
ENTROPY = 0.05


def tile_cost(source_embed, target_embed):
    sq_src = jnp.sum(jnp.square(source_embed.astype(jnp.float32)), axis=1)
    sq_tgt = jnp.sum(jnp.square(target_embed.astype(jnp.float32)), axis=1)
    cross = lax.dot_general(
        source_embed, target_embed, (((1,), (1,)), ((), ())), preferred_element_type=jnp.float32
    )
    return sq_src[:, None] + sq_tgt[None, :] - 2.0 * cross


def merge_blocks(parts):
    top = jnp.max(parts, axis=0)
    return top + jnp.log(jnp.sum(jnp.exp(parts - top[None, :]), axis=0))


def spread(value, axis, groups=None):
    n = lax.axis_size(axis) if groups is None else len(groups[0])
    return lax.all_to_all(
        jnp.broadcast_to(value[None], (n,) + value.shape), axis, 0, 0, axis_index_groups=groups
    )


def merge_all(value, axis):
    return merge_blocks(spread(value, axis))


def merge_steps(value, axis, inner):
    n = lax.axis_size(axis)
    near = [list(range(k, k + inner)) for k in range(0, n, inner)]
    far = [list(range(k, n, inner)) for k in range(inner)]
    return merge_blocks(spread(merge_blocks(spread(value, axis, near)), axis, far))


def local(source_embed, target_embed, target_feat, source_mass, target_mass):
    cost = tile_cost(source_embed, target_embed)
    log_src = ENTROPY * jnp.log(source_mass)
    log_tgt = ENTROPY * jnp.log(target_mass)
    n_tgt = lax.axis_size("tgt")
    share = source_mass.shape[0] // n_tgt

    def columns(pot):
        scores = (pot[:, None] - cost) / ENTROPY
        top = jnp.max(scores, axis=0)
        return top + jnp.log(jnp.sum(jnp.exp(scores - top[None, :]), axis=0))

    def rows(pot):
        scores = (pot[None, :] - cost) / ENTROPY
        top = jnp.max(scores, axis=1)
        expo = jnp.exp(scores - top[:, None])
        total = jnp.sum(expo, axis=1)
        return top + jnp.log(total), expo, total

    lse = merge_all(columns(jnp.zeros_like(source_mass)), "src")
    target_pot = log_tgt - ENTROPY * lse
    part, _, _ = rows(target_pot)
    lse = merge_steps(part, "tgt", 8)
    source_pot = log_src - ENTROPY * lse

    lse = merge_steps(columns(source_pot), "src", 4)
    target_pot = log_tgt - ENTROPY * lse
    part, expo, total = rows(target_pot)
    numer = jnp.dot(expo.astype(jnp.bfloat16), target_feat, preferred_element_type=jnp.float32)
    mean = (numer / total[:, None]).reshape(n_tgt, share, -1)
    width = mean.shape[-1]
    tail = jnp.broadcast_to(part.reshape(1, -1, width), (n_tgt, part.shape[0] // width, width))
    landed = lax.all_to_all(jnp.concatenate([mean, tail], axis=1), "tgt", 0, 0)
    parts = landed[:, share:, :].reshape(n_tgt, -1)
    whole = merge_blocks(parts)
    source_pot = log_src - ENTROPY * whole
    start = lax.axis_index("tgt") * share
    scale = jnp.exp(
        lax.dynamic_slice_in_dim(parts, start, share, 1)
        - lax.dynamic_slice_in_dim(whole, start, share, 0)[None, :]
    )
    projected = jnp.sum(landed[:, :share, :] * scale[:, :, None], axis=0)
    return (source_pot, target_pot, projected)


def solution(mesh):
    placed = (P("src", None), P("tgt", None), P("tgt", None), P("src"), P("tgt"))
    return jax.shard_map(
        local,
        mesh=mesh,
        in_specs=placed,
        out_specs=(P("src"), P("tgt"), P(("src", "tgt"), None)),
        check_vma=False,
    )
```

```python
import math

import jax
import jax.numpy as jnp
from jax import lax
from jax.experimental import pallas as pl
from jax.experimental.pallas import tpu as pltpu
from jax.sharding import PartitionSpec as P

ENTROPY = 0.05
LANES = 128
WIDTH = 256
TWO_SCALE = 2.0 / ENTROPY * math.log2(math.e)
ONE_SCALE = 1.0 / ENTROPY * math.log2(math.e)
NT = (((1,), (1,)), ((), ()))
NN = (((1,), (0,)), ((), ()))
VMEM_LIMIT = 40 * 1024 * 1024


def merge(parts):
    top = jnp.max(parts, axis=0)
    total = jnp.sum(jnp.exp2((parts - top[None]) * ONE_SCALE), axis=0)
    return top + ENTROPY * jnp.log(total)


def lanes_to_rows(values, col_ref):
    for k in range(values.shape[0]):
        square = jnp.broadcast_to(values[k : k + 1, :], (LANES, LANES))
        col_ref[pl.ds(k * LANES, LANES), :] = square.T


def chunk_scores(p_ref, q_ref, col_ref, z_ref, t):
    z = lax.dot_general(
        p_ref[...], q_ref[pl.ds(t * WIDTH, WIDTH), :], NT, preferred_element_type=jnp.float32
    )
    tops = []
    for h in range(WIDTH // LANES):
        part = z[:, h * LANES : (h + 1) * LANES] + col_ref[...]
        z_ref[:, pl.ds(t * WIDTH + h * LANES, LANES)] = part
        tops.append(jnp.max(jnp.max(part.reshape(-1, 8, LANES), axis=0), axis=0, keepdims=True))
    return tops


def chunk_weights(z_ref, t, h, top):
    part = z_ref[:, pl.ds(t * WIDTH + h * LANES, LANES)]
    weights = jnp.exp2((part - top) * TWO_SCALE)
    total = jnp.sum(jnp.sum(weights.reshape(-1, 8, LANES), axis=0), axis=0, keepdims=True)
    return weights, total


def log_sums(p_ref, q_ref, col_ref, z_ref, row_ref):
    for t in range(q_ref.shape[0] // WIDTH):
        tops = chunk_scores(p_ref, q_ref, col_ref, z_ref, t)
        for h, top in enumerate(tops):
            _, total = chunk_weights(z_ref, t, h, top)
            row = t * (WIDTH // LANES) + h
            row_ref[pl.ds(row, 1), :] = 2.0 * top + ENTROPY * jnp.log(total)


def first_kernel(p_ref, q_ref, out_ref, col_ref, z_ref, row_ref):
    p = p_ref[...].astype(jnp.float32)
    half = -0.5 * jnp.sum(p * p, axis=1, keepdims=True)
    col_ref[...] = jnp.broadcast_to(half, col_ref.shape)
    log_sums(p_ref, q_ref, col_ref, z_ref, row_ref)
    out_ref[...] = jnp.broadcast_to(row_ref[...][None], out_ref.shape)


def next_kernel(parts_ref, mass_ref, p_ref, q_ref, out_ref, col_ref, z_ref, row_ref):
    bias = ENTROPY * jnp.log(mass_ref[...]) - merge(parts_ref[...])
    lanes_to_rows(0.5 * bias, col_ref)
    log_sums(p_ref, q_ref, col_ref, z_ref, row_ref)
    out_ref[...] = jnp.broadcast_to(row_ref[...][None], out_ref.shape)


def last_kernel(
    parts_ref, mass_ref, p_ref, q_ref, feat_ref, out_ref, bias_ref, col_ref, z_ref, row_ref, flip_ref
):
    share = out_ref.shape[1] - row_ref.shape[0]
    bias = ENTROPY * jnp.log(mass_ref[...]) - merge(parts_ref[...])
    bias_ref[...] = bias
    lanes_to_rows(0.5 * bias, col_ref)
    flip_ref[...] = feat_ref[...].astype(jnp.float32).T.astype(jnp.bfloat16)
    for t in range(q_ref.shape[0] // WIDTH):
        tops = chunk_scores(p_ref, q_ref, col_ref, z_ref, t)
        weights, totals = [], []
        for h, top in enumerate(tops):
            weight, total = chunk_weights(z_ref, t, h, top)
            weights.append(weight.astype(jnp.bfloat16))
            totals.append(total)
            row_ref[pl.ds(t * (WIDTH // LANES) + h, 1), :] = 2.0 * top + ENTROPY * jnp.log(total)
        numer = lax.dot_general(
            flip_ref[...], jnp.concatenate(weights, axis=1), NN, preferred_element_type=jnp.float32
        )
        mean = numer / jnp.concatenate(totals, axis=1)
        for h in range(WIDTH // LANES):
            block = mean[:, h * LANES : (h + 1) * LANES].T
            first = (t * WIDTH + h * LANES) // share
            out_ref[pl.ds(first, LANES // share), pl.ds(0, share), :] = block.reshape(
                LANES // share, share, LANES
            )
    rows = row_ref.shape[0]
    out_ref[:, pl.ds(share, rows), :] = jnp.broadcast_to(
        row_ref[...][None], (out_ref.shape[0], rows, LANES)
    )


def scratch(p, q):
    return [
        pltpu.VMEM((p.shape[0], LANES), jnp.float32),
        pltpu.VMEM((p.shape[0], q.shape[0]), jnp.float32),
        pltpu.VMEM((q.shape[0] // LANES, LANES), jnp.float32),
    ]


def call(kernel, args, outs, scratch_shapes):
    whole = pl.BlockSpec(memory_space=pltpu.VMEM)
    return pl.pallas_call(
        kernel,
        out_shape=outs,
        in_specs=[whole] * len(args),
        out_specs=jax.tree.map(lambda _: whole, outs),
        scratch_shapes=scratch_shapes,
        compiler_params=pltpu.CompilerParams(vmem_limit_bytes=VMEM_LIMIT),
    )(*args)


def local(source_embed, target_embed, target_feat, source_mass, target_mass):
    n_src, n_tgt = lax.axis_size("src"), lax.axis_size("tgt")
    share = source_mass.shape[0] // n_tgt
    src_mass = source_mass.reshape(-1, LANES)
    tgt_mass = target_mass.reshape(-1, LANES)
    src_rows, tgt_rows = src_mass.shape[0], tgt_mass.shape[0]
    f32 = jnp.float32
    to_src = jax.ShapeDtypeStruct((n_src, tgt_rows, LANES), f32)
    to_tgt = jax.ShapeDtypeStruct((n_tgt, src_rows, LANES), f32)
    by_src = scratch(source_embed, target_embed)
    by_tgt = scratch(target_embed, source_embed)

    sent = call(first_kernel, (source_embed, target_embed), to_src, by_src)
    parts = lax.all_to_all(sent, "src", 0, 0)
    sent = call(next_kernel, (parts, tgt_mass, target_embed, source_embed), to_tgt, by_tgt)
    parts = lax.all_to_all(sent, "tgt", 0, 0)
    sent = call(next_kernel, (parts, src_mass, source_embed, target_embed), to_src, by_src)
    parts = lax.all_to_all(sent, "src", 0, 0)
    width = target_feat.shape[1]
    sent, bias = call(
        last_kernel,
        (parts, tgt_mass, target_embed, source_embed, target_feat),
        (
            jax.ShapeDtypeStruct((n_tgt, share + src_rows, width), f32),
            jax.ShapeDtypeStruct((tgt_rows, LANES), f32),
        ),
        by_tgt + [pltpu.VMEM(target_feat.shape[::-1], jnp.bfloat16)],
    )
    sq_tgt = jnp.sum(jnp.square(target_embed.astype(f32)), axis=1)
    target_pot = bias.reshape(-1) + sq_tgt
    landed = lax.all_to_all(sent, "tgt", 0, 0)

    parts = landed[:, share:, :].reshape(n_tgt, -1)
    whole = merge(parts)
    sq_src = jnp.sum(jnp.square(source_embed.astype(f32)), axis=1)
    source_pot = ENTROPY * jnp.log(source_mass) - whole + sq_src
    start = lax.axis_index("tgt") * share
    scale = jnp.exp2(
        ONE_SCALE
        * (
            lax.dynamic_slice_in_dim(parts, start, share, 1)
            - lax.dynamic_slice_in_dim(whole, start, share, 0)[None, :]
        )
    )
    projected = jnp.sum(landed[:, :share, :] * scale[:, :, None], axis=0)
    return (source_pot, target_pot, projected)


def solution(mesh):
    placed = (P("src", None), P("tgt", None), P("tgt", None), P("src"), P("tgt"))
    return jax.shard_map(
        local,
        mesh=mesh,
        in_specs=placed,
        out_specs=(P("src"), P("tgt"), P(("src", "tgt"), None)),
        check_vma=False,
    )
```

```python
import math

import jax
import jax.numpy as jnp
from jax import lax
from jax.experimental import pallas as pl
from jax.experimental.pallas import tpu as pltpu
from jax.sharding import PartitionSpec as P

ENTROPY = 0.05
LANES = 128
WIDTH = 256
TWO_SCALE = 2.0 / ENTROPY * math.log2(math.e)
ONE_SCALE = 1.0 / ENTROPY * math.log2(math.e)
NT = (((1,), (1,)), ((), ()))
NN = (((1,), (0,)), ((), ()))
PIECES = 4
VMEM_LIMIT = 40 * 1024 * 1024


def merge(parts):
    top = jnp.max(parts, axis=0)
    total = jnp.sum(jnp.exp2((parts - top[None]) * ONE_SCALE), axis=0)
    return top + ENTROPY * jnp.log(total)


def lanes_to_rows(values, col_ref):
    for k in range(values.shape[0]):
        square = jnp.broadcast_to(values[k : k + 1, :], (LANES, LANES))
        col_ref[pl.ds(k * LANES, LANES), :] = square.T


def chunk_scores(p_ref, q, col_ref, z_ref, t):
    z = lax.dot_general(p_ref[...], q, NT, preferred_element_type=jnp.float32)
    tops = []
    for h in range(WIDTH // LANES):
        part = z[:, h * LANES : (h + 1) * LANES] + col_ref[...]
        z_ref[:, pl.ds(t * WIDTH + h * LANES, LANES)] = part
        tops.append(jnp.max(jnp.max(part.reshape(-1, 8, LANES), axis=0), axis=0, keepdims=True))
    return tops


def chunk_weights(z_ref, t, h, top):
    part = z_ref[:, pl.ds(t * WIDTH + h * LANES, LANES)]
    weights = jnp.exp2((part - top) * TWO_SCALE)
    total = jnp.sum(jnp.sum(weights.reshape(-1, 8, LANES), axis=0), axis=0, keepdims=True)
    return weights, total


def log_sums(p_ref, q_ref, col_ref, z_ref, row_ref):
    for t in range(q_ref.shape[0] // WIDTH):
        tops = chunk_scores(p_ref, q_ref[pl.ds(t * WIDTH, WIDTH), :], col_ref, z_ref, t)
        for h, top in enumerate(tops):
            _, total = chunk_weights(z_ref, t, h, top)
            row = t * (WIDTH // LANES) + h
            row_ref[pl.ds(row, 1), :] = 2.0 * top + ENTROPY * jnp.log(total)


def first_kernel(p_hbm, q_hbm, out_ref, p_ref, q_ref, p_sems, q_sems, col_ref, z_ref, row_ref):
    rows = p_ref.shape[0] // PIECES
    copies = []
    for k in range(PIECES):
        part = pl.ds(k * rows, rows)
        copies.append(pltpu.make_async_copy(p_hbm.at[part, :], p_ref.at[part, :], p_sems.at[k]))
    load_q = pltpu.make_async_copy(q_hbm, q_ref, q_sems.at[0])
    for copy in copies:
        copy.start()
    load_q.start()
    for k, copy in enumerate(copies):
        copy.wait()
        part = pl.ds(k * rows, rows)
        p = p_ref[part, :].astype(jnp.float32)
        half = -0.5 * jnp.sum(p * p, axis=1, keepdims=True)
        col_ref[part, :] = jnp.broadcast_to(half, (rows, LANES))
    load_q.wait()
    log_sums(p_ref, q_ref, col_ref, z_ref, row_ref)
    out_ref[...] = jnp.broadcast_to(row_ref[...][None], out_ref.shape)


def next_kernel(parts_ref, mass_ref, p_ref, q_ref, out_ref, col_ref, z_ref, row_ref):
    bias = ENTROPY * jnp.log(mass_ref[...]) - merge(parts_ref[...])
    lanes_to_rows(0.5 * bias, col_ref)
    log_sums(p_ref, q_ref, col_ref, z_ref, row_ref)
    out_ref[...] = jnp.broadcast_to(row_ref[...][None], out_ref.shape)


def flip(feat_ref):
    return feat_ref[...].astype(jnp.float32).T.astype(jnp.bfloat16)


def last_kernel(
    parts_ref, mass_ref, p_ref, q_ref, feat_ref, sent_ref, keep_ref, own_ref, bias_ref, col_ref, z_ref
):
    core = lax.rem(lax.axis_index("tgt"), 2)
    chips, _, share, depth = q_ref.shape
    half = chips * share
    width = feat_ref.shape[1]
    bias = ENTROPY * jnp.log(mass_ref[...]) - merge(parts_ref[...])
    bias_ref[...] = bias
    lanes_to_rows(0.5 * bias, col_ref)
    feat = flip(feat_ref)
    sent_ref[pl.ds(width, 8), :] = jnp.zeros((8, half), jnp.float32)
    own_ref[...] = jnp.zeros((8, half), jnp.float32)
    blocks = WIDTH // share
    for t in range(2 * half // WIDTH):
        own = t // (half // WIDTH)
        first = t % (half // WIDTH)
        q = q_ref[pl.ds(first * blocks, blocks), core if own else 1 - core]
        tops = chunk_scores(p_ref, q.reshape(WIDTH, depth), col_ref, z_ref, t)
        weights, scales = [], []
        for h, top in enumerate(tops):
            lanes = pl.ds(first * WIDTH + h * LANES, LANES)
            weight, total = chunk_weights(z_ref, t, h, top)
            lse = 2.0 * top + ENTROPY * jnp.log(total)
            sent_ref[pl.ds(width + own, 1), lanes] = lse
            own_ref[pl.ds(own, 1), lanes] = lse
            weights.append(weight.astype(jnp.bfloat16))
            scales.append(1.0 / total)
        lanes = pl.ds(first * WIDTH, WIDTH)
        weight = jnp.concatenate(weights, axis=1)
        scale = jnp.concatenate(scales, axis=1)
        if own:
            keep_ref[:, lanes] = weight
            own_ref[pl.ds(2, 1), lanes] = scale
        else:
            numer = lax.dot_general(feat, weight, NN, preferred_element_type=jnp.float32)
            sent_ref[pl.ds(0, width), lanes] = numer * scale


def own_kernel(keep_ref, own_ref, feat_ref, mean_ref):
    numer = lax.dot_general(
        flip(feat_ref), keep_ref[...], NN, preferred_element_type=jnp.float32
    )
    mean_ref[...] = numer * own_ref[pl.ds(2, 1), :]


def pair_kernel(mean_ref, own_ref, came_ref, out_ref):
    width, half = mean_ref.shape
    share = half // out_ref.shape[0]
    rows = half // LANES
    for side in range(2):
        mine = own_ref[pl.ds(1 - side, 1), :]
        other = came_ref[pl.ds(width + side, 1), :]
        top = jnp.maximum(mine, other)
        mine_share = jnp.exp2((mine - top) * ONE_SCALE)
        other_share = jnp.exp2((other - top) * ONE_SCALE)
        total = mine_share + other_share
        lse = top + ENTROPY * jnp.log(total)
        for k in range(rows):
            row = lse[:, k * LANES : (k + 1) * LANES]
            out_ref[:, pl.ds(share + side * rows + k, 1), :] = jnp.broadcast_to(
                row[None], (out_ref.shape[0], 1, LANES)
            )
        if side == 0:
            scale = 1.0 / total
            mean = mean_ref[...] * (mine_share * scale)
            mean = mean + came_ref[pl.ds(0, width), :] * (other_share * scale)
            step = LANES // share
            for k in range(rows):
                block = mean[:, k * LANES : (k + 1) * LANES].T
                out_ref[pl.ds(k * step, step), pl.ds(0, share), :] = block.reshape(step, share, LANES)


def final_kernel(landed_ref, mass_ref, square_ref, pot_ref, out_ref, ratio_ref):
    index = lax.axis_index("tgt")
    core, chip = lax.rem(index, 2), lax.div(index, 2)
    share = out_ref.shape[0]
    chips = landed_ref.shape[0]
    parts = landed_ref[:, pl.ds(share, landed_ref.shape[1] - share), :]
    whole = merge(parts)
    rows = whole.shape[0] // 2
    ratio_ref[...] = jnp.exp2((parts[:, :rows] - whole[None, :rows]) * ONE_SCALE)
    mine = ratio_ref[:, pl.ds(lax.div(chip, 2), 1), :].reshape(chips, LANES)
    mine = jnp.where(lax.rem(chip, 2) == 0, mine, pltpu.roll(mine, share, 1))
    mine = jnp.concatenate([mine, jnp.zeros((LANES - chips, LANES), jnp.float32)], axis=0).T
    total = jnp.zeros(out_ref.shape, jnp.float32)
    for b in range(chips):
        scale = jnp.broadcast_to(mine[:share, b : b + 1], out_ref.shape)
        total = total + landed_ref[b, pl.ds(0, share), :] * scale
    out_ref[...] = total
    even = jnp.where(core == 0, whole[:rows], whole[rows:])
    odd = jnp.where(core == 0, whole[rows:], whole[:rows])
    lane = lax.broadcasted_iota(jnp.int32, (rows, LANES), 1)
    first = jnp.where(lane < share, even, pltpu.roll(odd, share, 1))
    second = jnp.where(lane < share, pltpu.roll(even, share, 1), odd)
    for k in range(rows):
        for side, values in enumerate((first, second)):
            row = pl.ds(2 * k + side, 1)
            pot_ref[row, :] = (
                ENTROPY * jnp.log(mass_ref[row, :]) - values[k : k + 1] + square_ref[row, :]
            )


def scratch(p, q):
    return [
        pltpu.VMEM((p.shape[0], LANES), jnp.float32),
        pltpu.VMEM((p.shape[0], q.shape[0]), jnp.float32),
        pltpu.VMEM((q.shape[0] // LANES, LANES), jnp.float32),
    ]


def call(kernel, args, outs, scratch_shapes, spaces=None):
    whole = pl.BlockSpec(memory_space=pltpu.VMEM)
    return pl.pallas_call(
        kernel,
        out_shape=outs,
        in_specs=spaces or [whole] * len(args),
        out_specs=jax.tree.map(lambda _: whole, outs),
        scratch_shapes=scratch_shapes,
        compiler_params=pltpu.CompilerParams(vmem_limit_bytes=VMEM_LIMIT),
    )(*args)


def squares(embed):
    return jnp.sum(jnp.square(embed.astype(jnp.float32)), axis=1).reshape(-1, LANES)


def local(source_embed, target_embed, target_feat, source_mass, target_mass):
    f32 = jnp.float32
    shape = jax.ShapeDtypeStruct
    n_src, n_tgt = lax.axis_size("src"), lax.axis_size("tgt")
    rows, depth = source_embed.shape
    width = target_feat.shape[1]
    share, half, chips = rows // n_tgt, rows // 2, n_tgt // 2
    src_mass = source_mass.reshape(-1, LANES)
    tgt_mass = target_mass.reshape(-1, LANES)
    src_rows, tgt_rows = src_mass.shape[0], tgt_mass.shape[0]
    to_src = shape((n_src, tgt_rows, LANES), f32)
    to_tgt = shape((n_tgt, src_rows, LANES), f32)
    by_src = scratch(source_embed, target_embed)
    by_tgt = scratch(target_embed, source_embed)
    same_core = [list(range(core, n_tgt, 2)) for core in range(2)]
    swap = [(index, index ^ 1) for index in range(n_tgt)]

    loads = [pltpu.SemaphoreType.DMA((PIECES,)), pltpu.SemaphoreType.DMA((1,))]
    hbm = [pl.BlockSpec(memory_space=pltpu.HBM)] * 2
    embeds = [
        pltpu.with_memory_space_constraint(embed, pltpu.HBM) for embed in (source_embed, target_embed)
    ]
    held = [shape(embed.shape, embed.dtype) for embed in embeds]
    sent, source_embed, target_embed = call(
        first_kernel, embeds, (to_src, *held), loads + by_src, hbm
    )
    parts = lax.all_to_all(sent, "src", 0, 0)
    sent = call(next_kernel, (parts, tgt_mass, target_embed, source_embed), to_tgt, by_tgt)
    parts = lax.all_to_all(sent, "tgt", 0, 0)
    sent = call(next_kernel, (parts, src_mass, source_embed, target_embed), to_src, by_src)
    parts = lax.all_to_all(sent, "src", 0, 0)
    sent, keep, own, bias = call(
        last_kernel,
        (parts, tgt_mass, target_embed, source_embed.reshape(chips, 2, share, depth), target_feat),
        (
            shape((width + 8, half), f32),
            shape((target_embed.shape[0], half), jnp.bfloat16),
            shape((8, half), f32),
            shape((tgt_rows, LANES), f32),
        ),
        by_tgt[:2],
    )
    came = lax.ppermute(sent, "tgt", swap)
    mean = call(own_kernel, (keep, own, target_feat), shape((width, half), f32), [])
    sent = call(pair_kernel, (mean, own, came), shape((chips, share + src_rows, LANES), f32), [])
    sent, source_late, target_late = lax.optimization_barrier((sent, source_embed, target_embed))
    landed = lax.all_to_all(sent, "tgt", 0, 0, axis_index_groups=same_core)
    target_pot = (bias + squares(target_late)).reshape(-1)
    source_pot, projected = call(
        final_kernel,
        (landed, src_mass, squares(source_late)),
        (shape((src_rows, LANES), f32), shape((share, width), f32)),
        [pltpu.VMEM((chips, src_rows // 2, LANES), f32)],
    )
    return (source_pot.reshape(-1), target_pot, projected)


def solution(mesh):
    placed = (P("src", None), P("tgt", None), P("tgt", None), P("src"), P("tgt"))
    return jax.shard_map(
        local,
        mesh=mesh,
        in_specs=placed,
        out_specs=(P("src"), P("tgt"), P(("src", "tgt"), None)),
        check_vma=False,
    )
```

```python
import math

import jax
import jax.numpy as jnp
from jax import lax
from jax.experimental import pallas as pl
from jax.experimental.pallas import tpu as pltpu
from jax.sharding import PartitionSpec as P

ENTROPY = 0.05
LANES = 128
WIDTH = 256
TWO_SCALE = 2.0 / ENTROPY * math.log2(math.e)
ONE_SCALE = 1.0 / ENTROPY * math.log2(math.e)
NT = (((1,), (1,)), ((), ()))
NN = (((1,), (0,)), ((), ()))
HALVES = WIDTH // LANES
SLAB = 512
ACCUMULATE = 32
VMEM_LIMIT = 40 * 1024 * 1024


def merge(parts):
    top = jnp.max(parts, axis=0)
    total = jnp.sum(jnp.exp2((parts - top[None]) * ONE_SCALE), axis=0)
    return top + ENTROPY * jnp.log(total)


def lanes_to_rows(values, col_ref):
    for k in range(values.shape[0]):
        square = jnp.broadcast_to(values[k : k + 1, :], (LANES, LANES))
        col_ref[pl.ds(k * LANES, LANES), :] = square.T


def fold(reduce, part):
    return reduce(part.reshape(-1, ACCUMULATE, LANES), axis=0)


def scores(p_ref, q, col_ref, z_ref, s, t):
    slab = pl.ds(s * SLAB, SLAB)
    z = lax.dot_general(p_ref[slab, :], q, NT, preferred_element_type=jnp.float32)
    col = col_ref[slab, :]
    tops = []
    for h in range(HALVES):
        part = z[:, h * LANES : (h + 1) * LANES] + col
        z_ref[slab, pl.ds(t * WIDTH + h * LANES, LANES)] = part
        tops.append(fold(jnp.max, part))
    return tops


def weigh(z_ref, tops, s, t):
    slab = pl.ds(s * SLAB, SLAB)
    weights, totals = [], []
    for h, top in enumerate(tops):
        part = z_ref[slab, pl.ds(t * WIDTH + h * LANES, LANES)]
        weight = jnp.exp2((part - top) * TWO_SCALE)
        weights.append(weight)
        totals.append(fold(jnp.sum, weight))
    return weights, totals


def join(op, held, more):
    return more if held is None else [op(a, b) for a, b in zip(held, more)]


def settle(reduce, values):
    return [reduce(value, axis=0, keepdims=True) for value in values]


def log_sum(top, total):
    return 2.0 * top + ENTROPY * jnp.log(total)


def write_rows(row_ref, t, tops, totals):
    for h, (top, total) in enumerate(zip(tops, totals)):
        row_ref[pl.ds(t * HALVES + h, 1), :] = log_sum(top, total)


def run_chunks(p_ref, chunk, chunks, col_ref, z_ref, emit):
    slabs = p_ref.shape[0] // SLAB
    tops = None
    for t in range(chunks + 1):
        q = chunk(t) if t < chunks else None
        later, totals, weights = None, None, []
        for s in range(slabs):
            if t < chunks:
                later = join(jnp.maximum, later, scores(p_ref, q, col_ref, z_ref, s, t))
            if t > 0:
                weight, total = weigh(z_ref, tops, s, t - 1)
                totals = join(jnp.add, totals, total)
                weights.append(weight)
        if t > 0:
            emit(t - 1, tops, settle(jnp.sum, totals), weights)
        if t < chunks:
            tops = settle(jnp.max, later)


def first_kernel(
    p_hbm, q_hbm, p_mass_hbm, q_mass_hbm, out_ref, p_ref, q_ref, p_log_ref, q_log_ref,
    p_sems, sems, col_ref, z_ref, row_ref,
):
    slabs, chunks = p_ref.shape[0] // SLAB, q_ref.shape[0] // WIDTH
    loads = []
    for s in range(slabs):
        slab = pl.ds(s * SLAB, SLAB)
        loads.append(pltpu.make_async_copy(p_hbm.at[slab, :], p_ref.at[slab, :], p_sems.at[s]))
    load_q = pltpu.make_async_copy(q_hbm, q_ref, sems.at[0])
    load_p_mass = pltpu.make_async_copy(p_mass_hbm, p_log_ref, sems.at[1])
    load_q_mass = pltpu.make_async_copy(q_mass_hbm, q_log_ref, sems.at[2])
    loads[0].start()
    load_q.start()
    for load in loads[1:]:
        load.start()
    load_p_mass.start()
    load_q_mass.start()
    tops = [None] * chunks
    for s, load in enumerate(loads):
        load.wait()
        slab = pl.ds(s * SLAB, SLAB)
        p = p_ref[slab, :].astype(jnp.float32)
        half = -0.5 * jnp.sum(p * p, axis=1, keepdims=True)
        col_ref[slab, :] = jnp.broadcast_to(half, (SLAB, LANES))
        if s == 0:
            load_q.wait()
        for t in range(chunks):
            q = q_ref[pl.ds(t * WIDTH, WIDTH), :]
            tops[t] = join(jnp.maximum, tops[t], scores(p_ref, q, col_ref, z_ref, s, t))
    for t in range(chunks):
        top = settle(jnp.max, tops[t])
        totals = None
        for s in range(slabs):
            totals = join(jnp.add, totals, weigh(z_ref, top, s, t)[1])
        write_rows(row_ref, t, top, settle(jnp.sum, totals))
    load_p_mass.wait()
    load_q_mass.wait()
    p_log_ref[...] = ENTROPY * jnp.log(p_log_ref[...])
    q_log_ref[...] = ENTROPY * jnp.log(q_log_ref[...])
    out_ref[...] = jnp.broadcast_to(row_ref[...][None], out_ref.shape)


def next_kernel(parts_ref, log_ref, p_ref, q_ref, out_ref, col_ref, z_ref, row_ref):
    lanes_to_rows(0.5 * (log_ref[...] - merge(parts_ref[...])), col_ref)
    run_chunks(
        p_ref,
        lambda t: q_ref[pl.ds(t * WIDTH, WIDTH), :],
        q_ref.shape[0] // WIDTH,
        col_ref,
        z_ref,
        lambda t, tops, totals, _: write_rows(row_ref, t, tops, totals),
    )
    out_ref[...] = jnp.broadcast_to(row_ref[...][None], out_ref.shape)


def last_kernel(
    parts_ref, log_ref, p_ref, q_ref, feat_ref,
    sent_ref, keep_ref, own_ref, bias_ref, flip_ref, col_ref, z_ref,
):
    core = lax.rem(lax.axis_index("tgt"), 2)
    chips, _, share, depth = q_ref.shape
    half = chips * share
    width = feat_ref.shape[1]
    blocks = WIDTH // share
    bias = log_ref[...] - merge(parts_ref[...])
    bias_ref[...] = bias
    lanes_to_rows(0.5 * bias, col_ref)
    flip_ref[...] = feat_ref[...].astype(jnp.float32).T.astype(jnp.bfloat16)
    sent_ref[pl.ds(width, 8), :] = jnp.zeros((8, half), jnp.float32)
    own_ref[...] = jnp.zeros((8, half), jnp.float32)

    def chunk(t):
        own, first = divmod(t * WIDTH, half)
        q = q_ref[pl.ds(first // share, blocks), core if own else 1 - core]
        return q.reshape(WIDTH, depth)

    def emit(t, tops, totals, weights):
        own, first = divmod(t * WIDTH, half)
        slabs = [
            jnp.concatenate([weight.astype(jnp.bfloat16) for weight in slab], axis=1)
            for slab in weights
        ]
        lanes = pl.ds(first, WIDTH)
        lse = jnp.concatenate([log_sum(*pair) for pair in zip(tops, totals)], axis=1)
        scale = 1.0 / jnp.concatenate(totals, axis=1)
        sent_ref[pl.ds(width + own, 1), lanes] = lse
        own_ref[pl.ds(own, 1), lanes] = lse
        if own:
            for s, slab in enumerate(slabs):
                keep_ref[pl.ds(s * SLAB, SLAB), lanes] = slab
            own_ref[pl.ds(2, 1), lanes] = scale
        else:
            weight = jnp.concatenate(slabs, axis=0)
            numer = lax.dot_general(
                flip_ref[...], weight, NN, preferred_element_type=jnp.float32
            )
            sent_ref[pl.ds(0, width), lanes] = numer * scale

    run_chunks(p_ref, chunk, 2 * half // WIDTH, col_ref, z_ref, emit)


def own_kernel(keep_ref, own_ref, flip_ref, mean_ref):
    numer = lax.dot_general(
        flip_ref[...], keep_ref[...], NN, preferred_element_type=jnp.float32
    )
    mean_ref[...] = numer * own_ref[pl.ds(2, 1), :]


def pair_kernel(mean_ref, own_ref, came_ref, out_ref):
    width, half = mean_ref.shape
    share = half // out_ref.shape[0]
    rows = half // LANES
    for side in range(2):
        mine = own_ref[pl.ds(1 - side, 1), :]
        other = came_ref[pl.ds(width + side, 1), :]
        top = jnp.maximum(mine, other)
        mine_share = jnp.exp2((mine - top) * ONE_SCALE)
        other_share = jnp.exp2((other - top) * ONE_SCALE)
        total = mine_share + other_share
        lse = top + ENTROPY * jnp.log(total)
        for k in range(rows):
            row = lse[:, k * LANES : (k + 1) * LANES]
            out_ref[:, pl.ds(share + side * rows + k, 1), :] = jnp.broadcast_to(
                row[None], (out_ref.shape[0], 1, LANES)
            )
        if side == 0:
            scale = 1.0 / total
            mean = mean_ref[...] * (mine_share * scale)
            mean = mean + came_ref[pl.ds(0, width), :] * (other_share * scale)
            step = LANES // share
            for k in range(rows):
                block = mean[:, k * LANES : (k + 1) * LANES].T
                out_ref[pl.ds(k * step, step), pl.ds(0, share), :] = block.reshape(step, share, LANES)


def final_kernel(landed_ref, log_ref, square_ref, pot_ref, out_ref, ratio_ref):
    index = lax.axis_index("tgt")
    core, chip = lax.rem(index, 2), lax.div(index, 2)
    share = out_ref.shape[0]
    chips = landed_ref.shape[0]
    parts = landed_ref[:, pl.ds(share, landed_ref.shape[1] - share), :]
    whole = merge(parts)
    rows = whole.shape[0] // 2
    ratio_ref[...] = jnp.exp2((parts[:, :rows] - whole[None, :rows]) * ONE_SCALE)
    mine = ratio_ref[:, pl.ds(lax.div(chip, 2), 1), :].reshape(chips, LANES)
    mine = jnp.where(lax.rem(chip, 2) == 0, mine, pltpu.roll(mine, share, 1))
    mine = jnp.concatenate([mine, jnp.zeros((LANES - chips, LANES), jnp.float32)], axis=0).T
    total = jnp.zeros(out_ref.shape, jnp.float32)
    for b in range(chips):
        scale = jnp.broadcast_to(mine[:share, b : b + 1], out_ref.shape)
        total = total + landed_ref[b, pl.ds(0, share), :] * scale
    out_ref[...] = total
    even = jnp.where(core == 0, whole[:rows], whole[rows:])
    odd = jnp.where(core == 0, whole[rows:], whole[:rows])
    lane = lax.broadcasted_iota(jnp.int32, (rows, LANES), 1)
    first = jnp.where(lane < share, even, pltpu.roll(odd, share, 1))
    second = jnp.where(lane < share, pltpu.roll(even, share, 1), odd)
    for k in range(rows):
        for side, values in enumerate((first, second)):
            row = pl.ds(2 * k + side, 1)
            pot_ref[row, :] = (
                log_ref[row, :] - values[k : k + 1] + square_ref[row, :]
            )


def scratch(p, q):
    return [
        pltpu.VMEM((p.shape[0], LANES), jnp.float32),
        pltpu.VMEM((p.shape[0], q.shape[0]), jnp.float32),
        pltpu.VMEM((q.shape[0] // LANES, LANES), jnp.float32),
    ]


def call(kernel, args, outs, scratch_shapes, spaces=None):
    whole = pl.BlockSpec(memory_space=pltpu.VMEM)
    return pl.pallas_call(
        kernel,
        out_shape=outs,
        in_specs=spaces or [whole] * len(args),
        out_specs=jax.tree.map(lambda _: whole, outs),
        scratch_shapes=scratch_shapes,
        compiler_params=pltpu.CompilerParams(vmem_limit_bytes=VMEM_LIMIT),
    )(*args)


def squares(embed):
    return jnp.sum(jnp.square(embed.astype(jnp.float32)), axis=1).reshape(-1, LANES)


def local(source_embed, target_embed, target_feat, source_mass, target_mass):
    f32 = jnp.float32
    shape = jax.ShapeDtypeStruct
    n_src, n_tgt = lax.axis_size("src"), lax.axis_size("tgt")
    rows, depth = source_embed.shape
    width = target_feat.shape[1]
    share, half, chips = rows // n_tgt, rows // 2, n_tgt // 2
    src_mass = source_mass.reshape(-1, LANES)
    tgt_mass = target_mass.reshape(-1, LANES)
    src_rows, tgt_rows = src_mass.shape[0], tgt_mass.shape[0]
    to_src = shape((n_src, tgt_rows, LANES), f32)
    to_tgt = shape((n_tgt, src_rows, LANES), f32)
    by_src = scratch(source_embed, target_embed)
    by_tgt = scratch(target_embed, source_embed)
    same_core = [list(range(core, n_tgt, 2)) for core in range(2)]
    swap = [(index, index ^ 1) for index in range(n_tgt)]

    sems = [pltpu.SemaphoreType.DMA((rows // SLAB,)), pltpu.SemaphoreType.DMA((3,))]
    inputs = [
        pltpu.with_memory_space_constraint(array, pltpu.HBM)
        for array in (source_embed, target_embed, src_mass, tgt_mass)
    ]
    held = [shape(array.shape, array.dtype) for array in inputs]
    sent, source_embed, target_embed, src_log, tgt_log = call(
        first_kernel,
        inputs,
        (to_src, *held),
        sems + by_src,
        [pl.BlockSpec(memory_space=pltpu.HBM)] * len(inputs),
    )
    parts = lax.all_to_all(sent, "src", 0, 0)
    sent = call(next_kernel, (parts, tgt_log, target_embed, source_embed), to_tgt, by_tgt)
    parts = lax.all_to_all(sent, "tgt", 0, 0)
    sent = call(next_kernel, (parts, src_log, source_embed, target_embed), to_src, by_src)
    parts = lax.all_to_all(sent, "src", 0, 0)
    sent, keep, own, bias, turned = call(
        last_kernel,
        (parts, tgt_log, target_embed, source_embed.reshape(chips, 2, share, depth), target_feat),
        (
            shape((width + 8, half), f32),
            shape((target_embed.shape[0], half), jnp.bfloat16),
            shape((8, half), f32),
            shape((tgt_rows, LANES), f32),
            shape(target_feat.shape[::-1], jnp.bfloat16),
        ),
        by_tgt[:2],
    )
    came = lax.ppermute(sent, "tgt", swap)
    mean = call(own_kernel, (keep, own, turned), shape((width, half), f32), [])
    sent = call(pair_kernel, (mean, own, came), shape((chips, share + src_rows, LANES), f32), [])
    sent, source_late, target_late = lax.optimization_barrier((sent, source_embed, target_embed))
    landed = lax.all_to_all(sent, "tgt", 0, 0, axis_index_groups=same_core)
    target_pot = (bias + squares(target_late)).reshape(-1)
    source_pot, projected = call(
        final_kernel,
        (landed, src_log, squares(source_late)),
        (shape((src_rows, LANES), f32), shape((share, width), f32)),
        [pltpu.VMEM((chips, src_rows // 2, LANES), f32)],
    )
    return (source_pot.reshape(-1), target_pot, projected)


def solution(mesh):
    placed = (P("src", None), P("tgt", None), P("tgt", None), P("src"), P("tgt"))
    return jax.shard_map(
        local,
        mesh=mesh,
        in_specs=placed,
        out_specs=(P("src"), P("tgt"), P(("src", "tgt"), None)),
        check_vma=False,
    )
```

```python
import math

import jax
import jax.numpy as jnp
from jax import lax
from jax.experimental import pallas as pl
from jax.experimental.pallas import tpu as pltpu
from jax.sharding import PartitionSpec as P

ENTROPY = 0.05
LANES = 128
WIDTH = 256
TWO_SCALE = 2.0 / ENTROPY * math.log2(math.e)
ONE_SCALE = 1.0 / ENTROPY * math.log2(math.e)
NT = (((1,), (1,)), ((), ()))
NN = (((1,), (0,)), ((), ()))
HALVES = WIDTH // LANES
SLAB = 512
ACCUMULATE = 32
VMEM_LIMIT = 40 * 1024 * 1024


def merge(parts):
    top = jnp.max(parts, axis=0)
    total = jnp.sum(jnp.exp2((parts - top[None]) * ONE_SCALE), axis=0)
    return top + ENTROPY * jnp.log(total)


def lanes_to_rows(values, col_ref):
    for k in range(values.shape[0]):
        square = jnp.broadcast_to(values[k : k + 1, :], (LANES, LANES))
        col_ref[pl.ds(k * LANES, LANES), :] = square.T


def fold(reduce, part):
    return reduce(part.reshape(-1, ACCUMULATE, LANES), axis=0)


def scores(p_ref, q, col_ref, z_ref, s, t):
    slab = pl.ds(s * SLAB, SLAB)
    z = lax.dot_general(p_ref[slab, :], q, NT, preferred_element_type=jnp.float32)
    col = col_ref[slab, :]
    tops = []
    for h in range(HALVES):
        part = z[:, h * LANES : (h + 1) * LANES] + col
        z_ref[slab, pl.ds(t * WIDTH + h * LANES, LANES)] = part
        tops.append(fold(jnp.max, part))
    return tops


def weigh(z_ref, tops, s, t):
    slab = pl.ds(s * SLAB, SLAB)
    weights, totals = [], []
    for h, top in enumerate(tops):
        part = z_ref[slab, pl.ds(t * WIDTH + h * LANES, LANES)]
        weight = jnp.exp2((part - top) * TWO_SCALE)
        weights.append(weight)
        totals.append(fold(jnp.sum, weight))
    return weights, totals


def join(op, held, more):
    return more if held is None else [op(a, b) for a, b in zip(held, more)]


def settle(reduce, values):
    return [reduce(value, axis=0, keepdims=True) for value in values]


def log_sum(top, total):
    return 2.0 * top + ENTROPY * jnp.log(total)


def write_rows(row_ref, t, tops, totals):
    for h, (top, total) in enumerate(zip(tops, totals)):
        row_ref[pl.ds(t * HALVES + h, 1), :] = log_sum(top, total)


def run_chunks(p_ref, chunk, chunks, col_ref, z_ref, emit):
    slabs = p_ref.shape[0] // SLAB
    tops = None
    for t in range(chunks + 1):
        q = chunk(t) if t < chunks else None
        later, totals, weights = None, None, []
        for s in range(slabs):
            if t < chunks:
                later = join(jnp.maximum, later, scores(p_ref, q, col_ref, z_ref, s, t))
            if t > 0:
                weight, total = weigh(z_ref, tops, s, t - 1)
                totals = join(jnp.add, totals, total)
                weights.append(weight)
        if t > 0:
            emit(t - 1, tops, settle(jnp.sum, totals), weights)
        if t < chunks:
            tops = settle(jnp.max, later)


def first_kernel(
    p_hbm, q_hbm, p_mass_hbm, q_mass_hbm, out_ref, p_ref, q_ref, p_log_ref, q_log_ref,
    p_sems, q_sems, sems, col_ref, z_ref, row_ref,
):
    slabs, chunks = p_ref.shape[0] // SLAB, q_ref.shape[0] // WIDTH

    def load(hbm, ref, sem, k, rows):
        part = pl.ds(k * rows, rows)
        return pltpu.make_async_copy(hbm.at[part, :], ref.at[part, :], sem.at[k])

    p_loads = [load(p_hbm, p_ref, p_sems, s, SLAB) for s in range(slabs)]
    q_loads = [load(q_hbm, q_ref, q_sems, t, WIDTH) for t in range(chunks)]
    masses = [
        pltpu.make_async_copy(p_mass_hbm, p_log_ref, sems.at[0]),
        pltpu.make_async_copy(q_mass_hbm, q_log_ref, sems.at[1]),
    ]
    for copy in p_loads[:1] + q_loads + p_loads[1:] + masses:
        copy.start()
    tops = [[] for _ in range(chunks)]
    totals = [[] for _ in range(chunks)]
    steps = [(s, t) for s in range(slabs) for t in range(chunks)]
    for step in range(len(steps) + 1):
        if step < len(steps):
            s, t = steps[step]
            if t == 0:
                p_loads[s].wait()
                slab = pl.ds(s * SLAB, SLAB)
                p = p_ref[slab, :].astype(jnp.float32)
                half = -0.5 * jnp.sum(p * p, axis=1, keepdims=True)
                col_ref[slab, :] = jnp.broadcast_to(half, (SLAB, LANES))
            if s == 0:
                q_loads[t].wait()
            q = q_ref[pl.ds(t * WIDTH, WIDTH), :]
            tops[t].append(settle(jnp.max, scores(p_ref, q, col_ref, z_ref, s, t)))
        if step > 0:
            s, t = steps[step - 1]
            totals[t].append(settle(jnp.sum, weigh(z_ref, tops[t][s], s, t)[1]))
    for t in range(chunks):
        top, total = [], []
        for h in range(HALVES):
            held = [slab[h] for slab in tops[t]]
            most = held[0]
            for value in held[1:]:
                most = jnp.maximum(most, value)
            top.append(most)
            total.append(
                sum(
                    slab[h] * jnp.exp2((value - most) * TWO_SCALE)
                    for slab, value in zip(totals[t], held)
                )
            )
        write_rows(row_ref, t, top, total)
    for copy in masses:
        copy.wait()
    p_log_ref[...] = ENTROPY * jnp.log(p_log_ref[...])
    q_log_ref[...] = ENTROPY * jnp.log(q_log_ref[...])
    out_ref[...] = jnp.broadcast_to(row_ref[...][None], out_ref.shape)


def next_kernel(parts_ref, log_ref, p_ref, q_ref, out_ref, col_ref, z_ref, row_ref):
    lanes_to_rows(0.5 * (log_ref[...] - merge(parts_ref[...])), col_ref)
    run_chunks(
        p_ref,
        lambda t: q_ref[pl.ds(t * WIDTH, WIDTH), :],
        q_ref.shape[0] // WIDTH,
        col_ref,
        z_ref,
        lambda t, tops, totals, _: write_rows(row_ref, t, tops, totals),
    )
    out_ref[...] = jnp.broadcast_to(row_ref[...][None], out_ref.shape)


def last_kernel(
    parts_ref, log_ref, p_ref, q_ref, feat_ref,
    sent_ref, keep_ref, own_ref, bias_ref, flip_ref, col_ref, z_ref,
):
    core = lax.rem(lax.axis_index("tgt"), 2)
    chips, _, share, depth = q_ref.shape
    half = chips * share
    width = feat_ref.shape[1]
    blocks = WIDTH // share
    bias = log_ref[...] - merge(parts_ref[...])
    bias_ref[...] = bias
    lanes_to_rows(0.5 * bias, col_ref)
    flip_ref[...] = feat_ref[...].astype(jnp.float32).T.astype(jnp.bfloat16)
    sent_ref[pl.ds(width, 8), :] = jnp.zeros((8, half), jnp.float32)
    own_ref[...] = jnp.zeros((8, half), jnp.float32)

    def chunk(t):
        own, first = divmod(t * WIDTH, half)
        q = q_ref[pl.ds(first // share, blocks), core if own else 1 - core]
        return q.reshape(WIDTH, depth)

    def emit(t, tops, totals, weights):
        own, first = divmod(t * WIDTH, half)
        slabs = [
            jnp.concatenate([weight.astype(jnp.bfloat16) for weight in slab], axis=1)
            for slab in weights
        ]
        lanes = pl.ds(first, WIDTH)
        lse = jnp.concatenate([log_sum(*pair) for pair in zip(tops, totals)], axis=1)
        scale = 1.0 / jnp.concatenate(totals, axis=1)
        sent_ref[pl.ds(width + own, 1), lanes] = lse
        own_ref[pl.ds(own, 1), lanes] = lse
        if own:
            for s, slab in enumerate(slabs):
                keep_ref[pl.ds(s * SLAB, SLAB), lanes] = slab
            own_ref[pl.ds(2, 1), lanes] = scale
        else:
            weight = jnp.concatenate(slabs, axis=0)
            numer = lax.dot_general(
                flip_ref[...], weight, NN, preferred_element_type=jnp.float32
            )
            sent_ref[pl.ds(0, width), lanes] = numer * scale

    run_chunks(p_ref, chunk, 2 * half // WIDTH, col_ref, z_ref, emit)


def squares(ref, k):
    rows = ref[pl.ds(k * LANES, LANES), :].astype(jnp.float32)
    norms = jnp.sum(rows * rows, axis=1, keepdims=True)
    return jnp.broadcast_to(norms, (LANES, LANES)).T[:1, :]


def own_kernel(
    keep_ref, own_ref, flip_ref, bias_ref, p_ref, q_ref, log_ref, mean_ref, pot_ref, base_ref
):
    numer = lax.dot_general(
        flip_ref[...], keep_ref[...], NN, preferred_element_type=jnp.float32
    )
    mean_ref[...] = numer * own_ref[pl.ds(2, 1), :]
    for k in range(pot_ref.shape[0]):
        row = pl.ds(k, 1)
        pot_ref[row, :] = bias_ref[row, :] + squares(p_ref, k)
    for k in range(base_ref.shape[0]):
        row = pl.ds(k, 1)
        base_ref[row, :] = log_ref[row, :] + squares(q_ref, k)


def pair_kernel(mean_ref, own_ref, came_ref, out_ref, row_ref):
    width, half = mean_ref.shape
    chips = out_ref.shape[0]
    share = half // chips
    rows = half // LANES
    for side in range(2):
        mine = own_ref[pl.ds(1 - side, 1), :]
        other = came_ref[pl.ds(width + side, 1), :]
        top = jnp.maximum(mine, other)
        mine_share = jnp.exp2((mine - top) * ONE_SCALE)
        other_share = jnp.exp2((other - top) * ONE_SCALE)
        total = mine_share + other_share
        lse = top + ENTROPY * jnp.log(total)
        for k in range(rows):
            row_ref[pl.ds(side * rows + k, 1), :] = lse[:, k * LANES : (k + 1) * LANES]
        if side == 0:
            scale = 1.0 / total
            mine_share, other_share = mine_share * scale, other_share * scale
            step = LANES // share
            for k in range(rows):
                lanes = slice(k * LANES, (k + 1) * LANES)
                block = (
                    mean_ref[:, lanes] * mine_share[:, lanes]
                    + came_ref[pl.ds(0, width), lanes] * other_share[:, lanes]
                )
                out_ref[pl.ds(k * step, step), pl.ds(0, share), :] = block.T.reshape(
                    step, share, LANES
                )
    out_ref[:, pl.ds(share, 2 * rows), :] = jnp.broadcast_to(
        row_ref[...][None], (chips, 2 * rows, LANES)
    )


def final_kernel(landed_ref, base_ref, pot_ref, out_ref, ratio_ref):
    index = lax.axis_index("tgt")
    core, chip = lax.rem(index, 2), lax.div(index, 2)
    share = out_ref.shape[0]
    chips = landed_ref.shape[0]
    parts = landed_ref[:, pl.ds(share, landed_ref.shape[1] - share), :]
    whole = merge(parts)
    rows = whole.shape[0] // 2
    ratio_ref[...] = jnp.exp2((parts[:, :rows] - whole[None, :rows]) * ONE_SCALE)
    mine = ratio_ref[:, pl.ds(lax.div(chip, 2), 1), :].reshape(chips, LANES)
    mine = jnp.where(lax.rem(chip, 2) == 0, mine, pltpu.roll(mine, share, 1))
    mine = jnp.concatenate([mine, jnp.zeros((LANES - chips, LANES), jnp.float32)], axis=0).T
    total = jnp.zeros(out_ref.shape, jnp.float32)
    for b in range(chips):
        scale = jnp.broadcast_to(mine[:share, b : b + 1], out_ref.shape)
        total = total + landed_ref[b, pl.ds(0, share), :] * scale
    out_ref[...] = total
    even = jnp.where(core == 0, whole[:rows], whole[rows:])
    odd = jnp.where(core == 0, whole[rows:], whole[:rows])
    lane = lax.broadcasted_iota(jnp.int32, (rows, LANES), 1)
    first = jnp.where(lane < share, even, pltpu.roll(odd, share, 1))
    second = jnp.where(lane < share, pltpu.roll(even, share, 1), odd)
    for k in range(rows):
        for side, values in enumerate((first, second)):
            row = pl.ds(2 * k + side, 1)
            pot_ref[row, :] = base_ref[row, :] - values[k : k + 1]


def scratch(p, q):
    return [
        pltpu.VMEM((p.shape[0], LANES), jnp.float32),
        pltpu.VMEM((p.shape[0], q.shape[0]), jnp.float32),
        pltpu.VMEM((q.shape[0] // LANES, LANES), jnp.float32),
    ]


def call(kernel, args, outs, scratch_shapes, spaces=None):
    whole = pl.BlockSpec(memory_space=pltpu.VMEM)
    return pl.pallas_call(
        kernel,
        out_shape=outs,
        in_specs=spaces or [whole] * len(args),
        out_specs=jax.tree.map(lambda _: whole, outs),
        scratch_shapes=scratch_shapes,
        compiler_params=pltpu.CompilerParams(vmem_limit_bytes=VMEM_LIMIT),
    )(*args)


def local(source_embed, target_embed, target_feat, source_mass, target_mass):
    f32 = jnp.float32
    shape = jax.ShapeDtypeStruct
    n_src, n_tgt = lax.axis_size("src"), lax.axis_size("tgt")
    rows, depth = source_embed.shape
    width = target_feat.shape[1]
    share, half, chips = rows // n_tgt, rows // 2, n_tgt // 2
    src_mass = source_mass.reshape(-1, LANES)
    tgt_mass = target_mass.reshape(-1, LANES)
    src_rows, tgt_rows = src_mass.shape[0], tgt_mass.shape[0]
    to_src = shape((n_src, tgt_rows, LANES), f32)
    to_tgt = shape((n_tgt, src_rows, LANES), f32)
    by_src = scratch(source_embed, target_embed)
    by_tgt = scratch(target_embed, source_embed)
    same_core = [list(range(core, n_tgt, 2)) for core in range(2)]
    swap = [(index, index ^ 1) for index in range(n_tgt)]

    pieces = (rows // SLAB, target_embed.shape[0] // WIDTH, 2)
    sems = [pltpu.SemaphoreType.DMA((count,)) for count in pieces]
    inputs = [
        pltpu.with_memory_space_constraint(array, pltpu.HBM)
        for array in (source_embed, target_embed, src_mass, tgt_mass)
    ]
    held = [shape(array.shape, array.dtype) for array in inputs]
    sent, source_embed, target_embed, src_log, tgt_log = call(
        first_kernel,
        inputs,
        (to_src, *held),
        sems + by_src,
        [pl.BlockSpec(memory_space=pltpu.HBM)] * len(inputs),
    )
    parts = lax.all_to_all(sent, "src", 0, 0)
    sent = call(next_kernel, (parts, tgt_log, target_embed, source_embed), to_tgt, by_tgt)
    parts = lax.all_to_all(sent, "tgt", 0, 0)
    sent = call(next_kernel, (parts, src_log, source_embed, target_embed), to_src, by_src)
    parts = lax.all_to_all(sent, "src", 0, 0)
    sent, keep, own, bias, turned = call(
        last_kernel,
        (parts, tgt_log, target_embed, source_embed.reshape(chips, 2, share, depth), target_feat),
        (
            shape((width + 8, half), f32),
            shape((target_embed.shape[0], half), jnp.bfloat16),
            shape((8, half), f32),
            shape((tgt_rows, LANES), f32),
            shape(target_feat.shape[::-1], jnp.bfloat16),
        ),
        by_tgt[:2],
    )
    came = lax.ppermute(sent, "tgt", swap)
    mean, target_pot, base = call(
        own_kernel,
        (keep, own, turned, bias, target_embed, source_embed, src_log),
        (shape((width, half), f32), shape(bias.shape, f32), shape(src_log.shape, f32)),
        [],
    )
    sent = call(
        pair_kernel,
        (mean, own, came),
        shape((chips, share + src_rows, LANES), f32),
        [pltpu.VMEM((src_rows, LANES), f32)],
    )
    landed = lax.all_to_all(sent, "tgt", 0, 0, axis_index_groups=same_core)
    source_pot, projected = call(
        final_kernel,
        (landed, base),
        (shape((src_rows, LANES), f32), shape((share, width), f32)),
        [pltpu.VMEM((chips, src_rows // 2, LANES), f32)],
    )
    return (source_pot.reshape(-1), target_pot.reshape(-1), projected)


def solution(mesh):
    placed = (P("src", None), P("tgt", None), P("tgt", None), P("src"), P("tgt"))
    return jax.shard_map(
        local,
        mesh=mesh,
        in_specs=placed,
        out_specs=(P("src"), P("tgt"), P(("src", "tgt"), None)),
        check_vma=False,
    )
```

```python
import math

import jax
import jax.numpy as jnp
from jax import lax
from jax.experimental import pallas as pl
from jax.experimental.pallas import tpu as pltpu
from jax.sharding import PartitionSpec as P

ENTROPY = 0.05
LANES = 128
WIDTH = 256
TWO_SCALE = 2.0 / ENTROPY * math.log2(math.e)
ONE_SCALE = 1.0 / ENTROPY * math.log2(math.e)
NT = (((1,), (1,)), ((), ()))
NN = (((1,), (0,)), ((), ()))
HALVES = WIDTH // LANES
SLAB = 512
ACCUMULATE = 32
VMEM_LIMIT = 40 * 1024 * 1024


def merge(parts):
    top = jnp.max(parts, axis=0)
    total = jnp.sum(jnp.exp2((parts - top[None]) * ONE_SCALE), axis=0)
    return top + ENTROPY * jnp.log(total)


def lanes_to_rows(values, col_ref):
    for k in range(values.shape[0]):
        square = jnp.broadcast_to(values[k : k + 1, :], (LANES, LANES))
        col_ref[pl.ds(k * LANES, LANES), :] = square.T


def fold(reduce, part):
    return reduce(part.reshape(-1, ACCUMULATE, LANES), axis=0)


def scores(p_ref, q, col_ref, z_ref, s):
    slab = pl.ds(s * SLAB, SLAB)
    z = lax.dot_general(p_ref[slab, :], q, NT, preferred_element_type=jnp.float32)
    col = col_ref[slab, :]
    tops = []
    for h in range(HALVES):
        part = z[:, h * LANES : (h + 1) * LANES] + col
        z_ref[slab, pl.ds(h * LANES, LANES)] = part
        tops.append(fold(jnp.max, part))
    return tops


def weigh(z_ref, tops, s):
    slab = pl.ds(s * SLAB, SLAB)
    weights, totals = [], []
    for h, top in enumerate(tops):
        part = z_ref[slab, pl.ds(h * LANES, LANES)]
        weight = jnp.exp2((part - top) * TWO_SCALE)
        weights.append(weight)
        totals.append(fold(jnp.sum, weight))
    return weights, totals


def join(op, held, more):
    return more if held is None else [op(a, b) for a, b in zip(held, more)]


def settle(reduce, values):
    return [reduce(value, axis=0, keepdims=True) for value in values]


def log_sum(top, total):
    return 2.0 * top + ENTROPY * jnp.log(total)


def write_rows(row_ref, t, tops, totals):
    for h, (top, total) in enumerate(zip(tops, totals)):
        row_ref[pl.ds(t * HALVES + h, 1), :] = log_sum(top, total)


def run_chunks(p_ref, chunk, chunks, col_ref, z_refs, emit):
    slabs = p_ref.shape[0] // SLAB
    tops = None
    for t in range(chunks + 1):
        q = chunk(t) if t < chunks else None
        later, totals, weights = None, None, []
        for s in range(slabs):
            if t < chunks:
                later = join(jnp.maximum, later, scores(p_ref, q, col_ref, z_refs[t % 2], s))
            if t > 0:
                weight, total = weigh(z_refs[(t - 1) % 2], tops, s)
                totals = join(jnp.add, totals, total)
                weights.append(weight)
        if t > 0:
            emit(t - 1, tops, settle(jnp.sum, totals), weights)
        if t < chunks:
            tops = settle(jnp.max, later)


def log_sums(p_ref, q_ref, col_ref, z_refs, row_ref):
    run_chunks(
        p_ref,
        lambda t: q_ref[pl.ds(t * WIDTH, WIDTH), :],
        q_ref.shape[0] // WIDTH,
        col_ref,
        z_refs,
        lambda t, tops, totals, _: write_rows(row_ref, t, tops, totals),
    )


def first_kernel(
    p_hbm, q_hbm, p_mass_hbm, q_mass_hbm, out_ref, p_ref, q_ref, p_log_ref, q_log_ref,
    p_sems, sems, col_ref, even_ref, odd_ref, row_ref,
):
    loads = []
    for s in range(p_ref.shape[0] // SLAB):
        slab = pl.ds(s * SLAB, SLAB)
        loads.append(pltpu.make_async_copy(p_hbm.at[slab, :], p_ref.at[slab, :], p_sems.at[s]))
    load_q = pltpu.make_async_copy(q_hbm, q_ref, sems.at[0])
    masses = [
        pltpu.make_async_copy(p_mass_hbm, p_log_ref, sems.at[1]),
        pltpu.make_async_copy(q_mass_hbm, q_log_ref, sems.at[2]),
    ]
    for copy in loads[:1] + [load_q] + loads[1:] + masses:
        copy.start()

    def ready(s):
        loads[s].wait()
        slab = pl.ds(s * SLAB, SLAB)
        p = p_ref[slab, :].astype(jnp.float32)
        half = -0.5 * jnp.sum(p * p, axis=1, keepdims=True)
        col_ref[slab, :] = jnp.broadcast_to(half, (SLAB, LANES))

    for s in range(len(loads)):
        ready(s)
    load_q.wait()
    log_sums(p_ref, q_ref, col_ref, (even_ref, odd_ref), row_ref)
    for copy in masses:
        copy.wait()
    p_log_ref[...] = ENTROPY * jnp.log(p_log_ref[...])
    q_log_ref[...] = ENTROPY * jnp.log(q_log_ref[...])
    out_ref[...] = jnp.broadcast_to(row_ref[...][None], out_ref.shape)


def next_kernel(parts_ref, log_ref, p_ref, q_ref, out_ref, col_ref, even_ref, odd_ref, row_ref):
    lanes_to_rows(0.5 * (log_ref[...] - merge(parts_ref[...])), col_ref)
    log_sums(p_ref, q_ref, col_ref, (even_ref, odd_ref), row_ref)
    out_ref[...] = jnp.broadcast_to(row_ref[...][None], out_ref.shape)


def last_kernel(
    parts_ref, log_ref, p_ref, q_ref, feat_ref,
    sent_ref, keep_ref, own_ref, bias_ref, flip_ref, col_ref, even_ref, odd_ref,
):
    core = lax.rem(lax.axis_index("tgt"), 2)
    chips, _, share, depth = q_ref.shape
    half = chips * share
    width = feat_ref.shape[1]
    blocks = WIDTH // share
    bias = log_ref[...] - merge(parts_ref[...])
    bias_ref[...] = bias
    lanes_to_rows(0.5 * bias, col_ref)
    flip_ref[...] = feat_ref[...].astype(jnp.float32).T.astype(jnp.bfloat16)
    sent_ref[pl.ds(width, 8), :] = jnp.zeros((8, half), jnp.float32)
    own_ref[...] = jnp.zeros((8, half), jnp.float32)

    def chunk(t):
        own, first = divmod(t * WIDTH, half)
        q = q_ref[pl.ds(first // share, blocks), core if own else 1 - core]
        return q.reshape(WIDTH, depth)

    def emit(t, tops, totals, weights):
        own, first = divmod(t * WIDTH, half)
        slabs = [
            jnp.concatenate([weight.astype(jnp.bfloat16) for weight in slab], axis=1)
            for slab in weights
        ]
        lanes = pl.ds(first, WIDTH)
        lse = jnp.concatenate([log_sum(*pair) for pair in zip(tops, totals)], axis=1)
        scale = 1.0 / jnp.concatenate(totals, axis=1)
        sent_ref[pl.ds(width + own, 1), lanes] = lse
        own_ref[pl.ds(own, 1), lanes] = lse
        if own:
            for s, slab in enumerate(slabs):
                keep_ref[pl.ds(s * SLAB, SLAB), lanes] = slab
            own_ref[pl.ds(2, 1), lanes] = scale
        else:
            weight = jnp.concatenate(slabs, axis=0)
            numer = lax.dot_general(
                flip_ref[...], weight, NN, preferred_element_type=jnp.float32
            )
            sent_ref[pl.ds(0, width), lanes] = numer * scale

    run_chunks(p_ref, chunk, 2 * half // WIDTH, col_ref, (even_ref, odd_ref), emit)


def squares(ref, k):
    rows = ref[pl.ds(k * LANES, LANES), :].astype(jnp.float32)
    norms = jnp.sum(rows * rows, axis=1, keepdims=True)
    return jnp.broadcast_to(norms, (LANES, LANES)).T[:1, :]


def own_kernel(
    keep_ref, own_ref, flip_ref, bias_ref, p_ref, q_ref, log_ref, mean_ref, pot_ref, base_ref
):
    numer = lax.dot_general(
        flip_ref[...], keep_ref[...], NN, preferred_element_type=jnp.float32
    )
    mean_ref[...] = numer * own_ref[pl.ds(2, 1), :]
    for k in range(pot_ref.shape[0]):
        row = pl.ds(k, 1)
        pot_ref[row, :] = bias_ref[row, :] + squares(p_ref, k)
    for k in range(base_ref.shape[0]):
        row = pl.ds(k, 1)
        base_ref[row, :] = log_ref[row, :] + squares(q_ref, k)


def pair_kernel(mean_ref, own_ref, came_ref, out_ref, row_ref):
    width, half = mean_ref.shape
    chips = out_ref.shape[0]
    share = half // chips
    rows = half // LANES
    for side in range(2):
        mine = own_ref[pl.ds(1 - side, 1), :]
        other = came_ref[pl.ds(width + side, 1), :]
        top = jnp.maximum(mine, other)
        mine_share = jnp.exp2((mine - top) * ONE_SCALE)
        other_share = jnp.exp2((other - top) * ONE_SCALE)
        total = mine_share + other_share
        lse = top + ENTROPY * jnp.log(total)
        for k in range(rows):
            row_ref[pl.ds(side * rows + k, 1), :] = lse[:, k * LANES : (k + 1) * LANES]
        if side == 0:
            scale = 1.0 / total
            mine_share, other_share = mine_share * scale, other_share * scale
            step = LANES // share
            for k in range(rows):
                lanes = slice(k * LANES, (k + 1) * LANES)
                block = (
                    mean_ref[:, lanes] * mine_share[:, lanes]
                    + came_ref[pl.ds(0, width), lanes] * other_share[:, lanes]
                )
                out_ref[pl.ds(k * step, step), pl.ds(0, share), :] = block.T.reshape(
                    step, share, LANES
                )
    out_ref[:, pl.ds(share, 2 * rows), :] = jnp.broadcast_to(
        row_ref[...][None], (chips, 2 * rows, LANES)
    )


def final_kernel(landed_ref, base_ref, pot_ref, out_ref):
    index = lax.axis_index("tgt")
    core, chip = lax.rem(index, 2), lax.div(index, 2)
    share = out_ref.shape[0]
    chips = landed_ref.shape[0]
    mine = landed_ref[:, pl.ds(share + lax.div(chip, 2), 1), :].reshape(chips, LANES)
    mine = jnp.exp2((mine - jnp.max(mine, axis=0, keepdims=True)) * ONE_SCALE)
    mine = mine / jnp.sum(mine, axis=0, keepdims=True)
    mine = jnp.where(lax.rem(chip, 2) == 0, mine, pltpu.roll(mine, share, 1))
    mine = jnp.concatenate([mine, jnp.zeros((LANES - chips, LANES), jnp.float32)], axis=0).T
    total = jnp.zeros(out_ref.shape, jnp.float32)
    for b in range(chips):
        scale = jnp.broadcast_to(mine[:share, b : b + 1], out_ref.shape)
        total = total + landed_ref[b, pl.ds(0, share), :] * scale
    out_ref[...] = total
    whole = merge(landed_ref[:, pl.ds(share, landed_ref.shape[1] - share), :])
    rows = whole.shape[0] // 2
    even = jnp.where(core == 0, whole[:rows], whole[rows:])
    odd = jnp.where(core == 0, whole[rows:], whole[:rows])
    lane = lax.broadcasted_iota(jnp.int32, (rows, LANES), 1)
    first = jnp.where(lane < share, even, pltpu.roll(odd, share, 1))
    second = jnp.where(lane < share, pltpu.roll(even, share, 1), odd)
    for k in range(rows):
        for side, values in enumerate((first, second)):
            row = pl.ds(2 * k + side, 1)
            pot_ref[row, :] = base_ref[row, :] - values[k : k + 1]


def scratch(p, q):
    return [
        pltpu.VMEM((p.shape[0], LANES), jnp.float32),
        pltpu.VMEM((p.shape[0], WIDTH), jnp.float32),
        pltpu.VMEM((p.shape[0], WIDTH), jnp.float32),
        pltpu.VMEM((q.shape[0] // LANES, LANES), jnp.float32),
    ]


def call(kernel, args, outs, scratch_shapes, spaces=None):
    whole = pl.BlockSpec(memory_space=pltpu.VMEM)
    return pl.pallas_call(
        kernel,
        out_shape=outs,
        in_specs=spaces or [whole] * len(args),
        out_specs=jax.tree.map(lambda _: whole, outs),
        scratch_shapes=scratch_shapes,
        compiler_params=pltpu.CompilerParams(vmem_limit_bytes=VMEM_LIMIT),
    )(*args)


def local(source_embed, target_embed, target_feat, source_mass, target_mass):
    f32 = jnp.float32
    shape = jax.ShapeDtypeStruct
    n_src, n_tgt = lax.axis_size("src"), lax.axis_size("tgt")
    rows, depth = source_embed.shape
    width = target_feat.shape[1]
    share, half, chips = rows // n_tgt, rows // 2, n_tgt // 2
    src_mass = source_mass.reshape(-1, LANES)
    tgt_mass = target_mass.reshape(-1, LANES)
    src_rows, tgt_rows = src_mass.shape[0], tgt_mass.shape[0]
    to_src = shape((n_src, tgt_rows, LANES), f32)
    by_src = scratch(source_embed, target_embed)
    by_tgt = scratch(target_embed, source_embed)
    same_core = [list(range(core, n_tgt, 2)) for core in range(2)]
    swap = [(index, index ^ 1) for index in range(n_tgt)]

    sems = [pltpu.SemaphoreType.DMA((rows // SLAB,)), pltpu.SemaphoreType.DMA((3,))]
    inputs = [
        pltpu.with_memory_space_constraint(array, pltpu.HBM)
        for array in (source_embed, target_embed, src_mass, tgt_mass)
    ]
    held = [shape(array.shape, array.dtype) for array in inputs]
    sent, source_embed, target_embed, src_log, tgt_log = call(
        first_kernel,
        inputs,
        (to_src, *held),
        sems + by_src,
        [pl.BlockSpec(memory_space=pltpu.HBM)] * len(inputs),
    )
    parts = lax.all_to_all(sent, "src", 0, 0)
    one = shape((1, src_rows, LANES), f32)
    sent = call(next_kernel, (parts, tgt_log, target_embed, source_embed), one, by_tgt)
    parts = lax.all_gather(sent, "tgt", axis=0, tiled=True)
    sent = call(next_kernel, (parts, src_log, source_embed, target_embed), to_src, by_src)
    parts = lax.all_to_all(sent, "src", 0, 0)
    sent, keep, own, bias, turned = call(
        last_kernel,
        (parts, tgt_log, target_embed, source_embed.reshape(chips, 2, share, depth), target_feat),
        (
            shape((width + 8, half), f32),
            shape((target_embed.shape[0], half), jnp.bfloat16),
            shape((8, half), f32),
            shape((tgt_rows, LANES), f32),
            shape(target_feat.shape[::-1], jnp.bfloat16),
        ),
        by_tgt[:3],
    )
    came = lax.ppermute(sent, "tgt", swap)
    mean, target_pot, base = call(
        own_kernel,
        (keep, own, turned, bias, target_embed, source_embed, src_log),
        (shape((width, half), f32), shape(bias.shape, f32), shape(src_log.shape, f32)),
        [],
    )
    sent = call(
        pair_kernel,
        (mean, own, came),
        shape((chips, share + src_rows, LANES), f32),
        [pltpu.VMEM((src_rows, LANES), f32)],
    )
    landed = lax.all_to_all(sent, "tgt", 0, 0, axis_index_groups=same_core)
    source_pot, projected = call(
        final_kernel,
        (landed, base),
        (shape((src_rows, LANES), f32), shape((share, width), f32)),
        [],
    )
    return (source_pot.reshape(-1), target_pot.reshape(-1), projected)


def solution(mesh):
    placed = (P("src", None), P("tgt", None), P("tgt", None), P("src"), P("tgt"))
    return jax.shard_map(
        local,
        mesh=mesh,
        in_specs=placed,
        out_specs=(P("src"), P("tgt"), P(("src", "tgt"), None)),
        check_vma=False,
    )
```

```python
import math

import jax
import jax.numpy as jnp
from jax import lax
from jax.experimental import pallas as pl
from jax.experimental.pallas import tpu as pltpu
from jax.sharding import PartitionSpec as P

ENTROPY = 0.05
LANES = 128
WIDTH = 256
TWO_SCALE = 2.0 / ENTROPY
ONE_SCALE = 1.0 / ENTROPY * math.log2(math.e)
NT = (((1,), (1,)), ((), ()))
NN = (((1,), (0,)), ((), ()))
HALVES = WIDTH // LANES
SLAB = 512
ACCUMULATE = 32
VMEM_LIMIT = 40 * 1024 * 1024


def merge(parts):
    top = jnp.max(parts, axis=0)
    total = jnp.sum(jnp.exp2((parts - top[None]) * ONE_SCALE), axis=0)
    return top + ENTROPY * jnp.log(total)


def lanes_to_rows(values, col_ref):
    for k in range(values.shape[0]):
        square = jnp.broadcast_to(values[k : k + 1, :], (LANES, LANES))
        col_ref[pl.ds(k * LANES, LANES), :] = square.T


def fold(reduce, part):
    return reduce(part.reshape(-1, ACCUMULATE, LANES), axis=0)


def scores(p_ref, q, col_ref, z_ref, s):
    slab = pl.ds(s * SLAB, SLAB)
    z = lax.dot_general(p_ref[slab, :], q, NT, preferred_element_type=jnp.float32)
    col = col_ref[slab, :]
    tops = []
    for h in range(HALVES):
        part = z[:, h * LANES : (h + 1) * LANES] + col
        z_ref[slab, pl.ds(h * LANES, LANES)] = part
        tops.append(fold(jnp.max, part))
    return tops


def weigh(z_ref, tops, s):
    slab = pl.ds(s * SLAB, SLAB)
    weights, totals = [], []
    for h, top in enumerate(tops):
        part = z_ref[slab, pl.ds(h * LANES, LANES)]
        weight = jnp.exp((part - top) * TWO_SCALE)
        weights.append(weight)
        totals.append(fold(jnp.sum, weight))
    return weights, totals


def join(op, held, more):
    return more if held is None else [op(a, b) for a, b in zip(held, more)]


def settle(reduce, values):
    return [reduce(value, axis=0, keepdims=True) for value in values]


def log_sum(top, total):
    return 2.0 * top + ENTROPY * jnp.log(total)


def write_rows(row_ref, t, tops, totals):
    for h, (top, total) in enumerate(zip(tops, totals)):
        row_ref[pl.ds(t * HALVES + h, 1), :] = log_sum(top, total)


def run_chunks(p_ref, chunk, chunks, col_ref, z_refs, emit, ready=lambda s: None):
    slabs = p_ref.shape[0] // SLAB
    tops = None
    for t in range(chunks + 1):
        q = chunk(t) if t < chunks else None
        later, totals, weights = None, None, []
        for s in range(slabs):
            if t == 0:
                ready(s)
            if t < chunks:
                later = join(jnp.maximum, later, scores(p_ref, q, col_ref, z_refs[t % 2], s))
            if t > 0:
                weight, total = weigh(z_refs[(t - 1) % 2], tops, s)
                totals = join(jnp.add, totals, total)
                weights.append(weight)
        if t > 0:
            emit(t - 1, tops, settle(jnp.sum, totals), weights)
        if t < chunks:
            tops = settle(jnp.max, later)


def log_sums(p_ref, q_ref, col_ref, z_refs, row_ref, **more):
    run_chunks(
        p_ref,
        lambda t: q_ref[pl.ds(t * WIDTH, WIDTH), :],
        q_ref.shape[0] // WIDTH,
        col_ref,
        z_refs,
        lambda t, tops, totals, _: write_rows(row_ref, t, tops, totals),
        **more,
    )


def first_kernel(
    p_hbm, q_hbm, p_mass_hbm, q_mass_hbm, out_ref, p_ref, q_ref, p_log_ref, q_log_ref,
    p_sems, sems, col_ref, even_ref, odd_ref, row_ref,
):
    loads = []
    for s in range(p_ref.shape[0] // SLAB):
        slab = pl.ds(s * SLAB, SLAB)
        loads.append(pltpu.make_async_copy(p_hbm.at[slab, :], p_ref.at[slab, :], p_sems.at[s]))
    load_q = pltpu.make_async_copy(q_hbm, q_ref, sems.at[0])
    masses = [
        pltpu.make_async_copy(p_mass_hbm, p_log_ref, sems.at[1]),
        pltpu.make_async_copy(q_mass_hbm, q_log_ref, sems.at[2]),
    ]
    for copy in loads[:1] + [load_q] + loads[1:] + masses:
        copy.start()

    def ready(s):
        loads[s].wait()
        slab = pl.ds(s * SLAB, SLAB)
        p = p_ref[slab, :].astype(jnp.float32)
        half = -0.5 * jnp.sum(p * p, axis=1, keepdims=True)
        col_ref[slab, :] = jnp.broadcast_to(half, (SLAB, LANES))

    load_q.wait()
    log_sums(p_ref, q_ref, col_ref, (even_ref, odd_ref), row_ref, ready=ready)
    for copy in masses:
        copy.wait()
    p_log_ref[...] = ENTROPY * jnp.log(p_log_ref[...])
    q_log_ref[...] = ENTROPY * jnp.log(q_log_ref[...])
    out_ref[...] = jnp.broadcast_to(row_ref[...][None], out_ref.shape)


def next_kernel(parts_ref, log_ref, p_ref, q_ref, out_ref, col_ref, even_ref, odd_ref, row_ref):
    lanes_to_rows(0.5 * (log_ref[...] - merge(parts_ref[...])), col_ref)
    log_sums(p_ref, q_ref, col_ref, (even_ref, odd_ref), row_ref)
    out_ref[...] = jnp.broadcast_to(row_ref[...][None], out_ref.shape)


def last_kernel(
    parts_ref, log_ref, p_ref, q_ref, feat_ref,
    sent_ref, keep_ref, own_ref, bias_ref, flip_ref, col_ref, even_ref, odd_ref,
):
    core = lax.rem(lax.axis_index("tgt"), 2)
    chips, _, share, depth = q_ref.shape
    half = chips * share
    width = feat_ref.shape[1]
    blocks = WIDTH // share
    bias = log_ref[...] - merge(parts_ref[...])
    bias_ref[...] = bias
    lanes_to_rows(0.5 * bias, col_ref)
    flip_ref[...] = feat_ref[...].astype(jnp.float32).T.astype(jnp.bfloat16)
    sent_ref[pl.ds(width, 8), :] = jnp.zeros((8, half), jnp.float32)
    own_ref[...] = jnp.zeros((8, half), jnp.float32)

    def chunk(t):
        own, first = divmod(t * WIDTH, half)
        q = q_ref[pl.ds(first // share, blocks), core if own else 1 - core]
        return q.reshape(WIDTH, depth)

    def emit(t, tops, totals, weights):
        own, first = divmod(t * WIDTH, half)
        slabs = [
            jnp.concatenate([weight.astype(jnp.bfloat16) for weight in slab], axis=1)
            for slab in weights
        ]
        lanes = pl.ds(first, WIDTH)
        lse = jnp.concatenate([log_sum(*pair) for pair in zip(tops, totals)], axis=1)
        scale = 1.0 / jnp.concatenate(totals, axis=1)
        sent_ref[pl.ds(width + own, 1), lanes] = lse
        own_ref[pl.ds(own, 1), lanes] = lse
        if own:
            for s, slab in enumerate(slabs):
                keep_ref[pl.ds(s * SLAB, SLAB), lanes] = slab
            own_ref[pl.ds(2, 1), lanes] = scale
        else:
            weight = jnp.concatenate(slabs, axis=0)
            numer = lax.dot_general(
                flip_ref[...], weight, NN, preferred_element_type=jnp.float32
            )
            sent_ref[pl.ds(0, width), lanes] = numer * scale

    run_chunks(p_ref, chunk, 2 * half // WIDTH, col_ref, (even_ref, odd_ref), emit)


def squares(ref, k):
    rows = ref[pl.ds(k * LANES, LANES), :].astype(jnp.float32)
    norms = jnp.sum(rows * rows, axis=1, keepdims=True)
    return jnp.broadcast_to(norms, (LANES, LANES)).T[:1, :]


def own_kernel(
    keep_ref, own_ref, flip_ref, bias_ref, p_ref, q_ref, log_ref, mean_ref, pot_ref, base_ref
):
    numer = lax.dot_general(
        flip_ref[...], keep_ref[...], NN, preferred_element_type=jnp.float32
    )
    mean_ref[...] = numer * own_ref[pl.ds(2, 1), :]
    for k in range(pot_ref.shape[0]):
        row = pl.ds(k, 1)
        pot_ref[row, :] = bias_ref[row, :] + squares(p_ref, k)
    for k in range(base_ref.shape[0]):
        row = pl.ds(k, 1)
        base_ref[row, :] = log_ref[row, :] + squares(q_ref, k)


def pair_kernel(mean_ref, own_ref, came_ref, out_ref, row_ref):
    width, half = mean_ref.shape
    chips = out_ref.shape[0]
    share = half // chips
    rows = half // LANES
    for side in range(2):
        mine = own_ref[pl.ds(1 - side, 1), :]
        other = came_ref[pl.ds(width + side, 1), :]
        top = jnp.maximum(mine, other)
        mine_share = jnp.exp2((mine - top) * ONE_SCALE)
        other_share = jnp.exp2((other - top) * ONE_SCALE)
        total = mine_share + other_share
        lse = top + ENTROPY * jnp.log(total)
        for k in range(rows):
            row_ref[pl.ds(side * rows + k, 1), :] = lse[:, k * LANES : (k + 1) * LANES]
        if side == 0:
            scale = 1.0 / total
            mine_share, other_share = mine_share * scale, other_share * scale
            step = LANES // share
            for k in range(rows):
                lanes = slice(k * LANES, (k + 1) * LANES)
                block = (
                    mean_ref[:, lanes] * mine_share[:, lanes]
                    + came_ref[pl.ds(0, width), lanes] * other_share[:, lanes]
                )
                out_ref[pl.ds(k * step, step), pl.ds(0, share), :] = block.T.reshape(
                    step, share, LANES
                )
    out_ref[:, pl.ds(share, 2 * rows), :] = jnp.broadcast_to(
        row_ref[...][None], (chips, 2 * rows, LANES)
    )


def final_kernel(landed_ref, base_ref, pot_ref, out_ref):
    index = lax.axis_index("tgt")
    core, chip = lax.rem(index, 2), lax.div(index, 2)
    share = out_ref.shape[0]
    chips = landed_ref.shape[0]
    mine = landed_ref[:, pl.ds(share + lax.div(chip, 2), 1), :].reshape(chips, LANES)
    mine = jnp.exp2((mine - jnp.max(mine, axis=0, keepdims=True)) * ONE_SCALE)
    mine = mine / jnp.sum(mine, axis=0, keepdims=True)
    mine = jnp.where(lax.rem(chip, 2) == 0, mine, pltpu.roll(mine, share, 1))
    mine = jnp.concatenate([mine, jnp.zeros((LANES - chips, LANES), jnp.float32)], axis=0).T
    total = jnp.zeros(out_ref.shape, jnp.float32)
    for b in range(chips):
        scale = jnp.broadcast_to(mine[:share, b : b + 1], out_ref.shape)
        total = total + landed_ref[b, pl.ds(0, share), :] * scale
    out_ref[...] = total
    whole = merge(landed_ref[:, pl.ds(share, landed_ref.shape[1] - share), :])
    rows = whole.shape[0] // 2
    even = jnp.where(core == 0, whole[:rows], whole[rows:])
    odd = jnp.where(core == 0, whole[rows:], whole[:rows])
    lane = lax.broadcasted_iota(jnp.int32, (rows, LANES), 1)
    first = jnp.where(lane < share, even, pltpu.roll(odd, share, 1))
    second = jnp.where(lane < share, pltpu.roll(even, share, 1), odd)
    for k in range(rows):
        for side, values in enumerate((first, second)):
            row = pl.ds(2 * k + side, 1)
            pot_ref[row, :] = base_ref[row, :] - values[k : k + 1]


def scratch(p, q):
    return [
        pltpu.VMEM((p.shape[0], LANES), jnp.float32),
        pltpu.VMEM((p.shape[0], WIDTH), jnp.float32),
        pltpu.VMEM((p.shape[0], WIDTH), jnp.float32),
        pltpu.VMEM((q.shape[0] // LANES, LANES), jnp.float32),
    ]


def call(kernel, args, outs, scratch_shapes, spaces=None):
    whole = pl.BlockSpec(memory_space=pltpu.VMEM)
    return pl.pallas_call(
        kernel,
        out_shape=outs,
        in_specs=spaces or [whole] * len(args),
        out_specs=jax.tree.map(lambda _: whole, outs),
        scratch_shapes=scratch_shapes,
        compiler_params=pltpu.CompilerParams(vmem_limit_bytes=VMEM_LIMIT),
    )(*args)


def local(source_embed, target_embed, target_feat, source_mass, target_mass):
    f32 = jnp.float32
    shape = jax.ShapeDtypeStruct
    n_src, n_tgt = lax.axis_size("src"), lax.axis_size("tgt")
    rows, depth = source_embed.shape
    width = target_feat.shape[1]
    share, half, chips = rows // n_tgt, rows // 2, n_tgt // 2
    src_mass = source_mass.reshape(-1, LANES)
    tgt_mass = target_mass.reshape(-1, LANES)
    src_rows, tgt_rows = src_mass.shape[0], tgt_mass.shape[0]
    to_src = shape((n_src, tgt_rows, LANES), f32)
    to_tgt = shape((n_tgt, src_rows, LANES), f32)
    by_src = scratch(source_embed, target_embed)
    by_tgt = scratch(target_embed, source_embed)
    same_core = [list(range(core, n_tgt, 2)) for core in range(2)]
    swap = [(index, index ^ 1) for index in range(n_tgt)]

    sems = [pltpu.SemaphoreType.DMA((rows // SLAB,)), pltpu.SemaphoreType.DMA((3,))]
    inputs = [
        pltpu.with_memory_space_constraint(array, pltpu.HBM)
        for array in (source_embed, target_embed, src_mass, tgt_mass)
    ]
    held = [shape(array.shape, array.dtype) for array in inputs]
    sent, source_embed, target_embed, src_log, tgt_log = call(
        first_kernel,
        inputs,
        (to_src, *held),
        sems + by_src,
        [pl.BlockSpec(memory_space=pltpu.HBM)] * len(inputs),
    )
    parts = lax.all_to_all(sent, "src", 0, 0)
    sent = call(next_kernel, (parts, tgt_log, target_embed, source_embed), to_tgt, by_tgt)
    parts = lax.all_to_all(sent, "tgt", 0, 0)
    sent = call(next_kernel, (parts, src_log, source_embed, target_embed), to_src, by_src)
    parts = lax.all_to_all(sent, "src", 0, 0)
    sent, keep, own, bias, turned = call(
        last_kernel,
        (parts, tgt_log, target_embed, source_embed.reshape(chips, 2, share, depth), target_feat),
        (
            shape((width + 8, half), f32),
            shape((target_embed.shape[0], half), jnp.bfloat16),
            shape((8, half), f32),
            shape((tgt_rows, LANES), f32),
            shape(target_feat.shape[::-1], jnp.bfloat16),
        ),
        by_tgt[:3],
    )
    came = lax.ppermute(sent, "tgt", swap)
    mean, target_pot, base = call(
        own_kernel,
        (keep, own, turned, bias, target_embed, source_embed, src_log),
        (shape((width, half), f32), shape(bias.shape, f32), shape(src_log.shape, f32)),
        [],
    )
    sent = call(
        pair_kernel,
        (mean, own, came),
        shape((chips, share + src_rows, LANES), f32),
        [pltpu.VMEM((src_rows, LANES), f32)],
    )
    landed = lax.all_to_all(sent, "tgt", 0, 0, axis_index_groups=same_core)
    source_pot, projected = call(
        final_kernel,
        (landed, base),
        (shape((src_rows, LANES), f32), shape((share, width), f32)),
        [],
    )
    return (source_pot.reshape(-1), target_pot.reshape(-1), projected)


def solution(mesh):
    placed = (P("src", None), P("tgt", None), P("tgt", None), P("src"), P("tgt"))
    return jax.shard_map(
        local,
        mesh=mesh,
        in_specs=placed,
        out_specs=(P("src"), P("tgt"), P(("src", "tgt"), None)),
        check_vma=False,
    )
```

```python
import math

import jax
import jax.numpy as jnp
from jax import lax
from jax.experimental import pallas as pl
from jax.experimental.pallas import tpu as pltpu
from jax.sharding import PartitionSpec as P

ENTROPY = 0.05
LANES = 128
WIDTH = 256
ONE_SCALE = 1.0 / ENTROPY * math.log2(math.e)
TWO_SCALE = 2.0 * ONE_SCALE
ONE_UNIT = ENTROPY * math.log(2.0)
LOWEST, HIGHEST = 2.0**-90, 2.0**110
NT = (((1,), (1,)), ((), ()))
NN = (((1,), (0,)), ((), ()))
HALVES = WIDTH // LANES
SLAB = 512
ACCUMULATE = 32
VMEM_LIMIT = 40 * 1024 * 1024


def merge(parts):
    top = jnp.max(parts, axis=0)
    total = jnp.sum(jnp.exp2((parts - top[None]) * ONE_SCALE), axis=0)
    return top + ENTROPY * jnp.log(total)


def lanes_to_rows(values, col_ref):
    for k in range(values.shape[0]):
        square = jnp.broadcast_to(values[k : k + 1, :], (LANES, LANES))
        col_ref[pl.ds(k * LANES, LANES), :] = square.T


def fold(reduce, part):
    return reduce(part.reshape(-1, ACCUMULATE, LANES), axis=0)


def exponents(p_ref, q, col_ref, s):
    slab = pl.ds(s * SLAB, SLAB)
    cross = lax.dot_general(p_ref[slab, :], q, NT, preferred_element_type=jnp.float32)
    col = col_ref[slab, :]
    return [cross[:, h * LANES : (h + 1) * LANES] * TWO_SCALE + col for h in range(HALVES)]


def scores(p_ref, q, col_ref, z_ref, s):
    slab = pl.ds(s * SLAB, SLAB)
    tops = []
    for h, part in enumerate(exponents(p_ref, q, col_ref, s)):
        z_ref[slab, pl.ds(h * LANES, LANES)] = part
        tops.append(fold(jnp.max, part))
    return tops


def weigh(z_ref, tops, s):
    slab = pl.ds(s * SLAB, SLAB)
    weights, totals = [], []
    for h, top in enumerate(tops):
        part = z_ref[slab, pl.ds(h * LANES, LANES)]
        weight = jnp.exp2(part - top)
        weights.append(weight)
        totals.append(fold(jnp.sum, weight))
    return weights, totals


def join(op, held, more):
    return more if held is None else [op(a, b) for a, b in zip(held, more)]


def settle(reduce, values):
    return [reduce(value, axis=0, keepdims=True) for value in values]


def log_sum(top, total):
    return ONE_UNIT * top + ENTROPY * jnp.log(total)


def run_chunks(p_ref, chunk, chunks, col_ref, z_refs, emit):
    slabs = p_ref.shape[0] // SLAB
    tops = None
    for t in range(chunks + 1):
        q = chunk(t) if t < chunks else None
        later, totals, weights = None, None, []
        for s in range(slabs):
            if t < chunks:
                later = join(jnp.maximum, later, scores(p_ref, q, col_ref, z_refs[t % 2], s))
            if t > 0:
                weight, total = weigh(z_refs[(t - 1) % 2], tops, s)
                totals = join(jnp.add, totals, total)
                weights.append(weight)
        if t > 0:
            emit(t - 1, tops, settle(jnp.sum, totals), weights)
        if t < chunks:
            tops = settle(jnp.max, later)


def log_sums(p_ref, q_ref, col_ref, z_ref, row_ref, ready=lambda s: None):
    slabs, chunks = p_ref.shape[0] // SLAB, q_ref.shape[0] // WIDTH
    totals = [None] * chunks
    for s in range(slabs):
        ready(s)
        for t in range(chunks):
            parts = exponents(p_ref, q_ref[pl.ds(t * WIDTH, WIDTH), :], col_ref, s)
            totals[t] = join(jnp.add, totals[t], [fold(jnp.sum, jnp.exp2(part)) for part in parts])
    for t in range(chunks):
        for h, total in enumerate(settle(jnp.sum, totals[t])):
            row_ref[pl.ds(t * HALVES + h, 1), :] = total
    sums = row_ref[...]
    row_ref[...] = ENTROPY * jnp.log(sums)
    safe = jnp.logical_and(jnp.min(sums) >= LOWEST, jnp.max(sums) <= HIGHEST)

    @pl.when(jnp.logical_not(safe))
    def _():
        @pl.loop(0, chunks)
        def _(t):
            q = q_ref[pl.ds(pl.multiple_of(t * WIDTH, WIDTH), WIDTH), :]
            tops, sums = None, None
            for s in range(slabs):
                tops = join(jnp.maximum, tops, scores(p_ref, q, col_ref, z_ref, s))
            tops = settle(jnp.max, tops)
            for s in range(slabs):
                sums = join(jnp.add, sums, weigh(z_ref, tops, s)[1])
            for h, pair in enumerate(zip(tops, settle(jnp.sum, sums))):
                row_ref[pl.ds(t * HALVES + h, 1), :] = log_sum(*pair)


def first_kernel(
    p_hbm, q_hbm, p_mass_hbm, q_mass_hbm, out_ref, p_ref, q_ref, p_log_ref, q_log_ref,
    p_sems, sems, col_ref, z_ref, row_ref,
):
    loads = []
    for s in range(p_ref.shape[0] // SLAB):
        slab = pl.ds(s * SLAB, SLAB)
        loads.append(pltpu.make_async_copy(p_hbm.at[slab, :], p_ref.at[slab, :], p_sems.at[s]))
    load_q = pltpu.make_async_copy(q_hbm, q_ref, sems.at[0])
    masses = [
        pltpu.make_async_copy(p_mass_hbm, p_log_ref, sems.at[1]),
        pltpu.make_async_copy(q_mass_hbm, q_log_ref, sems.at[2]),
    ]
    for copy in loads[:1] + [load_q] + loads[1:] + masses:
        copy.start()

    def ready(s):
        loads[s].wait()
        slab = pl.ds(s * SLAB, SLAB)
        p = p_ref[slab, :].astype(jnp.float32)
        norms = jnp.sum(p * p, axis=1, keepdims=True)
        col_ref[slab, :] = jnp.broadcast_to(-ONE_SCALE * norms, (SLAB, LANES))
        if s == 0:
            load_q.wait()

    log_sums(p_ref, q_ref, col_ref, z_ref, row_ref, ready)
    for copy in masses:
        copy.wait()
    p_log_ref[...] = ENTROPY * jnp.log(p_log_ref[...])
    q_log_ref[...] = ENTROPY * jnp.log(q_log_ref[...])
    out_ref[...] = jnp.broadcast_to(row_ref[...][None], out_ref.shape)


def next_kernel(parts_ref, log_ref, p_ref, q_ref, out_ref, col_ref, z_ref, row_ref):
    lanes_to_rows(ONE_SCALE * (log_ref[...] - merge(parts_ref[...])), col_ref)
    log_sums(p_ref, q_ref, col_ref, z_ref, row_ref)
    out_ref[...] = jnp.broadcast_to(row_ref[...][None], out_ref.shape)


def last_kernel(
    parts_ref, log_ref, p_ref, q_ref, feat_ref,
    sent_ref, keep_ref, own_ref, bias_ref, flip_ref, col_ref, even_ref, odd_ref,
):
    core = lax.rem(lax.axis_index("tgt"), 2)
    chips, _, share, depth = q_ref.shape
    half = chips * share
    width = feat_ref.shape[1]
    blocks = WIDTH // share
    bias = log_ref[...] - merge(parts_ref[...])
    bias_ref[...] = bias
    lanes_to_rows(ONE_SCALE * bias, col_ref)
    flip_ref[...] = feat_ref[...].astype(jnp.float32).T.astype(jnp.bfloat16)
    sent_ref[pl.ds(width, 8), :] = jnp.zeros((8, half), jnp.float32)
    own_ref[...] = jnp.zeros((8, half), jnp.float32)

    def chunk(t):
        own, first = divmod(t * WIDTH, half)
        q = q_ref[pl.ds(first // share, blocks), core if own else 1 - core]
        return q.reshape(WIDTH, depth)

    def emit(t, tops, totals, weights):
        own, first = divmod(t * WIDTH, half)
        slabs = [
            jnp.concatenate([weight.astype(jnp.bfloat16) for weight in slab], axis=1)
            for slab in weights
        ]
        lanes = pl.ds(first, WIDTH)
        lse = jnp.concatenate([log_sum(*pair) for pair in zip(tops, totals)], axis=1)
        scale = 1.0 / jnp.concatenate(totals, axis=1)
        sent_ref[pl.ds(width + own, 1), lanes] = lse
        own_ref[pl.ds(own, 1), lanes] = lse
        if own:
            for s, slab in enumerate(slabs):
                keep_ref[pl.ds(s * SLAB, SLAB), lanes] = slab
            own_ref[pl.ds(2, 1), lanes] = scale
        else:
            weight = jnp.concatenate(slabs, axis=0)
            numer = lax.dot_general(
                flip_ref[...], weight, NN, preferred_element_type=jnp.float32
            )
            sent_ref[pl.ds(0, width), lanes] = numer * scale

    run_chunks(p_ref, chunk, 2 * half // WIDTH, col_ref, (even_ref, odd_ref), emit)


def squares(ref, k):
    rows = ref[pl.ds(k * LANES, LANES), :].astype(jnp.float32)
    norms = jnp.sum(rows * rows, axis=1, keepdims=True)
    return jnp.broadcast_to(norms, (LANES, LANES)).T[:1, :]


def own_kernel(
    keep_ref, own_ref, flip_ref, bias_ref, p_ref, q_ref, log_ref, mean_ref, pot_ref, base_ref
):
    numer = lax.dot_general(
        flip_ref[...], keep_ref[...], NN, preferred_element_type=jnp.float32
    )
    mean_ref[...] = numer * own_ref[pl.ds(2, 1), :]
    for k in range(pot_ref.shape[0]):
        row = pl.ds(k, 1)
        pot_ref[row, :] = bias_ref[row, :] + squares(p_ref, k)
    for k in range(base_ref.shape[0]):
        row = pl.ds(k, 1)
        base_ref[row, :] = log_ref[row, :] + squares(q_ref, k)


def pair_kernel(mean_ref, own_ref, came_ref, out_ref, row_ref):
    width, half = mean_ref.shape
    chips = out_ref.shape[0]
    share = half // chips
    rows = half // LANES
    for side in range(2):
        mine = own_ref[pl.ds(1 - side, 1), :]
        other = came_ref[pl.ds(width + side, 1), :]
        top = jnp.maximum(mine, other)
        mine_share = jnp.exp2((mine - top) * ONE_SCALE)
        other_share = jnp.exp2((other - top) * ONE_SCALE)
        total = mine_share + other_share
        lse = top + ENTROPY * jnp.log(total)
        for k in range(rows):
            row_ref[pl.ds(side * rows + k, 1), :] = lse[:, k * LANES : (k + 1) * LANES]
        if side == 0:
            scale = 1.0 / total
            mine_share, other_share = mine_share * scale, other_share * scale
            step = LANES // share
            for k in range(rows):
                lanes = slice(k * LANES, (k + 1) * LANES)
                block = (
                    mean_ref[:, lanes] * mine_share[:, lanes]
                    + came_ref[pl.ds(0, width), lanes] * other_share[:, lanes]
                )
                out_ref[pl.ds(k * step, step), pl.ds(0, share), :] = block.T.reshape(
                    step, share, LANES
                )
    out_ref[:, pl.ds(share, 2 * rows), :] = jnp.broadcast_to(
        row_ref[...][None], (chips, 2 * rows, LANES)
    )


def final_kernel(landed_ref, base_ref, pot_ref, out_ref):
    index = lax.axis_index("tgt")
    core, chip = lax.rem(index, 2), lax.div(index, 2)
    share = out_ref.shape[0]
    chips = landed_ref.shape[0]
    mine = landed_ref[:, pl.ds(share + lax.div(chip, 2), 1), :].reshape(chips, LANES)
    mine = jnp.exp2((mine - jnp.max(mine, axis=0, keepdims=True)) * ONE_SCALE)
    mine = mine / jnp.sum(mine, axis=0, keepdims=True)
    mine = jnp.where(lax.rem(chip, 2) == 0, mine, pltpu.roll(mine, share, 1))
    mine = jnp.concatenate([mine, jnp.zeros((LANES - chips, LANES), jnp.float32)], axis=0).T
    total = jnp.zeros(out_ref.shape, jnp.float32)
    for b in range(chips):
        scale = jnp.broadcast_to(mine[:share, b : b + 1], out_ref.shape)
        total = total + landed_ref[b, pl.ds(0, share), :] * scale
    out_ref[...] = total
    whole = merge(landed_ref[:, pl.ds(share, landed_ref.shape[1] - share), :])
    rows = whole.shape[0] // 2
    even = jnp.where(core == 0, whole[:rows], whole[rows:])
    odd = jnp.where(core == 0, whole[rows:], whole[:rows])
    lane = lax.broadcasted_iota(jnp.int32, (rows, LANES), 1)
    first = jnp.where(lane < share, even, pltpu.roll(odd, share, 1))
    second = jnp.where(lane < share, pltpu.roll(even, share, 1), odd)
    for k in range(rows):
        for side, values in enumerate((first, second)):
            row = pl.ds(2 * k + side, 1)
            pot_ref[row, :] = base_ref[row, :] - values[k : k + 1]


def scratch(p, q):
    return [
        pltpu.VMEM((p.shape[0], LANES), jnp.float32),
        pltpu.VMEM((p.shape[0], WIDTH), jnp.float32),
        pltpu.VMEM((q.shape[0] // LANES, LANES), jnp.float32),
    ]


def call(kernel, args, outs, scratch_shapes, spaces=None):
    whole = pl.BlockSpec(memory_space=pltpu.VMEM)
    return pl.pallas_call(
        kernel,
        out_shape=outs,
        in_specs=spaces or [whole] * len(args),
        out_specs=jax.tree.map(lambda _: whole, outs),
        scratch_shapes=scratch_shapes,
        compiler_params=pltpu.CompilerParams(vmem_limit_bytes=VMEM_LIMIT),
    )(*args)


def local(source_embed, target_embed, target_feat, source_mass, target_mass):
    f32 = jnp.float32
    shape = jax.ShapeDtypeStruct
    n_src, n_tgt = lax.axis_size("src"), lax.axis_size("tgt")
    rows, depth = source_embed.shape
    width = target_feat.shape[1]
    share, half, chips = rows // n_tgt, rows // 2, n_tgt // 2
    src_mass = source_mass.reshape(-1, LANES)
    tgt_mass = target_mass.reshape(-1, LANES)
    src_rows, tgt_rows = src_mass.shape[0], tgt_mass.shape[0]
    to_src = shape((n_src, tgt_rows, LANES), f32)
    to_tgt = shape((n_tgt, src_rows, LANES), f32)
    by_src = scratch(source_embed, target_embed)
    by_tgt = scratch(target_embed, source_embed)
    same_core = [list(range(core, n_tgt, 2)) for core in range(2)]
    swap = [(index, index ^ 1) for index in range(n_tgt)]

    sems = [pltpu.SemaphoreType.DMA((rows // SLAB,)), pltpu.SemaphoreType.DMA((3,))]
    inputs = [
        pltpu.with_memory_space_constraint(array, pltpu.HBM)
        for array in (source_embed, target_embed, src_mass, tgt_mass)
    ]
    held = [shape(array.shape, array.dtype) for array in inputs]
    sent, source_embed, target_embed, src_log, tgt_log = call(
        first_kernel,
        inputs,
        (to_src, *held),
        sems + by_src,
        [pl.BlockSpec(memory_space=pltpu.HBM)] * len(inputs),
    )
    parts = lax.all_to_all(sent, "src", 0, 0)
    sent = call(next_kernel, (parts, tgt_log, target_embed, source_embed), to_tgt, by_tgt)
    parts = lax.all_to_all(sent, "tgt", 0, 0)
    sent = call(next_kernel, (parts, src_log, source_embed, target_embed), to_src, by_src)
    parts = lax.all_to_all(sent, "src", 0, 0)
    sent, keep, own, bias, turned = call(
        last_kernel,
        (parts, tgt_log, target_embed, source_embed.reshape(chips, 2, share, depth), target_feat),
        (
            shape((width + 8, half), f32),
            shape((target_embed.shape[0], half), jnp.bfloat16),
            shape((8, half), f32),
            shape((tgt_rows, LANES), f32),
            shape(target_feat.shape[::-1], jnp.bfloat16),
        ),
        by_tgt[:2] + by_tgt[1:2],
    )
    came = lax.ppermute(sent, "tgt", swap)
    mean, target_pot, base = call(
        own_kernel,
        (keep, own, turned, bias, target_embed, source_embed, src_log),
        (shape((width, half), f32), shape(bias.shape, f32), shape(src_log.shape, f32)),
        [],
    )
    sent = call(
        pair_kernel,
        (mean, own, came),
        shape((chips, share + src_rows, LANES), f32),
        [pltpu.VMEM((src_rows, LANES), f32)],
    )
    landed = lax.all_to_all(sent, "tgt", 0, 0, axis_index_groups=same_core)
    source_pot, projected = call(
        final_kernel,
        (landed, base),
        (shape((src_rows, LANES), f32), shape((share, width), f32)),
        [],
    )
    return (source_pot.reshape(-1), target_pot.reshape(-1), projected)


def solution(mesh):
    placed = (P("src", None), P("tgt", None), P("tgt", None), P("src"), P("tgt"))
    return jax.shard_map(
        local,
        mesh=mesh,
        in_specs=placed,
        out_specs=(P("src"), P("tgt"), P(("src", "tgt"), None)),
        check_vma=False,
    )
```

```python
import math

import jax
import jax.numpy as jnp
from jax import lax
from jax.experimental import pallas as pl
from jax.experimental.pallas import tpu as pltpu
from jax.sharding import PartitionSpec as P

ENTROPY = 0.05
LANES = 128
WIDTH = 256
ONE_SCALE = 1.0 / ENTROPY * math.log2(math.e)
TWO_SCALE = 2.0 * ONE_SCALE
ONE_UNIT = ENTROPY * math.log(2.0)
LOWEST, HIGHEST = 2.0**-90, 2.0**110
NT = (((1,), (1,)), ((), ()))
NN = (((1,), (0,)), ((), ()))
HALVES = WIDTH // LANES
SLAB = 512
PIECE = 256
ACCUMULATE = 32
VMEM_LIMIT = 40 * 1024 * 1024


def merge(parts):
    top = jnp.max(parts, axis=0)
    total = jnp.sum(jnp.exp2((parts - top[None]) * ONE_SCALE), axis=0)
    return top + ENTROPY * jnp.log(total)


def lanes_to_rows(values, col_ref):
    for k in range(values.shape[0]):
        square = jnp.broadcast_to(values[k : k + 1, :], (LANES, LANES))
        col_ref[pl.ds(k * LANES, LANES), :] = square.T


def fold(reduce, part):
    return reduce(part.reshape(-1, ACCUMULATE, LANES), axis=0)


def exponents(p_ref, q, col_ref, s, rows=SLAB):
    slab = pl.ds(s * rows, rows)
    cross = lax.dot_general(p_ref[slab, :], q, NT, preferred_element_type=jnp.float32)
    col = col_ref[slab, :]
    return [cross[:, h * LANES : (h + 1) * LANES] * TWO_SCALE + col for h in range(HALVES)]


def scores(p_ref, q, col_ref, z_ref, s):
    slab = pl.ds(s * SLAB, SLAB)
    tops = []
    for h, part in enumerate(exponents(p_ref, q, col_ref, s)):
        z_ref[slab, pl.ds(h * LANES, LANES)] = part
        tops.append(fold(jnp.max, part))
    return tops


def weigh(z_ref, tops, s):
    slab = pl.ds(s * SLAB, SLAB)
    weights, totals = [], []
    for h, top in enumerate(tops):
        part = z_ref[slab, pl.ds(h * LANES, LANES)]
        weight = jnp.exp2(part - top)
        weights.append(weight)
        totals.append(fold(jnp.sum, weight))
    return weights, totals


def join(op, held, more):
    return more if held is None else [op(a, b) for a, b in zip(held, more)]


def settle(reduce, values):
    return [reduce(value, axis=0, keepdims=True) for value in values]


def log_sum(top, total):
    return ONE_UNIT * top + ENTROPY * jnp.log(total)


def run_chunks(p_ref, chunk, chunks, col_ref, z_refs, emit):
    slabs = p_ref.shape[0] // SLAB
    tops = None
    for t in range(chunks + 1):
        q = chunk(t) if t < chunks else None
        later, totals, weights = None, None, []
        for s in range(slabs):
            if t < chunks:
                later = join(jnp.maximum, later, scores(p_ref, q, col_ref, z_refs[t % 2], s))
            if t > 0:
                weight, total = weigh(z_refs[(t - 1) % 2], tops, s)
                totals = join(jnp.add, totals, total)
                weights.append(weight)
        if t > 0:
            emit(t - 1, tops, settle(jnp.sum, totals), weights)
        if t < chunks:
            tops = settle(jnp.max, later)


def log_sums(p_ref, q_ref, col_ref, z_ref, row_ref, rows=2 * SLAB, ready=lambda s, t: None):
    slabs, chunks = p_ref.shape[0] // SLAB, q_ref.shape[0] // WIDTH
    totals = [None] * chunks
    for s in range(p_ref.shape[0] // rows):
        for t in range(chunks):
            ready(s, t)
            parts = exponents(p_ref, q_ref[pl.ds(t * WIDTH, WIDTH), :], col_ref, s, rows)
            totals[t] = join(jnp.add, totals[t], [fold(jnp.sum, jnp.exp2(part)) for part in parts])
    for t in range(chunks):
        for h, total in enumerate(settle(jnp.sum, totals[t])):
            row_ref[pl.ds(t * HALVES + h, 1), :] = total
    sums = row_ref[...]
    row_ref[...] = ENTROPY * jnp.log(sums)
    safe = jnp.logical_and(jnp.min(sums) >= LOWEST, jnp.max(sums) <= HIGHEST)

    @pl.when(jnp.logical_not(safe))
    def _():
        @pl.loop(0, chunks)
        def _(t):
            q = q_ref[pl.ds(pl.multiple_of(t * WIDTH, WIDTH), WIDTH), :]
            tops, sums = None, None
            for s in range(slabs):
                tops = join(jnp.maximum, tops, scores(p_ref, q, col_ref, z_ref, s))
            tops = settle(jnp.max, tops)
            for s in range(slabs):
                sums = join(jnp.add, sums, weigh(z_ref, tops, s)[1])
            for h, pair in enumerate(zip(tops, settle(jnp.sum, sums))):
                row_ref[pl.ds(t * HALVES + h, 1), :] = log_sum(*pair)


def first_kernel(
    p_hbm, q_hbm, p_mass_hbm, q_mass_hbm, out_ref, p_ref, q_ref, p_log_ref, q_log_ref,
    p_sems, q_sems, sems, col_ref, z_ref, row_ref,
):
    def load(hbm, ref, sem, k, rows):
        part = pl.ds(k * rows, rows)
        return pltpu.make_async_copy(hbm.at[part, :], ref.at[part, :], sem.at[k])

    p_loads = [load(p_hbm, p_ref, p_sems, s, PIECE) for s in range(p_ref.shape[0] // PIECE)]
    q_loads = [load(q_hbm, q_ref, q_sems, t, WIDTH) for t in range(q_ref.shape[0] // WIDTH)]
    masses = [
        pltpu.make_async_copy(p_mass_hbm, p_log_ref, sems.at[0]),
        pltpu.make_async_copy(q_mass_hbm, q_log_ref, sems.at[1]),
    ]
    for copy in p_loads[:1] + q_loads + p_loads[1:] + masses:
        copy.start()

    def ready(s, t):
        if t == 0:
            p_loads[s].wait()
            piece = pl.ds(s * PIECE, PIECE)
            p = p_ref[piece, :].astype(jnp.float32)
            norms = jnp.sum(p * p, axis=1, keepdims=True)
            col_ref[piece, :] = jnp.broadcast_to(-ONE_SCALE * norms, (PIECE, LANES))
        if s == 0:
            q_loads[t].wait()

    log_sums(p_ref, q_ref, col_ref, z_ref, row_ref, PIECE, ready)
    for copy in masses:
        copy.wait()
    p_log_ref[...] = ENTROPY * jnp.log(p_log_ref[...])
    q_log_ref[...] = ENTROPY * jnp.log(q_log_ref[...])
    out_ref[...] = jnp.broadcast_to(row_ref[...][None], out_ref.shape)


def next_kernel(parts_ref, log_ref, p_ref, q_ref, out_ref, col_ref, z_ref, row_ref):
    lanes_to_rows(ONE_SCALE * (log_ref[...] - merge(parts_ref[...])), col_ref)
    log_sums(p_ref, q_ref, col_ref, z_ref, row_ref)
    out_ref[...] = jnp.broadcast_to(row_ref[...][None], out_ref.shape)


def last_kernel(
    parts_ref, log_ref, p_ref, q_ref, feat_ref,
    sent_ref, keep_ref, own_ref, bias_ref, flip_ref, col_ref, even_ref, odd_ref,
):
    core = lax.rem(lax.axis_index("tgt"), 2)
    chips, _, share, depth = q_ref.shape
    half = chips * share
    width = feat_ref.shape[1]
    blocks = WIDTH // share
    bias = log_ref[...] - merge(parts_ref[...])
    bias_ref[...] = bias
    lanes_to_rows(ONE_SCALE * bias, col_ref)
    flip_ref[...] = feat_ref[...].astype(jnp.float32).T.astype(jnp.bfloat16)
    sent_ref[pl.ds(width, 8), :] = jnp.zeros((8, half), jnp.float32)
    own_ref[...] = jnp.zeros((8, half), jnp.float32)

    def chunk(t):
        own, first = divmod(t * WIDTH, half)
        q = q_ref[pl.ds(first // share, blocks), core if own else 1 - core]
        return q.reshape(WIDTH, depth)

    def emit(t, tops, totals, weights):
        own, first = divmod(t * WIDTH, half)
        slabs = [
            jnp.concatenate([weight.astype(jnp.bfloat16) for weight in slab], axis=1)
            for slab in weights
        ]
        lanes = pl.ds(first, WIDTH)
        lse = jnp.concatenate([log_sum(*pair) for pair in zip(tops, totals)], axis=1)
        scale = 1.0 / jnp.concatenate(totals, axis=1)
        sent_ref[pl.ds(width + own, 1), lanes] = lse
        own_ref[pl.ds(own, 1), lanes] = lse
        if own:
            for s, slab in enumerate(slabs):
                keep_ref[pl.ds(s * SLAB, SLAB), lanes] = slab
            own_ref[pl.ds(2, 1), lanes] = scale
        else:
            weight = jnp.concatenate(slabs, axis=0)
            numer = lax.dot_general(
                flip_ref[...], weight, NN, preferred_element_type=jnp.float32
            )
            sent_ref[pl.ds(0, width), lanes] = numer * scale

    run_chunks(p_ref, chunk, 2 * half // WIDTH, col_ref, (even_ref, odd_ref), emit)


def squares(ref, k):
    rows = ref[pl.ds(k * LANES, LANES), :].astype(jnp.float32)
    norms = jnp.sum(rows * rows, axis=1, keepdims=True)
    return jnp.broadcast_to(norms, (LANES, LANES)).T[:1, :]


def own_kernel(
    keep_ref, own_ref, flip_ref, bias_ref, p_ref, q_ref, log_ref, mean_ref, pot_ref, base_ref
):
    numer = lax.dot_general(
        flip_ref[...], keep_ref[...], NN, preferred_element_type=jnp.float32
    )
    mean_ref[...] = numer * own_ref[pl.ds(2, 1), :]
    for k in range(pot_ref.shape[0]):
        row = pl.ds(k, 1)
        pot_ref[row, :] = bias_ref[row, :] + squares(p_ref, k)
    for k in range(base_ref.shape[0]):
        row = pl.ds(k, 1)
        base_ref[row, :] = log_ref[row, :] + squares(q_ref, k)


def pair_kernel(mean_ref, own_ref, came_ref, out_ref, row_ref):
    width, half = mean_ref.shape
    chips = out_ref.shape[0]
    share = half // chips
    rows = half // LANES
    for side in range(2):
        mine = own_ref[pl.ds(1 - side, 1), :]
        other = came_ref[pl.ds(width + side, 1), :]
        top = jnp.maximum(mine, other)
        mine_share = jnp.exp2((mine - top) * ONE_SCALE)
        other_share = jnp.exp2((other - top) * ONE_SCALE)
        total = mine_share + other_share
        lse = top + ENTROPY * jnp.log(total)
        for k in range(rows):
            row_ref[pl.ds(side * rows + k, 1), :] = lse[:, k * LANES : (k + 1) * LANES]
        if side == 0:
            scale = 1.0 / total
            mine_share, other_share = mine_share * scale, other_share * scale
            step = LANES // share
            for k in range(rows):
                lanes = slice(k * LANES, (k + 1) * LANES)
                block = (
                    mean_ref[:, lanes] * mine_share[:, lanes]
                    + came_ref[pl.ds(0, width), lanes] * other_share[:, lanes]
                )
                out_ref[pl.ds(k * step, step), pl.ds(0, share), :] = block.T.reshape(
                    step, share, LANES
                )
    out_ref[:, pl.ds(share, 2 * rows), :] = jnp.broadcast_to(
        row_ref[...][None], (chips, 2 * rows, LANES)
    )


def final_kernel(landed_ref, base_ref, pot_ref, out_ref):
    index = lax.axis_index("tgt")
    core, chip = lax.rem(index, 2), lax.div(index, 2)
    share = out_ref.shape[0]
    chips = landed_ref.shape[0]
    mine = landed_ref[:, pl.ds(share + lax.div(chip, 2), 1), :].reshape(chips, LANES)
    mine = jnp.exp2((mine - jnp.max(mine, axis=0, keepdims=True)) * ONE_SCALE)
    mine = mine / jnp.sum(mine, axis=0, keepdims=True)
    mine = jnp.where(lax.rem(chip, 2) == 0, mine, pltpu.roll(mine, share, 1))
    mine = jnp.concatenate([mine, jnp.zeros((LANES - chips, LANES), jnp.float32)], axis=0).T
    total = jnp.zeros(out_ref.shape, jnp.float32)
    for b in range(chips):
        scale = jnp.broadcast_to(mine[:share, b : b + 1], out_ref.shape)
        total = total + landed_ref[b, pl.ds(0, share), :] * scale
    out_ref[...] = total
    whole = merge(landed_ref[:, pl.ds(share, landed_ref.shape[1] - share), :])
    rows = whole.shape[0] // 2
    even = jnp.where(core == 0, whole[:rows], whole[rows:])
    odd = jnp.where(core == 0, whole[rows:], whole[:rows])
    lane = lax.broadcasted_iota(jnp.int32, (rows, LANES), 1)
    first = jnp.where(lane < share, even, pltpu.roll(odd, share, 1))
    second = jnp.where(lane < share, pltpu.roll(even, share, 1), odd)
    for k in range(rows):
        for side, values in enumerate((first, second)):
            row = pl.ds(2 * k + side, 1)
            pot_ref[row, :] = base_ref[row, :] - values[k : k + 1]


def scratch(p, q):
    return [
        pltpu.VMEM((p.shape[0], LANES), jnp.float32),
        pltpu.VMEM((p.shape[0], WIDTH), jnp.float32),
        pltpu.VMEM((q.shape[0] // LANES, LANES), jnp.float32),
    ]


def call(kernel, args, outs, scratch_shapes, spaces=None):
    whole = pl.BlockSpec(memory_space=pltpu.VMEM)
    return pl.pallas_call(
        kernel,
        out_shape=outs,
        in_specs=spaces or [whole] * len(args),
        out_specs=jax.tree.map(lambda _: whole, outs),
        scratch_shapes=scratch_shapes,
        compiler_params=pltpu.CompilerParams(vmem_limit_bytes=VMEM_LIMIT),
    )(*args)


def local(source_embed, target_embed, target_feat, source_mass, target_mass):
    f32 = jnp.float32
    shape = jax.ShapeDtypeStruct
    n_src, n_tgt = lax.axis_size("src"), lax.axis_size("tgt")
    rows, depth = source_embed.shape
    width = target_feat.shape[1]
    share, half, chips = rows // n_tgt, rows // 2, n_tgt // 2
    src_mass = source_mass.reshape(-1, LANES)
    tgt_mass = target_mass.reshape(-1, LANES)
    src_rows, tgt_rows = src_mass.shape[0], tgt_mass.shape[0]
    to_src = shape((n_src, tgt_rows, LANES), f32)
    to_tgt = shape((n_tgt, src_rows, LANES), f32)
    by_src = scratch(source_embed, target_embed)
    by_tgt = scratch(target_embed, source_embed)
    same_core = [list(range(core, n_tgt, 2)) for core in range(2)]
    swap = [(index, index ^ 1) for index in range(n_tgt)]

    pieces = (rows // PIECE, target_embed.shape[0] // WIDTH, 2)
    sems = [pltpu.SemaphoreType.DMA((count,)) for count in pieces]
    inputs = [
        pltpu.with_memory_space_constraint(array, pltpu.HBM)
        for array in (source_embed, target_embed, src_mass, tgt_mass)
    ]
    held = [shape(array.shape, array.dtype) for array in inputs]
    sent, source_embed, target_embed, src_log, tgt_log = call(
        first_kernel,
        inputs,
        (to_src, *held),
        sems + by_src,
        [pl.BlockSpec(memory_space=pltpu.HBM)] * len(inputs),
    )
    parts = lax.all_to_all(sent, "src", 0, 0)
    sent = call(next_kernel, (parts, tgt_log, target_embed, source_embed), to_tgt, by_tgt)
    parts = lax.all_to_all(sent, "tgt", 0, 0)
    sent = call(next_kernel, (parts, src_log, source_embed, target_embed), to_src, by_src)
    parts = lax.all_to_all(sent, "src", 0, 0)
    sent, keep, own, bias, turned = call(
        last_kernel,
        (parts, tgt_log, target_embed, source_embed.reshape(chips, 2, share, depth), target_feat),
        (
            shape((width + 8, half), f32),
            shape((target_embed.shape[0], half), jnp.bfloat16),
            shape((8, half), f32),
            shape((tgt_rows, LANES), f32),
            shape(target_feat.shape[::-1], jnp.bfloat16),
        ),
        by_tgt[:2] + by_tgt[1:2],
    )
    came = lax.ppermute(sent, "tgt", swap)
    mean, target_pot, base = call(
        own_kernel,
        (keep, own, turned, bias, target_embed, source_embed, src_log),
        (shape((width, half), f32), shape(bias.shape, f32), shape(src_log.shape, f32)),
        [],
    )
    sent = call(
        pair_kernel,
        (mean, own, came),
        shape((chips, share + src_rows, LANES), f32),
        [pltpu.VMEM((src_rows, LANES), f32)],
    )
    landed = lax.all_to_all(sent, "tgt", 0, 0, axis_index_groups=same_core)
    source_pot, projected = call(
        final_kernel,
        (landed, base),
        (shape((src_rows, LANES), f32), shape((share, width), f32)),
        [],
    )
    return (source_pot.reshape(-1), target_pot.reshape(-1), projected)


def solution(mesh):
    placed = (P("src", None), P("tgt", None), P("tgt", None), P("src"), P("tgt"))
    return jax.shard_map(
        local,
        mesh=mesh,
        in_specs=placed,
        out_specs=(P("src"), P("tgt"), P(("src", "tgt"), None)),
        check_vma=False,
    )
```

```python
import math

import jax
import jax.numpy as jnp
from jax import lax
from jax.experimental import pallas as pl
from jax.experimental.pallas import tpu as pltpu
from jax.sharding import PartitionSpec as P

ENTROPY = 0.05
LANES = 128
WIDTH = 256
ONE_SCALE = 1.0 / ENTROPY * math.log2(math.e)
TWO_SCALE = 2.0 * ONE_SCALE
ONE_UNIT = ENTROPY * math.log(2.0)
LOWEST, HIGHEST = 2.0**-90, 2.0**110
NT = (((1,), (1,)), ((), ()))
NN = (((1,), (0,)), ((), ()))
HALVES = WIDTH // LANES
SLAB = 512
ACCUMULATE = 32
VMEM_LIMIT = 40 * 1024 * 1024


def merge(parts):
    top = jnp.max(parts, axis=0)
    total = jnp.sum(jnp.exp2((parts - top[None]) * ONE_SCALE), axis=0)
    return top + ENTROPY * jnp.log(total)


def lanes_to_rows(values, col_ref):
    for k in range(values.shape[0]):
        square = jnp.broadcast_to(values[k : k + 1, :], (LANES, LANES))
        col_ref[pl.ds(k * LANES, LANES), :] = square.T


def fold(reduce, part):
    return reduce(part.reshape(-1, ACCUMULATE, LANES), axis=0)


def exponents(p_ref, q, col_ref, s, rows=SLAB):
    slab = pl.ds(s * rows, rows)
    cross = lax.dot_general(p_ref[slab, :], q, NT, preferred_element_type=jnp.float32)
    col = col_ref[slab, :]
    return [cross[:, h * LANES : (h + 1) * LANES] * TWO_SCALE + col for h in range(HALVES)]


def scores(p_ref, q, col_ref, z_ref, s):
    slab = pl.ds(s * SLAB, SLAB)
    tops = []
    for h, part in enumerate(exponents(p_ref, q, col_ref, s)):
        z_ref[slab, pl.ds(h * LANES, LANES)] = part
        tops.append(fold(jnp.max, part))
    return tops


def weigh(z_ref, tops, s):
    slab = pl.ds(s * SLAB, SLAB)
    weights, totals = [], []
    for h, top in enumerate(tops):
        part = z_ref[slab, pl.ds(h * LANES, LANES)]
        weight = jnp.exp2(part - top)
        weights.append(weight)
        totals.append(fold(jnp.sum, weight))
    return weights, totals


def join(op, held, more):
    return more if held is None else [op(a, b) for a, b in zip(held, more)]


def settle(reduce, values):
    return [reduce(value, axis=0, keepdims=True) for value in values]


def log_sum(top, total):
    return ONE_UNIT * top + ENTROPY * jnp.log(total)


def run_chunks(p_ref, chunk, chunks, col_ref, z_refs, emit):
    slabs = p_ref.shape[0] // SLAB
    tops = None
    for t in range(chunks + 1):
        q = chunk(t) if t < chunks else None
        later, totals, weights = None, None, []
        for s in range(slabs):
            if t < chunks:
                later = join(jnp.maximum, later, scores(p_ref, q, col_ref, z_refs[t % 2], s))
            if t > 0:
                weight, total = weigh(z_refs[(t - 1) % 2], tops, s)
                totals = join(jnp.add, totals, total)
                weights.append(weight)
        if t > 0:
            emit(t - 1, tops, settle(jnp.sum, totals), weights)
        if t < chunks:
            tops = settle(jnp.max, later)


def log_sums(p_ref, q_ref, col_ref, z_ref, row_ref, rows=2 * SLAB):
    slabs, chunks = p_ref.shape[0] // SLAB, q_ref.shape[0] // WIDTH
    totals = [None] * chunks
    for s in range(p_ref.shape[0] // rows):
        for t in range(chunks):
            parts = exponents(p_ref, q_ref[pl.ds(t * WIDTH, WIDTH), :], col_ref, s, rows)
            totals[t] = join(jnp.add, totals[t], [fold(jnp.sum, jnp.exp2(part)) for part in parts])
    for t in range(chunks):
        for h, total in enumerate(settle(jnp.sum, totals[t])):
            row_ref[pl.ds(t * HALVES + h, 1), :] = total
    sums = row_ref[...]
    row_ref[...] = ENTROPY * jnp.log(sums)
    safe = jnp.logical_and(jnp.min(sums) >= LOWEST, jnp.max(sums) <= HIGHEST)

    @pl.when(jnp.logical_not(safe))
    def _():
        @pl.loop(0, chunks)
        def _(t):
            q = q_ref[pl.ds(pl.multiple_of(t * WIDTH, WIDTH), WIDTH), :]
            tops, sums = None, None
            for s in range(slabs):
                tops = join(jnp.maximum, tops, scores(p_ref, q, col_ref, z_ref, s))
            tops = settle(jnp.max, tops)
            for s in range(slabs):
                sums = join(jnp.add, sums, weigh(z_ref, tops, s)[1])
            for h, pair in enumerate(zip(tops, settle(jnp.sum, sums))):
                row_ref[pl.ds(t * HALVES + h, 1), :] = log_sum(*pair)


def first_kernel(
    p_hbm, q_hbm, p_mass_hbm, q_mass_hbm, out_ref, p_ref, q_ref, p_log_ref, q_log_ref,
    p_sems, sems, col_ref, z_ref, row_ref,
):
    loads = []
    for s in range(p_ref.shape[0] // SLAB):
        slab = pl.ds(s * SLAB, SLAB)
        loads.append(pltpu.make_async_copy(p_hbm.at[slab, :], p_ref.at[slab, :], p_sems.at[s]))
    load_q = pltpu.make_async_copy(q_hbm, q_ref, sems.at[0])
    masses = [
        pltpu.make_async_copy(p_mass_hbm, p_log_ref, sems.at[1]),
        pltpu.make_async_copy(q_mass_hbm, q_log_ref, sems.at[2]),
    ]
    for copy in loads + [load_q] + masses:
        copy.start()
    for s, copy in enumerate(loads):
        copy.wait()
        slab = pl.ds(s * SLAB, SLAB)
        p = p_ref[slab, :].astype(jnp.float32)
        norms = jnp.sum(p * p, axis=1, keepdims=True)
        col_ref[slab, :] = jnp.broadcast_to(-ONE_SCALE * norms, (SLAB, LANES))
    load_q.wait()
    log_sums(p_ref, q_ref, col_ref, z_ref, row_ref)
    for copy in masses:
        copy.wait()
    p_log_ref[...] = ENTROPY * jnp.log(p_log_ref[...])
    q_log_ref[...] = ENTROPY * jnp.log(q_log_ref[...])
    out_ref[...] = jnp.broadcast_to(row_ref[...][None], out_ref.shape)


def merge_kernel(parts_ref, out_ref):
    out_ref[...] = merge(parts_ref[...])


def next_kernel(parts_ref, log_ref, p_ref, q_ref, out_ref, col_ref, z_ref, row_ref):
    lanes_to_rows(ONE_SCALE * (log_ref[...] - merge(parts_ref[...])), col_ref)
    log_sums(p_ref, q_ref, col_ref, z_ref, row_ref)
    out_ref[...] = jnp.broadcast_to(row_ref[...][None], out_ref.shape)


def pair_next_kernel(
    mine_ref, came_ref, log_ref, p_ref, q_ref, out_ref, col_ref, z_ref, row_ref
):
    parts = jnp.stack([mine_ref[...], came_ref[...]])
    lanes_to_rows(ONE_SCALE * (log_ref[...] - merge(parts)), col_ref)
    log_sums(p_ref, q_ref, col_ref, z_ref, row_ref)
    out_ref[...] = jnp.broadcast_to(row_ref[...][None], out_ref.shape)


def last_kernel(
    parts_ref, log_ref, p_ref, q_ref, feat_ref,
    sent_ref, keep_ref, own_ref, bias_ref, flip_ref, col_ref, even_ref, odd_ref,
):
    core = lax.rem(lax.axis_index("tgt"), 2)
    chips, _, share, depth = q_ref.shape
    half = chips * share
    width = feat_ref.shape[1]
    blocks = WIDTH // share
    bias = log_ref[...] - merge(parts_ref[...])
    bias_ref[...] = bias
    lanes_to_rows(ONE_SCALE * bias, col_ref)
    flip_ref[...] = feat_ref[...].astype(jnp.float32).T.astype(jnp.bfloat16)
    sent_ref[pl.ds(width, 8), :] = jnp.zeros((8, half), jnp.float32)
    own_ref[...] = jnp.zeros((8, half), jnp.float32)

    def chunk(t):
        own, first = divmod(t * WIDTH, half)
        q = q_ref[pl.ds(first // share, blocks), core if own else 1 - core]
        return q.reshape(WIDTH, depth)

    def emit(t, tops, totals, weights):
        own, first = divmod(t * WIDTH, half)
        slabs = [
            jnp.concatenate([weight.astype(jnp.bfloat16) for weight in slab], axis=1)
            for slab in weights
        ]
        lanes = pl.ds(first, WIDTH)
        lse = jnp.concatenate([log_sum(*pair) for pair in zip(tops, totals)], axis=1)
        scale = 1.0 / jnp.concatenate(totals, axis=1)
        sent_ref[pl.ds(width + own, 1), lanes] = lse
        own_ref[pl.ds(own, 1), lanes] = lse
        if own:
            for s, slab in enumerate(slabs):
                keep_ref[pl.ds(s * SLAB, SLAB), lanes] = slab
            own_ref[pl.ds(2, 1), lanes] = scale
        else:
            weight = jnp.concatenate(slabs, axis=0)
            numer = lax.dot_general(
                flip_ref[...], weight, NN, preferred_element_type=jnp.float32
            )
            sent_ref[pl.ds(0, width), lanes] = numer * scale

    run_chunks(p_ref, chunk, 2 * half // WIDTH, col_ref, (even_ref, odd_ref), emit)


def squares(ref, k):
    rows = ref[pl.ds(k * LANES, LANES), :].astype(jnp.float32)
    norms = jnp.sum(rows * rows, axis=1, keepdims=True)
    return jnp.broadcast_to(norms, (LANES, LANES)).T[:1, :]


def own_kernel(
    keep_ref, own_ref, flip_ref, bias_ref, p_ref, q_ref, log_ref, mean_ref, pot_ref, base_ref
):
    numer = lax.dot_general(
        flip_ref[...], keep_ref[...], NN, preferred_element_type=jnp.float32
    )
    mean_ref[...] = numer * own_ref[pl.ds(2, 1), :]
    for k in range(pot_ref.shape[0]):
        row = pl.ds(k, 1)
        pot_ref[row, :] = bias_ref[row, :] + squares(p_ref, k)
    for k in range(base_ref.shape[0]):
        row = pl.ds(k, 1)
        base_ref[row, :] = log_ref[row, :] + squares(q_ref, k)


def pair_kernel(mean_ref, own_ref, came_ref, out_ref, row_ref):
    width, half = mean_ref.shape
    chips = out_ref.shape[0]
    share = half // chips
    rows = half // LANES
    for side in range(2):
        mine = own_ref[pl.ds(1 - side, 1), :]
        other = came_ref[pl.ds(width + side, 1), :]
        top = jnp.maximum(mine, other)
        mine_share = jnp.exp2((mine - top) * ONE_SCALE)
        other_share = jnp.exp2((other - top) * ONE_SCALE)
        total = mine_share + other_share
        lse = top + ENTROPY * jnp.log(total)
        for k in range(rows):
            row_ref[pl.ds(side * rows + k, 1), :] = lse[:, k * LANES : (k + 1) * LANES]
        if side == 0:
            scale = 1.0 / total
            mine_share, other_share = mine_share * scale, other_share * scale
            step = LANES // share
            for k in range(rows):
                lanes = slice(k * LANES, (k + 1) * LANES)
                block = (
                    mean_ref[:, lanes] * mine_share[:, lanes]
                    + came_ref[pl.ds(0, width), lanes] * other_share[:, lanes]
                )
                out_ref[pl.ds(k * step, step), pl.ds(0, share), :] = block.T.reshape(
                    step, share, LANES
                )
    out_ref[:, pl.ds(share, 2 * rows), :] = jnp.broadcast_to(
        row_ref[...][None], (chips, 2 * rows, LANES)
    )


def final_kernel(landed_ref, base_ref, pot_ref, out_ref):
    index = lax.axis_index("tgt")
    core, chip = lax.rem(index, 2), lax.div(index, 2)
    share = out_ref.shape[0]
    chips = landed_ref.shape[0]
    mine = landed_ref[:, pl.ds(share + lax.div(chip, 2), 1), :].reshape(chips, LANES)
    mine = jnp.exp2((mine - jnp.max(mine, axis=0, keepdims=True)) * ONE_SCALE)
    mine = mine / jnp.sum(mine, axis=0, keepdims=True)
    mine = jnp.where(lax.rem(chip, 2) == 0, mine, pltpu.roll(mine, share, 1))
    mine = jnp.concatenate([mine, jnp.zeros((LANES - chips, LANES), jnp.float32)], axis=0).T
    total = jnp.zeros(out_ref.shape, jnp.float32)
    for b in range(chips):
        scale = jnp.broadcast_to(mine[:share, b : b + 1], out_ref.shape)
        total = total + landed_ref[b, pl.ds(0, share), :] * scale
    out_ref[...] = total
    whole = merge(landed_ref[:, pl.ds(share, landed_ref.shape[1] - share), :])
    rows = whole.shape[0] // 2
    even = jnp.where(core == 0, whole[:rows], whole[rows:])
    odd = jnp.where(core == 0, whole[rows:], whole[:rows])
    lane = lax.broadcasted_iota(jnp.int32, (rows, LANES), 1)
    first = jnp.where(lane < share, even, pltpu.roll(odd, share, 1))
    second = jnp.where(lane < share, pltpu.roll(even, share, 1), odd)
    for k in range(rows):
        for side, values in enumerate((first, second)):
            row = pl.ds(2 * k + side, 1)
            pot_ref[row, :] = base_ref[row, :] - values[k : k + 1]


def scratch(p, q):
    return [
        pltpu.VMEM((p.shape[0], LANES), jnp.float32),
        pltpu.VMEM((p.shape[0], WIDTH), jnp.float32),
        pltpu.VMEM((q.shape[0] // LANES, LANES), jnp.float32),
    ]


def call(kernel, args, outs, scratch_shapes, spaces=None):
    whole = pl.BlockSpec(memory_space=pltpu.VMEM)
    return pl.pallas_call(
        kernel,
        out_shape=outs,
        in_specs=spaces or [whole] * len(args),
        out_specs=jax.tree.map(lambda _: whole, outs),
        scratch_shapes=scratch_shapes,
        compiler_params=pltpu.CompilerParams(vmem_limit_bytes=VMEM_LIMIT),
    )(*args)


def local(source_embed, target_embed, target_feat, source_mass, target_mass):
    f32 = jnp.float32
    shape = jax.ShapeDtypeStruct
    n_src, n_tgt = lax.axis_size("src"), lax.axis_size("tgt")
    rows, depth = source_embed.shape
    width = target_feat.shape[1]
    share, half, chips = rows // n_tgt, rows // 2, n_tgt // 2
    src_mass = source_mass.reshape(-1, LANES)
    tgt_mass = target_mass.reshape(-1, LANES)
    src_rows, tgt_rows = src_mass.shape[0], tgt_mass.shape[0]
    to_src = shape((n_src, tgt_rows, LANES), f32)
    to_tgt = shape((chips, src_rows, LANES), f32)
    by_src = scratch(source_embed, target_embed)
    by_tgt = scratch(target_embed, source_embed)
    same_core = [list(range(core, n_tgt, 2)) for core in range(2)]
    swap = [(index, index ^ 1) for index in range(n_tgt)]

    sems = [pltpu.SemaphoreType.DMA((rows // SLAB,)), pltpu.SemaphoreType.DMA((3,))]
    inputs = [
        pltpu.with_memory_space_constraint(array, pltpu.HBM)
        for array in (source_embed, target_embed, src_mass, tgt_mass)
    ]
    held = [shape(array.shape, array.dtype) for array in inputs]
    sent, source_embed, target_embed, src_log, tgt_log = call(
        first_kernel,
        inputs,
        (to_src, *held),
        sems + by_src,
        [pl.BlockSpec(memory_space=pltpu.HBM)] * len(inputs),
    )
    parts = lax.all_to_all(sent, "src", 0, 0)
    sent = call(next_kernel, (parts, tgt_log, target_embed, source_embed), to_tgt, by_tgt)
    parts = lax.all_to_all(sent, "tgt", 0, 0, axis_index_groups=same_core)
    mine = call(merge_kernel, (parts,), shape((src_rows, LANES), f32), [])
    came = lax.ppermute(mine, "tgt", swap)
    sent = call(
        pair_next_kernel, (mine, came, src_log, source_embed, target_embed), to_src, by_src
    )
    parts = lax.all_to_all(sent, "src", 0, 0)
    sent, keep, own, bias, turned = call(
        last_kernel,
        (parts, tgt_log, target_embed, source_embed.reshape(chips, 2, share, depth), target_feat),
        (
            shape((width + 8, half), f32),
            shape((target_embed.shape[0], half), jnp.bfloat16),
            shape((8, half), f32),
            shape((tgt_rows, LANES), f32),
            shape(target_feat.shape[::-1], jnp.bfloat16),
        ),
        by_tgt[:2] + by_tgt[1:2],
    )
    came = lax.ppermute(sent, "tgt", swap)
    mean, target_pot, base = call(
        own_kernel,
        (keep, own, turned, bias, target_embed, source_embed, src_log),
        (shape((width, half), f32), shape(bias.shape, f32), shape(src_log.shape, f32)),
        [],
    )
    sent = call(
        pair_kernel,
        (mean, own, came),
        shape((chips, share + src_rows, LANES), f32),
        [pltpu.VMEM((src_rows, LANES), f32)],
    )
    landed = lax.all_to_all(sent, "tgt", 0, 0, axis_index_groups=same_core)
    source_pot, projected = call(
        final_kernel,
        (landed, base),
        (shape((src_rows, LANES), f32), shape((share, width), f32)),
        [],
    )
    return (source_pot.reshape(-1), target_pot.reshape(-1), projected)


def solution(mesh):
    placed = (P("src", None), P("tgt", None), P("tgt", None), P("src"), P("tgt"))
    return jax.shard_map(
        local,
        mesh=mesh,
        in_specs=placed,
        out_specs=(P("src"), P("tgt"), P(("src", "tgt"), None)),
        check_vma=False,
    )
```

```python
import functools
import math

import jax
import jax.numpy as jnp
from jax import lax
from jax.experimental import pallas as pl
from jax.experimental.pallas import tpu as pltpu
from jax.sharding import PartitionSpec as P

ENTROPY = 0.05
LANES = 128
WIDTH = 256
ONE_SCALE = 1.0 / ENTROPY * math.log2(math.e)
TWO_SCALE = 2.0 * ONE_SCALE
ONE_UNIT = ENTROPY * math.log(2.0)
LOWEST, HIGHEST = 2.0**-90, 2.0**110
NT = (((1,), (1,)), ((), ()))
NN = (((1,), (0,)), ((), ()))
HALVES = WIDTH // LANES
SLAB = 512
ACCUMULATE = 32
VMEM_LIMIT = 40 * 1024 * 1024


def merge(parts):
    top = jnp.max(parts, axis=0)
    total = jnp.sum(jnp.exp2((parts - top[None]) * ONE_SCALE), axis=0)
    return top + ENTROPY * jnp.log(total)


def lanes_to_rows(values, col_ref):
    for k in range(values.shape[0]):
        square = jnp.broadcast_to(values[k : k + 1, :], (LANES, LANES))
        col_ref[pl.ds(k * LANES, LANES), :] = square.T


def fold(reduce, part):
    return reduce(part.reshape(-1, ACCUMULATE, LANES), axis=0)


def exponents(p_ref, q, col_ref, s, rows=SLAB):
    slab = pl.ds(s * rows, rows)
    cross = lax.dot_general(p_ref[slab, :], q, NT, preferred_element_type=jnp.float32)
    col = col_ref[slab, :]
    return [cross[:, h * LANES : (h + 1) * LANES] * TWO_SCALE + col for h in range(HALVES)]


def scores(p_ref, q, col_ref, z_ref, s):
    slab = pl.ds(s * SLAB, SLAB)
    tops = []
    for h, part in enumerate(exponents(p_ref, q, col_ref, s)):
        z_ref[slab, pl.ds(h * LANES, LANES)] = part
        tops.append(fold(jnp.max, part))
    return tops


def weigh(z_ref, tops, s):
    slab = pl.ds(s * SLAB, SLAB)
    weights, totals = [], []
    for h, top in enumerate(tops):
        part = z_ref[slab, pl.ds(h * LANES, LANES)]
        weight = jnp.exp2(part - top)
        weights.append(weight)
        totals.append(fold(jnp.sum, weight))
    return weights, totals


def join(op, held, more):
    return more if held is None else [op(a, b) for a, b in zip(held, more)]


def settle(reduce, values):
    return [reduce(value, axis=0, keepdims=True) for value in values]


def log_sum(top, total):
    return ONE_UNIT * top + ENTROPY * jnp.log(total)


def run_chunks(p_ref, chunk, chunks, col_ref, z_refs, emit):
    slabs = p_ref.shape[0] // SLAB
    tops = None
    for t in range(chunks + 1):
        q = chunk(t) if t < chunks else None
        later, totals, weights = None, None, []
        for s in range(slabs):
            if t < chunks:
                later = join(jnp.maximum, later, scores(p_ref, q, col_ref, z_refs[t % 2], s))
            if t > 0:
                weight, total = weigh(z_refs[(t - 1) % 2], tops, s)
                totals = join(jnp.add, totals, total)
                weights.append(weight)
        if t > 0:
            emit(t - 1, tops, settle(jnp.sum, totals), weights)
        if t < chunks:
            tops = settle(jnp.max, later)


def log_sums(p_ref, q_ref, col_ref, z_ref, row_ref, rows=2 * SLAB):
    slabs, chunks = p_ref.shape[0] // SLAB, q_ref.shape[0] // WIDTH
    totals = [None] * chunks
    for s in range(p_ref.shape[0] // rows):
        for t in range(chunks):
            parts = exponents(p_ref, q_ref[pl.ds(t * WIDTH, WIDTH), :], col_ref, s, rows)
            totals[t] = join(jnp.add, totals[t], [fold(jnp.sum, jnp.exp2(part)) for part in parts])
    for t in range(chunks):
        for h, total in enumerate(settle(jnp.sum, totals[t])):
            row_ref[pl.ds(t * HALVES + h, 1), :] = total
    sums = row_ref[...]
    row_ref[...] = ENTROPY * jnp.log(sums)
    safe = jnp.logical_and(jnp.min(sums) >= LOWEST, jnp.max(sums) <= HIGHEST)

    @pl.when(jnp.logical_not(safe))
    def _():
        @pl.loop(0, chunks)
        def _(t):
            q = q_ref[pl.ds(pl.multiple_of(t * WIDTH, WIDTH), WIDTH), :]
            tops, sums = None, None
            for s in range(slabs):
                tops = join(jnp.maximum, tops, scores(p_ref, q, col_ref, z_ref, s))
            tops = settle(jnp.max, tops)
            for s in range(slabs):
                sums = join(jnp.add, sums, weigh(z_ref, tops, s)[1])
            for h, pair in enumerate(zip(tops, settle(jnp.sum, sums))):
                row_ref[pl.ds(t * HALVES + h, 1), :] = log_sum(*pair)


def first_kernel(
    p_hbm, q_hbm, p_mass_hbm, q_mass_hbm, out_ref, p_ref, q_ref, p_log_ref, q_log_ref,
    p_sems, sems, col_ref, z_ref, row_ref,
):
    loads = []
    for s in range(p_ref.shape[0] // SLAB):
        slab = pl.ds(s * SLAB, SLAB)
        loads.append(pltpu.make_async_copy(p_hbm.at[slab, :], p_ref.at[slab, :], p_sems.at[s]))
    load_q = pltpu.make_async_copy(q_hbm, q_ref, sems.at[0])
    masses = [
        pltpu.make_async_copy(p_mass_hbm, p_log_ref, sems.at[1]),
        pltpu.make_async_copy(q_mass_hbm, q_log_ref, sems.at[2]),
    ]
    for copy in loads + [load_q] + masses:
        copy.start()
    for s, copy in enumerate(loads):
        copy.wait()
        slab = pl.ds(s * SLAB, SLAB)
        p = p_ref[slab, :].astype(jnp.float32)
        norms = jnp.sum(p * p, axis=1, keepdims=True)
        col_ref[slab, :] = jnp.broadcast_to(-ONE_SCALE * norms, (SLAB, LANES))
    load_q.wait()
    log_sums(p_ref, q_ref, col_ref, z_ref, row_ref)
    for copy in masses:
        copy.wait()
    p_log_ref[...] = ENTROPY * jnp.log(p_log_ref[...])
    q_log_ref[...] = ENTROPY * jnp.log(q_log_ref[...])
    out_ref[...] = jnp.broadcast_to(row_ref[...][None], out_ref.shape)


def next_kernel(parts_ref, log_ref, p_ref, q_ref, out_ref, col_ref, z_ref, row_ref):
    lanes_to_rows(ONE_SCALE * (log_ref[...] - merge(parts_ref[...])), col_ref)
    log_sums(p_ref, q_ref, col_ref, z_ref, row_ref)
    out_ref[...] = jnp.broadcast_to(row_ref[...][None], out_ref.shape)


def last_kernel(
    parts_ref, log_ref, p_ref, q_ref, feat_ref,
    sent_ref, keep_ref, own_ref, bias_ref, flip_ref, col_ref, even_ref, odd_ref,
):
    core = lax.rem(lax.axis_index("tgt"), 2)
    chips, _, share, depth = q_ref.shape
    half = chips * share
    width = feat_ref.shape[1]
    blocks = WIDTH // share
    bias = log_ref[...] - merge(parts_ref[...])
    bias_ref[...] = bias
    lanes_to_rows(ONE_SCALE * bias, col_ref)
    flip_ref[...] = feat_ref[...].astype(jnp.float32).T.astype(jnp.bfloat16)
    sent_ref[pl.ds(width, 8), :] = jnp.zeros((8, half), jnp.float32)
    own_ref[...] = jnp.zeros((8, half), jnp.float32)

    def chunk(t):
        own, first = divmod(t * WIDTH, half)
        q = q_ref[pl.ds(first // share, blocks), core if own else 1 - core]
        return q.reshape(WIDTH, depth)

    def emit(t, tops, totals, weights):
        own, first = divmod(t * WIDTH, half)
        slabs = [
            jnp.concatenate([weight.astype(jnp.bfloat16) for weight in slab], axis=1)
            for slab in weights
        ]
        lanes = pl.ds(first, WIDTH)
        lse = jnp.concatenate([log_sum(*pair) for pair in zip(tops, totals)], axis=1)
        scale = 1.0 / jnp.concatenate(totals, axis=1)
        sent_ref[pl.ds(width + own, 1), lanes] = lse
        own_ref[pl.ds(own, 1), lanes] = lse
        if own:
            for s, slab in enumerate(slabs):
                keep_ref[pl.ds(s * SLAB, SLAB), lanes] = slab
            own_ref[pl.ds(2, 1), lanes] = scale
        else:
            weight = jnp.concatenate(slabs, axis=0)
            numer = lax.dot_general(
                flip_ref[...], weight, NN, preferred_element_type=jnp.float32
            )
            sent_ref[pl.ds(0, width), lanes] = numer * scale

    run_chunks(p_ref, chunk, 2 * half // WIDTH, col_ref, (even_ref, odd_ref), emit)


def squares(ref, k):
    rows = ref[pl.ds(k * LANES, LANES), :].astype(jnp.float32)
    norms = jnp.sum(rows * rows, axis=1, keepdims=True)
    return jnp.broadcast_to(norms, (LANES, LANES)).T[:1, :]


def own_kernel(
    keep_ref, own_ref, flip_ref, bias_ref, p_ref, q_ref, log_ref, mean_ref, pot_ref, base_ref
):
    numer = lax.dot_general(
        flip_ref[...], keep_ref[...], NN, preferred_element_type=jnp.float32
    )
    mean_ref[...] = numer * own_ref[pl.ds(2, 1), :]
    for k in range(pot_ref.shape[0]):
        row = pl.ds(k, 1)
        pot_ref[row, :] = bias_ref[row, :] + squares(p_ref, k)
    for k in range(base_ref.shape[0]):
        row = pl.ds(k, 1)
        base_ref[row, :] = log_ref[row, :] + squares(q_ref, k)


def pair_kernel(far_chip, mean_ref, own_ref, came_ref, out_ref, row_ref):
    width, half = mean_ref.shape
    chips = out_ref.shape[0]
    share = half // chips
    rows = half // LANES
    for side in range(2):
        mine = own_ref[pl.ds(1 - side, 1), :]
        other = came_ref[pl.ds(width + side, 1), :]
        top = jnp.maximum(mine, other)
        mine_share = jnp.exp2((mine - top) * ONE_SCALE)
        other_share = jnp.exp2((other - top) * ONE_SCALE)
        total = mine_share + other_share
        lse = top + ENTROPY * jnp.log(total)
        for k in range(rows):
            row_ref[pl.ds(side * rows + k, 1), :] = lse[:, k * LANES : (k + 1) * LANES]
        if side == 0:
            scale = 1.0 / total
            mine_share, other_share = mine_share * scale, other_share * scale
            step = LANES // share
            for k in range(rows):
                lanes = slice(k * LANES, (k + 1) * LANES)
                block = (
                    mean_ref[:, lanes] * mine_share[:, lanes]
                    + came_ref[pl.ds(0, width), lanes] * other_share[:, lanes]
                )
                place = (k * step - far_chip) % chips
                out_ref[pl.ds(place, step), pl.ds(0, share), :] = block.T.reshape(
                    step, share, LANES
                )
    out_ref[:, pl.ds(share, 2 * rows), :] = jnp.broadcast_to(
        row_ref[...][None], (chips, 2 * rows, LANES)
    )


def final_kernel(landed_ref, base_ref, pot_ref, out_ref):
    index = lax.axis_index("tgt")
    core, chip = lax.rem(index, 2), lax.div(index, 2)
    share = out_ref.shape[0]
    chips = landed_ref.shape[0]
    mine = landed_ref[:, pl.ds(share + lax.div(chip, 2), 1), :].reshape(chips, LANES)
    mine = jnp.exp2((mine - jnp.max(mine, axis=0, keepdims=True)) * ONE_SCALE)
    mine = mine / jnp.sum(mine, axis=0, keepdims=True)
    mine = jnp.where(lax.rem(chip, 2) == 0, mine, pltpu.roll(mine, share, 1))
    mine = jnp.concatenate([mine, jnp.zeros((LANES - chips, LANES), jnp.float32)], axis=0).T
    total = jnp.zeros(out_ref.shape, jnp.float32)
    for b in range(chips):
        scale = jnp.broadcast_to(mine[:share, b : b + 1], out_ref.shape)
        total = total + landed_ref[b, pl.ds(0, share), :] * scale
    out_ref[...] = total
    whole = merge(landed_ref[:, pl.ds(share, landed_ref.shape[1] - share), :])
    rows = whole.shape[0] // 2
    even = jnp.where(core == 0, whole[:rows], whole[rows:])
    odd = jnp.where(core == 0, whole[rows:], whole[:rows])
    lane = lax.broadcasted_iota(jnp.int32, (rows, LANES), 1)
    first = jnp.where(lane < share, even, pltpu.roll(odd, share, 1))
    second = jnp.where(lane < share, pltpu.roll(even, share, 1), odd)
    for k in range(rows):
        for side, values in enumerate((first, second)):
            row = pl.ds(2 * k + side, 1)
            pot_ref[row, :] = base_ref[row, :] - values[k : k + 1]


def rotated(n, first):
    return [(first + place) % n for place in range(n)]


def scratch(p, q):
    return [
        pltpu.VMEM((p.shape[0], LANES), jnp.float32),
        pltpu.VMEM((p.shape[0], WIDTH), jnp.float32),
        pltpu.VMEM((q.shape[0] // LANES, LANES), jnp.float32),
    ]


def call(kernel, args, outs, scratch_shapes, spaces=None):
    whole = pl.BlockSpec(memory_space=pltpu.VMEM)
    return pl.pallas_call(
        kernel,
        out_shape=outs,
        in_specs=spaces or [whole] * len(args),
        out_specs=jax.tree.map(lambda _: whole, outs),
        scratch_shapes=scratch_shapes,
        compiler_params=pltpu.CompilerParams(vmem_limit_bytes=VMEM_LIMIT),
    )(*args)


def local(source_embed, target_embed, target_feat, source_mass, target_mass):
    f32 = jnp.float32
    shape = jax.ShapeDtypeStruct
    n_src, n_tgt = lax.axis_size("src"), lax.axis_size("tgt")
    rows, depth = source_embed.shape
    width = target_feat.shape[1]
    share, half, chips = rows // n_tgt, rows // 2, n_tgt // 2
    src_mass = source_mass.reshape(-1, LANES)
    tgt_mass = target_mass.reshape(-1, LANES)
    src_rows, tgt_rows = src_mass.shape[0], tgt_mass.shape[0]
    to_src = shape((n_src, tgt_rows, LANES), f32)
    to_tgt = shape((n_tgt, src_rows, LANES), f32)
    by_src = scratch(source_embed, target_embed)
    by_tgt = scratch(target_embed, source_embed)
    far_chip = chips // 2 + math.isqrt(chips) // 2
    same_core = [[2 * chip + core for chip in rotated(chips, far_chip)] for core in range(2)]
    swap = [(index, index ^ 1) for index in range(n_tgt)]

    sems = [pltpu.SemaphoreType.DMA((rows // SLAB,)), pltpu.SemaphoreType.DMA((3,))]
    inputs = [
        pltpu.with_memory_space_constraint(array, pltpu.HBM)
        for array in (source_embed, target_embed, src_mass, tgt_mass)
    ]
    held = [shape(array.shape, array.dtype) for array in inputs]
    sent, source_embed, target_embed, src_log, tgt_log = call(
        first_kernel,
        inputs,
        (to_src, *held),
        sems + by_src,
        [pl.BlockSpec(memory_space=pltpu.HBM)] * len(inputs),
    )
    parts = lax.all_to_all(sent, "src", 0, 0, axis_index_groups=[rotated(n_src, n_src // 2)])
    sent = call(next_kernel, (parts, tgt_log, target_embed, source_embed), to_tgt, by_tgt)
    parts = lax.all_to_all(sent, "tgt", 0, 0, axis_index_groups=[rotated(n_tgt, 2 * far_chip)])
    sent = call(next_kernel, (parts, src_log, source_embed, target_embed), to_src, by_src)
    parts = lax.all_to_all(sent, "src", 0, 0, axis_index_groups=[rotated(n_src, n_src // 2)])
    sent, keep, own, bias, turned = call(
        last_kernel,
        (parts, tgt_log, target_embed, source_embed.reshape(chips, 2, share, depth), target_feat),
        (
            shape((width + 8, half), f32),
            shape((target_embed.shape[0], half), jnp.bfloat16),
            shape((8, half), f32),
            shape((tgt_rows, LANES), f32),
            shape(target_feat.shape[::-1], jnp.bfloat16),
        ),
        by_tgt[:2] + by_tgt[1:2],
    )
    came = lax.ppermute(sent, "tgt", swap)
    mean, target_pot, base = call(
        own_kernel,
        (keep, own, turned, bias, target_embed, source_embed, src_log),
        (shape((width, half), f32), shape(bias.shape, f32), shape(src_log.shape, f32)),
        [],
    )
    sent = call(
        functools.partial(pair_kernel, far_chip),
        (mean, own, came),
        shape((chips, share + src_rows, LANES), f32),
        [pltpu.VMEM((src_rows, LANES), f32)],
    )
    landed = lax.all_to_all(sent, "tgt", 0, 0, axis_index_groups=same_core)
    source_pot, projected = call(
        final_kernel,
        (landed, base),
        (shape((src_rows, LANES), f32), shape((share, width), f32)),
        [],
    )
    return (source_pot.reshape(-1), target_pot.reshape(-1), projected)


def solution(mesh):
    placed = (P("src", None), P("tgt", None), P("tgt", None), P("src"), P("tgt"))
    return jax.shard_map(
        local,
        mesh=mesh,
        in_specs=placed,
        out_specs=(P("src"), P("tgt"), P(("src", "tgt"), None)),
        check_vma=False,
    )
```

```python
import functools
import math

import jax
import jax.numpy as jnp
from jax import lax
from jax.experimental import pallas as pl
from jax.experimental.pallas import tpu as pltpu
from jax.sharding import PartitionSpec as P

ENTROPY = 0.05
LANES = 128
WIDTH = 256
ONE_SCALE = 1.0 / ENTROPY * math.log2(math.e)
TWO_SCALE = 2.0 * ONE_SCALE
ONE_UNIT = ENTROPY * math.log(2.0)
LOWEST, HIGHEST = 2.0**-90, 2.0**110
NT = (((1,), (1,)), ((), ()))
NN = (((1,), (0,)), ((), ()))
HALVES = WIDTH // LANES
SLAB = 512
ACCUMULATE = 32
VMEM_LIMIT = 40 * 1024 * 1024


def merge(parts):
    top = jnp.max(parts, axis=0)
    total = jnp.sum(jnp.exp2((parts - top[None]) * ONE_SCALE), axis=0)
    return top + ENTROPY * jnp.log(total)


def lanes_to_rows(values, col_ref):
    for k in range(values.shape[0]):
        square = jnp.broadcast_to(values[k : k + 1, :], (LANES, LANES))
        col_ref[pl.ds(k * LANES, LANES), :] = square.T


def fold(reduce, part):
    return reduce(part.reshape(-1, ACCUMULATE, LANES), axis=0)


def exponents(p_ref, q, col_ref, s, rows=SLAB):
    slab = pl.ds(s * rows, rows)
    cross = lax.dot_general(p_ref[slab, :], q, NT, preferred_element_type=jnp.float32)
    col = col_ref[slab, :]
    return [cross[:, h * LANES : (h + 1) * LANES] * TWO_SCALE + col for h in range(HALVES)]


def scores(p_ref, q, col_ref, z_ref, s):
    slab = pl.ds(s * SLAB, SLAB)
    tops = []
    for h, part in enumerate(exponents(p_ref, q, col_ref, s)):
        z_ref[slab, pl.ds(h * LANES, LANES)] = part
        tops.append(fold(jnp.max, part))
    return tops


def weigh(z_ref, tops, s):
    slab = pl.ds(s * SLAB, SLAB)
    weights, totals = [], []
    for h, top in enumerate(tops):
        part = z_ref[slab, pl.ds(h * LANES, LANES)]
        weight = jnp.exp2(part - top)
        weights.append(weight)
        totals.append(fold(jnp.sum, weight))
    return weights, totals


def join(op, held, more):
    return more if held is None else [op(a, b) for a, b in zip(held, more)]


def settle(reduce, values):
    return [reduce(value, axis=0, keepdims=True) for value in values]


def log_sum(top, total):
    return ONE_UNIT * top + ENTROPY * jnp.log(total)


def run_chunks(p_ref, chunk, chunks, col_ref, z_refs, emit):
    slabs = p_ref.shape[0] // SLAB
    tops = None
    for t in range(chunks + 1):
        q = chunk(t) if t < chunks else None
        later, totals, weights = None, None, []
        for s in range(slabs):
            if t < chunks:
                later = join(jnp.maximum, later, scores(p_ref, q, col_ref, z_refs[t % 2], s))
            if t > 0:
                weight, total = weigh(z_refs[(t - 1) % 2], tops, s)
                totals = join(jnp.add, totals, total)
                weights.append(weight)
        if t > 0:
            emit(t - 1, tops, settle(jnp.sum, totals), weights)
        if t < chunks:
            tops = settle(jnp.max, later)


def log_sums(p_ref, q_ref, col_ref, z_ref, row_ref, rows=2 * SLAB):
    slabs, chunks = p_ref.shape[0] // SLAB, q_ref.shape[0] // WIDTH
    totals = [None] * chunks
    for s in range(p_ref.shape[0] // rows):
        for t in range(chunks):
            parts = exponents(p_ref, q_ref[pl.ds(t * WIDTH, WIDTH), :], col_ref, s, rows)
            totals[t] = join(jnp.add, totals[t], [fold(jnp.sum, jnp.exp2(part)) for part in parts])
    for t in range(chunks):
        for h, total in enumerate(settle(jnp.sum, totals[t])):
            row_ref[pl.ds(t * HALVES + h, 1), :] = total
    sums = row_ref[...]
    row_ref[...] = ENTROPY * jnp.log(sums)
    safe = jnp.logical_and(jnp.min(sums) >= LOWEST, jnp.max(sums) <= HIGHEST)

    @pl.when(jnp.logical_not(safe))
    def _():
        @pl.loop(0, chunks)
        def _(t):
            q = q_ref[pl.ds(pl.multiple_of(t * WIDTH, WIDTH), WIDTH), :]
            tops, sums = None, None
            for s in range(slabs):
                tops = join(jnp.maximum, tops, scores(p_ref, q, col_ref, z_ref, s))
            tops = settle(jnp.max, tops)
            for s in range(slabs):
                sums = join(jnp.add, sums, weigh(z_ref, tops, s)[1])
            for h, pair in enumerate(zip(tops, settle(jnp.sum, sums))):
                row_ref[pl.ds(t * HALVES + h, 1), :] = log_sum(*pair)


def first_kernel(
    p_hbm, q_hbm, p_mass_hbm, q_mass_hbm, out_ref, p_ref, q_ref, p_log_ref, q_log_ref,
    p_sems, sems, col_ref, z_ref, row_ref,
):
    loads = []
    for s in range(p_ref.shape[0] // SLAB):
        slab = pl.ds(s * SLAB, SLAB)
        loads.append(pltpu.make_async_copy(p_hbm.at[slab, :], p_ref.at[slab, :], p_sems.at[s]))
    load_q = pltpu.make_async_copy(q_hbm, q_ref, sems.at[0])
    masses = [
        pltpu.make_async_copy(p_mass_hbm, p_log_ref, sems.at[1]),
        pltpu.make_async_copy(q_mass_hbm, q_log_ref, sems.at[2]),
    ]
    for copy in loads + [load_q] + masses:
        copy.start()
    for s, copy in enumerate(loads):
        copy.wait()
        slab = pl.ds(s * SLAB, SLAB)
        p = p_ref[slab, :].astype(jnp.float32)
        norms = jnp.sum(p * p, axis=1, keepdims=True)
        col_ref[slab, :] = jnp.broadcast_to(-ONE_SCALE * norms, (SLAB, LANES))
    load_q.wait()
    log_sums(p_ref, q_ref, col_ref, z_ref, row_ref)
    for copy in masses:
        copy.wait()
    p_log_ref[...] = ENTROPY * jnp.log(p_log_ref[...])
    q_log_ref[...] = ENTROPY * jnp.log(q_log_ref[...])
    out_ref[...] = jnp.broadcast_to(row_ref[...][None], out_ref.shape)


def next_kernel(parts_ref, log_ref, p_ref, q_ref, out_ref, col_ref, z_ref, row_ref):
    lanes_to_rows(ONE_SCALE * (log_ref[...] - merge(parts_ref[...])), col_ref)
    log_sums(p_ref, q_ref, col_ref, z_ref, row_ref)
    out_ref[...] = jnp.broadcast_to(row_ref[...][None], out_ref.shape)


def last_kernel(
    parts_ref, log_ref, p_ref, q_ref, feat_ref,
    sent_ref, keep_ref, own_ref, bias_ref, flip_ref, col_ref, even_ref, odd_ref,
):
    core = lax.rem(lax.axis_index("tgt"), 2)
    chips, _, share, depth = q_ref.shape
    half = chips * share
    width = feat_ref.shape[1]
    blocks = WIDTH // share
    bias = log_ref[...] - merge(parts_ref[...])
    bias_ref[...] = bias
    lanes_to_rows(ONE_SCALE * bias, col_ref)
    flip_ref[...] = feat_ref[...].astype(jnp.float32).T.astype(jnp.bfloat16)
    sent_ref[pl.ds(width, 8), :] = jnp.zeros((8, half), jnp.float32)
    own_ref[...] = jnp.zeros((8, half), jnp.float32)

    def chunk(t):
        own, first = divmod(t * WIDTH, half)
        q = q_ref[pl.ds(first // share, blocks), core if own else 1 - core]
        return q.reshape(WIDTH, depth)

    def emit(t, tops, totals, weights):
        own, first = divmod(t * WIDTH, half)
        slabs = [
            jnp.concatenate([weight.astype(jnp.bfloat16) for weight in slab], axis=1)
            for slab in weights
        ]
        lanes = pl.ds(first, WIDTH)
        lse = jnp.concatenate([log_sum(*pair) for pair in zip(tops, totals)], axis=1)
        scale = 1.0 / jnp.concatenate(totals, axis=1)
        sent_ref[pl.ds(width + own, 1), lanes] = lse
        own_ref[pl.ds(own, 1), lanes] = lse
        if own:
            for s, slab in enumerate(slabs):
                keep_ref[pl.ds(s * SLAB, SLAB), lanes] = slab
            own_ref[pl.ds(2, 1), lanes] = scale
        else:
            weight = jnp.concatenate(slabs, axis=0)
            numer = lax.dot_general(
                flip_ref[...], weight, NN, preferred_element_type=jnp.float32
            )
            sent_ref[pl.ds(0, width), lanes] = numer * scale

    run_chunks(p_ref, chunk, 2 * half // WIDTH, col_ref, (even_ref, odd_ref), emit)


def squares(ref, k):
    rows = ref[pl.ds(k * LANES, LANES), :].astype(jnp.float32)
    norms = jnp.sum(rows * rows, axis=1, keepdims=True)
    return jnp.broadcast_to(norms, (LANES, LANES)).T[:1, :]


def own_kernel(
    keep_ref, own_ref, flip_ref, bias_ref, p_ref, q_ref, log_ref, mean_ref, pot_ref, base_ref
):
    numer = lax.dot_general(
        flip_ref[...], keep_ref[...], NN, preferred_element_type=jnp.float32
    )
    mean_ref[...] = numer * own_ref[pl.ds(2, 1), :]
    for k in range(pot_ref.shape[0]):
        row = pl.ds(k, 1)
        pot_ref[row, :] = bias_ref[row, :] + squares(p_ref, k)
    for k in range(base_ref.shape[0]):
        row = pl.ds(k, 1)
        base_ref[row, :] = log_ref[row, :] + squares(q_ref, k)


def pair_kernel(far_chip, mean_ref, own_ref, came_ref, out_ref, row_ref):
    width, half = mean_ref.shape
    chips = out_ref.shape[0]
    share = half // chips
    rows = half // LANES
    for side in range(2):
        mine = own_ref[pl.ds(1 - side, 1), :]
        other = came_ref[pl.ds(width + side, 1), :]
        top = jnp.maximum(mine, other)
        mine_share = jnp.exp2((mine - top) * ONE_SCALE)
        other_share = jnp.exp2((other - top) * ONE_SCALE)
        total = mine_share + other_share
        lse = top + ENTROPY * jnp.log(total)
        for k in range(rows):
            row_ref[pl.ds(side * rows + k, 1), :] = lse[:, k * LANES : (k + 1) * LANES]
        if side == 0:
            scale = 1.0 / total
            mine_share, other_share = mine_share * scale, other_share * scale
            step = LANES // share
            for k in range(rows):
                lanes = slice(k * LANES, (k + 1) * LANES)
                block = (
                    mean_ref[:, lanes] * mine_share[:, lanes]
                    + came_ref[pl.ds(0, width), lanes] * other_share[:, lanes]
                )
                place = (k * step - far_chip) % chips
                out_ref[pl.ds(place, step), pl.ds(0, share), :] = block.T.reshape(
                    step, share, LANES
                )
    out_ref[:, pl.ds(share, 2 * rows), :] = jnp.broadcast_to(
        row_ref[...][None], (chips, 2 * rows, LANES)
    )


def final_kernel(landed_ref, base_ref, pot_ref, out_ref):
    index = lax.axis_index("tgt")
    core, chip = lax.rem(index, 2), lax.div(index, 2)
    share = out_ref.shape[0]
    chips = landed_ref.shape[0]
    mine = landed_ref[:, pl.ds(share + lax.div(chip, 2), 1), :].reshape(chips, LANES)
    mine = jnp.exp2((mine - jnp.max(mine, axis=0, keepdims=True)) * ONE_SCALE)
    mine = mine / jnp.sum(mine, axis=0, keepdims=True)
    mine = jnp.where(lax.rem(chip, 2) == 0, mine, pltpu.roll(mine, share, 1))
    mine = jnp.concatenate([mine, jnp.zeros((LANES - chips, LANES), jnp.float32)], axis=0).T
    total = jnp.zeros(out_ref.shape, jnp.float32)
    for b in range(chips):
        scale = jnp.broadcast_to(mine[:share, b : b + 1], out_ref.shape)
        total = total + landed_ref[b, pl.ds(0, share), :] * scale
    out_ref[...] = total
    whole = merge(landed_ref[:, pl.ds(share, landed_ref.shape[1] - share), :])
    rows = whole.shape[0] // 2
    even = jnp.where(core == 0, whole[:rows], whole[rows:])
    odd = jnp.where(core == 0, whole[rows:], whole[:rows])
    lane = lax.broadcasted_iota(jnp.int32, (rows, LANES), 1)
    first = jnp.where(lane < share, even, pltpu.roll(odd, share, 1))
    second = jnp.where(lane < share, pltpu.roll(even, share, 1), odd)
    for k in range(rows):
        for side, values in enumerate((first, second)):
            row = pl.ds(2 * k + side, 1)
            pot_ref[row, :] = base_ref[row, :] - values[k : k + 1]


def rotated(n, first, stride=1):
    return [(first + stride * place) % n for place in range(n)]


def scratch(p, q):
    return [
        pltpu.VMEM((p.shape[0], LANES), jnp.float32),
        pltpu.VMEM((p.shape[0], WIDTH), jnp.float32),
        pltpu.VMEM((q.shape[0] // LANES, LANES), jnp.float32),
    ]


def call(kernel, args, outs, scratch_shapes, spaces=None):
    whole = pl.BlockSpec(memory_space=pltpu.VMEM)
    return pl.pallas_call(
        kernel,
        out_shape=outs,
        in_specs=spaces or [whole] * len(args),
        out_specs=jax.tree.map(lambda _: whole, outs),
        scratch_shapes=scratch_shapes,
        compiler_params=pltpu.CompilerParams(vmem_limit_bytes=VMEM_LIMIT),
    )(*args)


def local(source_embed, target_embed, target_feat, source_mass, target_mass):
    f32 = jnp.float32
    shape = jax.ShapeDtypeStruct
    n_src, n_tgt = lax.axis_size("src"), lax.axis_size("tgt")
    rows, depth = source_embed.shape
    width = target_feat.shape[1]
    share, half, chips = rows // n_tgt, rows // 2, n_tgt // 2
    src_mass = source_mass.reshape(-1, LANES)
    tgt_mass = target_mass.reshape(-1, LANES)
    src_rows, tgt_rows = src_mass.shape[0], tgt_mass.shape[0]
    to_src = shape((n_src, tgt_rows, LANES), f32)
    to_tgt = shape((n_tgt, src_rows, LANES), f32)
    by_src = scratch(source_embed, target_embed)
    by_tgt = scratch(target_embed, source_embed)
    far_chip = chips // 2 + math.isqrt(chips) // 2
    same_core = [[2 * chip + core for chip in rotated(chips, far_chip)] for core in range(2)]
    swap = [(index, index ^ 1) for index in range(n_tgt)]

    sems = [pltpu.SemaphoreType.DMA((rows // SLAB,)), pltpu.SemaphoreType.DMA((3,))]
    inputs = [
        pltpu.with_memory_space_constraint(array, pltpu.HBM)
        for array in (source_embed, target_embed, src_mass, tgt_mass)
    ]
    held = [shape(array.shape, array.dtype) for array in inputs]
    sent, source_embed, target_embed, src_log, tgt_log = call(
        first_kernel,
        inputs,
        (to_src, *held),
        sems + by_src,
        [pl.BlockSpec(memory_space=pltpu.HBM)] * len(inputs),
    )
    parts = lax.all_to_all(sent, "src", 0, 0, axis_index_groups=[rotated(n_src, n_src // 2)])
    sent = call(next_kernel, (parts, tgt_log, target_embed, source_embed), to_tgt, by_tgt)
    parts = lax.all_to_all(sent, "tgt", 0, 0, axis_index_groups=[rotated(n_tgt, 2 * far_chip + 1)])
    sent = call(next_kernel, (parts, src_log, source_embed, target_embed), to_src, by_src)
    parts = lax.all_to_all(sent, "src", 0, 0, axis_index_groups=[rotated(n_src, n_src // 2, n_src // 2 - 1)])
    sent, keep, own, bias, turned = call(
        last_kernel,
        (parts, tgt_log, target_embed, source_embed.reshape(chips, 2, share, depth), target_feat),
        (
            shape((width + 8, half), f32),
            shape((target_embed.shape[0], half), jnp.bfloat16),
            shape((8, half), f32),
            shape((tgt_rows, LANES), f32),
            shape(target_feat.shape[::-1], jnp.bfloat16),
        ),
        by_tgt[:2] + by_tgt[1:2],
    )
    came = lax.ppermute(sent, "tgt", swap)
    mean, target_pot, base = call(
        own_kernel,
        (keep, own, turned, bias, target_embed, source_embed, src_log),
        (shape((width, half), f32), shape(bias.shape, f32), shape(src_log.shape, f32)),
        [],
    )
    sent = call(
        functools.partial(pair_kernel, far_chip),
        (mean, own, came),
        shape((chips, share + src_rows, LANES), f32),
        [pltpu.VMEM((src_rows, LANES), f32)],
    )
    landed = lax.all_to_all(sent, "tgt", 0, 0, axis_index_groups=same_core)
    source_pot, projected = call(
        final_kernel,
        (landed, base),
        (shape((src_rows, LANES), f32), shape((share, width), f32)),
        [],
    )
    return (source_pot.reshape(-1), target_pot.reshape(-1), projected)


def solution(mesh):
    placed = (P("src", None), P("tgt", None), P("tgt", None), P("src"), P("tgt"))
    return jax.shard_map(
        local,
        mesh=mesh,
        in_specs=placed,
        out_specs=(P("src"), P("tgt"), P(("src", "tgt"), None)),
        check_vma=False,
    )
```

```python
import functools
import math

import jax
import jax.numpy as jnp
from jax import lax
from jax.experimental import pallas as pl
from jax.experimental.pallas import tpu as pltpu
from jax.sharding import PartitionSpec as P

ENTROPY = 0.05
LANES = 128
WIDTH = 256
ONE_SCALE = 1.0 / ENTROPY * math.log2(math.e)
TWO_SCALE = 2.0 * ONE_SCALE
ONE_UNIT = ENTROPY * math.log(2.0)
LOWEST, HIGHEST = 2.0**-90, 2.0**110
NT = (((1,), (1,)), ((), ()))
NN = (((1,), (0,)), ((), ()))
HALVES = WIDTH // LANES
SLAB = 512
ACCUMULATE = 32
VMEM_LIMIT = 40 * 1024 * 1024


def merge(parts):
    top = jnp.max(parts, axis=0)
    total = jnp.sum(jnp.exp2((parts - top[None]) * ONE_SCALE), axis=0)
    return top + ENTROPY * jnp.log(total)


def lanes_to_rows(values, col_ref):
    for k in range(values.shape[0]):
        square = jnp.broadcast_to(values[k : k + 1, :], (LANES, LANES))
        col_ref[pl.ds(k * LANES, LANES), :] = square.T


def fold(reduce, part):
    return reduce(part.reshape(-1, ACCUMULATE, LANES), axis=0)


def exponents(p_ref, q, col_ref, s, rows=SLAB):
    slab = pl.ds(s * rows, rows)
    cross = lax.dot_general(p_ref[slab, :], q, NT, preferred_element_type=jnp.float32)
    col = col_ref[slab, :]
    return [cross[:, h * LANES : (h + 1) * LANES] * TWO_SCALE + col for h in range(HALVES)]


def scores(p_ref, q, col_ref, z_ref, s):
    slab = pl.ds(s * SLAB, SLAB)
    tops = []
    for h, part in enumerate(exponents(p_ref, q, col_ref, s)):
        z_ref[slab, pl.ds(h * LANES, LANES)] = part
        tops.append(fold(jnp.max, part))
    return tops


def weigh(z_ref, tops, s):
    slab = pl.ds(s * SLAB, SLAB)
    weights, totals = [], []
    for h, top in enumerate(tops):
        part = z_ref[slab, pl.ds(h * LANES, LANES)]
        weight = jnp.exp2(part - top)
        weights.append(weight)
        totals.append(fold(jnp.sum, weight))
    return weights, totals


def join(op, held, more):
    return more if held is None else [op(a, b) for a, b in zip(held, more)]


def settle(reduce, values):
    return [reduce(value, axis=0, keepdims=True) for value in values]


def log_sum(top, total):
    return ONE_UNIT * top + ENTROPY * jnp.log(total)


def run_chunks(p_ref, chunk, chunks, col_ref, z_refs, emit):
    slabs = p_ref.shape[0] // SLAB
    tops = None
    for t in range(chunks + 1):
        q = chunk(t) if t < chunks else None
        later, totals, weights = None, None, []
        for s in range(slabs):
            if t < chunks:
                later = join(jnp.maximum, later, scores(p_ref, q, col_ref, z_refs[t % 2], s))
            if t > 0:
                weight, total = weigh(z_refs[(t - 1) % 2], tops, s)
                totals = join(jnp.add, totals, total)
                weights.append(weight)
        if t > 0:
            emit(t - 1, tops, settle(jnp.sum, totals), weights)
        if t < chunks:
            tops = settle(jnp.max, later)


def log_sums(p_ref, q_ref, col_ref, z_ref, row_ref, rows=2 * SLAB):
    slabs, chunks = p_ref.shape[0] // SLAB, q_ref.shape[0] // WIDTH
    totals = [None] * chunks
    for s in range(p_ref.shape[0] // rows):
        for t in range(chunks):
            parts = exponents(p_ref, q_ref[pl.ds(t * WIDTH, WIDTH), :], col_ref, s, rows)
            totals[t] = join(jnp.add, totals[t], [fold(jnp.sum, jnp.exp2(part)) for part in parts])
    for t in range(chunks):
        for h, total in enumerate(settle(jnp.sum, totals[t])):
            row_ref[pl.ds(t * HALVES + h, 1), :] = total
    sums = row_ref[...]
    row_ref[...] = ENTROPY * jnp.log(sums)
    safe = jnp.logical_and(jnp.min(sums) >= LOWEST, jnp.max(sums) <= HIGHEST)

    @pl.when(jnp.logical_not(safe))
    def _():
        @pl.loop(0, chunks)
        def _(t):
            q = q_ref[pl.ds(pl.multiple_of(t * WIDTH, WIDTH), WIDTH), :]
            tops, sums = None, None
            for s in range(slabs):
                tops = join(jnp.maximum, tops, scores(p_ref, q, col_ref, z_ref, s))
            tops = settle(jnp.max, tops)
            for s in range(slabs):
                sums = join(jnp.add, sums, weigh(z_ref, tops, s)[1])
            for h, pair in enumerate(zip(tops, settle(jnp.sum, sums))):
                row_ref[pl.ds(t * HALVES + h, 1), :] = log_sum(*pair)


def first_kernel(
    p_hbm, q_hbm, p_mass_hbm, q_mass_hbm, out_ref, p_ref, q_ref, p_log_ref, q_log_ref,
    p_sems, sems, col_ref, z_ref, row_ref,
):
    loads = []
    for s in range(p_ref.shape[0] // SLAB):
        slab = pl.ds(s * SLAB, SLAB)
        loads.append(pltpu.make_async_copy(p_hbm.at[slab, :], p_ref.at[slab, :], p_sems.at[s]))
    load_q = pltpu.make_async_copy(q_hbm, q_ref, sems.at[0])
    masses = [
        pltpu.make_async_copy(p_mass_hbm, p_log_ref, sems.at[1]),
        pltpu.make_async_copy(q_mass_hbm, q_log_ref, sems.at[2]),
    ]
    for copy in loads + [load_q] + masses:
        copy.start()
    for s, copy in enumerate(loads):
        copy.wait()
        slab = pl.ds(s * SLAB, SLAB)
        p = p_ref[slab, :].astype(jnp.float32)
        norms = jnp.sum(p * p, axis=1, keepdims=True)
        col_ref[slab, :] = jnp.broadcast_to(-ONE_SCALE * norms, (SLAB, LANES))
    load_q.wait()
    log_sums(p_ref, q_ref, col_ref, z_ref, row_ref)
    for copy in masses:
        copy.wait()
    p_log_ref[...] = ENTROPY * jnp.log(p_log_ref[...])
    q_log_ref[...] = ENTROPY * jnp.log(q_log_ref[...])
    out_ref[...] = jnp.broadcast_to(row_ref[...][None], out_ref.shape)


def next_kernel(parts_ref, log_ref, p_ref, q_ref, out_ref, col_ref, z_ref, row_ref):
    lanes_to_rows(ONE_SCALE * (log_ref[...] - merge(parts_ref[...])), col_ref)
    log_sums(p_ref, q_ref, col_ref, z_ref, row_ref)
    out_ref[...] = jnp.broadcast_to(row_ref[...][None], out_ref.shape)


def last_kernel(
    parts_ref, log_ref, p_ref, q_ref, feat_ref,
    sent_ref, keep_ref, own_ref, bias_ref, flip_ref, col_ref, even_ref, odd_ref,
):
    core = lax.rem(lax.axis_index("tgt"), 2)
    chips, _, share, depth = q_ref.shape
    half = chips * share
    width = feat_ref.shape[1]
    blocks = WIDTH // share
    bias = log_ref[...] - merge(parts_ref[...])
    bias_ref[...] = bias
    lanes_to_rows(ONE_SCALE * bias, col_ref)
    flip_ref[...] = feat_ref[...].astype(jnp.float32).T.astype(jnp.bfloat16)
    sent_ref[pl.ds(width, 8), :] = jnp.zeros((8, half), jnp.float32)
    own_ref[...] = jnp.zeros((8, half), jnp.float32)

    def chunk(t):
        own, first = divmod(t * WIDTH, half)
        q = q_ref[pl.ds(first // share, blocks), core if own else 1 - core]
        return q.reshape(WIDTH, depth)

    def emit(t, tops, totals, weights):
        own, first = divmod(t * WIDTH, half)
        slabs = [
            jnp.concatenate([weight.astype(jnp.bfloat16) for weight in slab], axis=1)
            for slab in weights
        ]
        lanes = pl.ds(first, WIDTH)
        lse = jnp.concatenate([log_sum(*pair) for pair in zip(tops, totals)], axis=1)
        scale = 1.0 / jnp.concatenate(totals, axis=1)
        sent_ref[pl.ds(width + own, 1), lanes] = lse
        own_ref[pl.ds(own, 1), lanes] = lse
        if own:
            for s, slab in enumerate(slabs):
                keep_ref[pl.ds(s * SLAB, SLAB), lanes] = slab
            own_ref[pl.ds(2, 1), lanes] = scale
        else:
            weight = jnp.concatenate(slabs, axis=0)
            numer = lax.dot_general(
                flip_ref[...], weight, NN, preferred_element_type=jnp.float32
            )
            sent_ref[pl.ds(0, width), lanes] = numer * scale

    run_chunks(p_ref, chunk, 2 * half // WIDTH, col_ref, (even_ref, odd_ref), emit)


def squares(ref, k):
    rows = ref[pl.ds(k * LANES, LANES), :].astype(jnp.float32)
    norms = jnp.sum(rows * rows, axis=1, keepdims=True)
    return jnp.broadcast_to(norms, (LANES, LANES)).T[:1, :]


def own_kernel(
    keep_ref, own_ref, flip_ref, bias_ref, p_ref, q_ref, log_ref, mean_ref, pot_ref, base_ref
):
    numer = lax.dot_general(
        flip_ref[...], keep_ref[...], NN, preferred_element_type=jnp.float32
    )
    mean_ref[...] = numer * own_ref[pl.ds(2, 1), :]
    for k in range(pot_ref.shape[0]):
        row = pl.ds(k, 1)
        pot_ref[row, :] = bias_ref[row, :] + squares(p_ref, k)
    for k in range(base_ref.shape[0]):
        row = pl.ds(k, 1)
        base_ref[row, :] = log_ref[row, :] + squares(q_ref, k)


def pair_kernel(far_chip, mean_ref, own_ref, came_ref, out_ref, row_ref):
    width, half = mean_ref.shape
    chips = out_ref.shape[0]
    share = half // chips
    rows = half // LANES
    for side in range(2):
        mine = own_ref[pl.ds(1 - side, 1), :]
        other = came_ref[pl.ds(width + side, 1), :]
        top = jnp.maximum(mine, other)
        mine_share = jnp.exp2((mine - top) * ONE_SCALE)
        other_share = jnp.exp2((other - top) * ONE_SCALE)
        total = mine_share + other_share
        lse = top + ENTROPY * jnp.log(total)
        for k in range(rows):
            row_ref[pl.ds(side * rows + k, 1), :] = lse[:, k * LANES : (k + 1) * LANES]
        if side == 0:
            scale = 1.0 / total
            mine_share, other_share = mine_share * scale, other_share * scale
            step = LANES // share
            for k in range(rows):
                lanes = slice(k * LANES, (k + 1) * LANES)
                block = (
                    mean_ref[:, lanes] * mine_share[:, lanes]
                    + came_ref[pl.ds(0, width), lanes] * other_share[:, lanes]
                )
                place = (k * step - far_chip) % chips
                out_ref[pl.ds(place, step), pl.ds(0, share), :] = block.T.reshape(
                    step, share, LANES
                )
    out_ref[:, pl.ds(share, 2 * rows), :] = jnp.broadcast_to(
        row_ref[...][None], (chips, 2 * rows, LANES)
    )


def final_kernel(landed_ref, base_ref, pot_ref, out_ref):
    index = lax.axis_index("tgt")
    core, chip = lax.rem(index, 2), lax.div(index, 2)
    share = out_ref.shape[0]
    chips = landed_ref.shape[0]
    mine = landed_ref[:, pl.ds(share + lax.div(chip, 2), 1), :].reshape(chips, LANES)
    mine = jnp.exp2((mine - jnp.max(mine, axis=0, keepdims=True)) * ONE_SCALE)
    mine = mine / jnp.sum(mine, axis=0, keepdims=True)
    mine = jnp.where(lax.rem(chip, 2) == 0, mine, pltpu.roll(mine, share, 1))
    mine = jnp.concatenate([mine, jnp.zeros((LANES - chips, LANES), jnp.float32)], axis=0).T
    total = jnp.zeros(out_ref.shape, jnp.float32)
    for b in range(chips):
        scale = jnp.broadcast_to(mine[:share, b : b + 1], out_ref.shape)
        total = total + landed_ref[b, pl.ds(0, share), :] * scale
    out_ref[...] = total
    whole = merge(landed_ref[:, pl.ds(share, landed_ref.shape[1] - share), :])
    rows = whole.shape[0] // 2
    even = jnp.where(core == 0, whole[:rows], whole[rows:])
    odd = jnp.where(core == 0, whole[rows:], whole[:rows])
    lane = lax.broadcasted_iota(jnp.int32, (rows, LANES), 1)
    first = jnp.where(lane < share, even, pltpu.roll(odd, share, 1))
    second = jnp.where(lane < share, pltpu.roll(even, share, 1), odd)
    for k in range(rows):
        for side, values in enumerate((first, second)):
            row = pl.ds(2 * k + side, 1)
            pot_ref[row, :] = base_ref[row, :] - values[k : k + 1]


def rotated(n, first):
    return [(first + place) % n for place in range(n)]


def near_first(n):
    return [n // 2] + sorted(set(range(n)) - {n // 2}, key=lambda place: min(place, n - place))


def scratch(p, q):
    return [
        pltpu.VMEM((p.shape[0], LANES), jnp.float32),
        pltpu.VMEM((p.shape[0], WIDTH), jnp.float32),
        pltpu.VMEM((q.shape[0] // LANES, LANES), jnp.float32),
    ]


def call(kernel, args, outs, scratch_shapes, spaces=None):
    whole = pl.BlockSpec(memory_space=pltpu.VMEM)
    return pl.pallas_call(
        kernel,
        out_shape=outs,
        in_specs=spaces or [whole] * len(args),
        out_specs=jax.tree.map(lambda _: whole, outs),
        scratch_shapes=scratch_shapes,
        compiler_params=pltpu.CompilerParams(vmem_limit_bytes=VMEM_LIMIT),
    )(*args)


def local(source_embed, target_embed, target_feat, source_mass, target_mass):
    f32 = jnp.float32
    shape = jax.ShapeDtypeStruct
    n_src, n_tgt = lax.axis_size("src"), lax.axis_size("tgt")
    rows, depth = source_embed.shape
    width = target_feat.shape[1]
    share, half, chips = rows // n_tgt, rows // 2, n_tgt // 2
    src_mass = source_mass.reshape(-1, LANES)
    tgt_mass = target_mass.reshape(-1, LANES)
    src_rows, tgt_rows = src_mass.shape[0], tgt_mass.shape[0]
    to_src = shape((n_src, tgt_rows, LANES), f32)
    to_tgt = shape((n_tgt, src_rows, LANES), f32)
    by_src = scratch(source_embed, target_embed)
    by_tgt = scratch(target_embed, source_embed)
    far_chip = chips // 2 + math.isqrt(chips) // 2
    same_core = [[2 * chip + core for chip in rotated(chips, far_chip)] for core in range(2)]
    swap = [(index, index ^ 1) for index in range(n_tgt)]

    sems = [pltpu.SemaphoreType.DMA((rows // SLAB,)), pltpu.SemaphoreType.DMA((3,))]
    inputs = [
        pltpu.with_memory_space_constraint(array, pltpu.HBM)
        for array in (source_embed, target_embed, src_mass, tgt_mass)
    ]
    held = [shape(array.shape, array.dtype) for array in inputs]
    sent, source_embed, target_embed, src_log, tgt_log = call(
        first_kernel,
        inputs,
        (to_src, *held),
        sems + by_src,
        [pl.BlockSpec(memory_space=pltpu.HBM)] * len(inputs),
    )
    parts = lax.all_to_all(sent, "src", 0, 0, axis_index_groups=[near_first(n_src)])
    sent = call(next_kernel, (parts, tgt_log, target_embed, source_embed), to_tgt, by_tgt)
    parts = lax.all_to_all(sent, "tgt", 0, 0, axis_index_groups=[rotated(n_tgt, 2 * far_chip + 1)])
    sent = call(next_kernel, (parts, src_log, source_embed, target_embed), to_src, by_src)
    parts = lax.all_to_all(sent, "src", 0, 0, axis_index_groups=[near_first(n_src)])
    sent, keep, own, bias, turned = call(
        last_kernel,
        (parts, tgt_log, target_embed, source_embed.reshape(chips, 2, share, depth), target_feat),
        (
            shape((width + 8, half), f32),
            shape((target_embed.shape[0], half), jnp.bfloat16),
            shape((8, half), f32),
            shape((tgt_rows, LANES), f32),
            shape(target_feat.shape[::-1], jnp.bfloat16),
        ),
        by_tgt[:2] + by_tgt[1:2],
    )
    came = lax.ppermute(sent, "tgt", swap)
    mean, target_pot, base = call(
        own_kernel,
        (keep, own, turned, bias, target_embed, source_embed, src_log),
        (shape((width, half), f32), shape(bias.shape, f32), shape(src_log.shape, f32)),
        [],
    )
    sent = call(
        functools.partial(pair_kernel, far_chip),
        (mean, own, came),
        shape((chips, share + src_rows, LANES), f32),
        [pltpu.VMEM((src_rows, LANES), f32)],
    )
    landed = lax.all_to_all(sent, "tgt", 0, 0, axis_index_groups=same_core)
    source_pot, projected = call(
        final_kernel,
        (landed, base),
        (shape((src_rows, LANES), f32), shape((share, width), f32)),
        [],
    )
    return (source_pot.reshape(-1), target_pot.reshape(-1), projected)


def solution(mesh):
    placed = (P("src", None), P("tgt", None), P("tgt", None), P("src"), P("tgt"))
    return jax.shard_map(
        local,
        mesh=mesh,
        in_specs=placed,
        out_specs=(P("src"), P("tgt"), P(("src", "tgt"), None)),
        check_vma=False,
    )
```

```python
import functools
import math

import jax
import jax.numpy as jnp
from jax import lax
from jax.experimental import pallas as pl
from jax.experimental.pallas import tpu as pltpu
from jax.sharding import PartitionSpec as P

ENTROPY = 0.05
LANES = 128
WIDTH = 256
ONE_SCALE = 1.0 / ENTROPY * math.log2(math.e)
TWO_SCALE = 2.0 * ONE_SCALE
ONE_UNIT = ENTROPY * math.log(2.0)
LOWEST, HIGHEST = 2.0**-90, 2.0**110
NT = (((1,), (1,)), ((), ()))
NN = (((1,), (0,)), ((), ()))
HALVES = WIDTH // LANES
SLAB = 512
ACCUMULATE = 32
VMEM_LIMIT = 40 * 1024 * 1024


def merge(parts):
    top = jnp.max(parts, axis=0)
    total = jnp.sum(jnp.exp2((parts - top[None]) * ONE_SCALE), axis=0)
    return top + ENTROPY * jnp.log(total)


def lanes_to_rows(values, col_ref):
    for k in range(values.shape[0]):
        square = jnp.broadcast_to(values[k : k + 1, :], (LANES, LANES))
        col_ref[pl.ds(k * LANES, LANES), :] = square.T


def fold(reduce, part):
    return reduce(part.reshape(-1, ACCUMULATE, LANES), axis=0)


def exponents(p_ref, q, col_ref, s, rows=SLAB):
    slab = pl.ds(s * rows, rows)
    cross = lax.dot_general(p_ref[slab, :], q, NT, preferred_element_type=jnp.float32)
    col = col_ref[slab, :]
    return [cross[:, h * LANES : (h + 1) * LANES] * TWO_SCALE + col for h in range(HALVES)]


def scores(p_ref, q, col_ref, z_ref, s):
    slab = pl.ds(s * SLAB, SLAB)
    tops = []
    for h, part in enumerate(exponents(p_ref, q, col_ref, s)):
        z_ref[slab, pl.ds(h * LANES, LANES)] = part
        tops.append(fold(jnp.max, part))
    return tops


def weigh(z_ref, tops, s):
    slab = pl.ds(s * SLAB, SLAB)
    weights, totals = [], []
    for h, top in enumerate(tops):
        part = z_ref[slab, pl.ds(h * LANES, LANES)]
        weight = jnp.exp2(part - top)
        weights.append(weight)
        totals.append(fold(jnp.sum, weight))
    return weights, totals


def join(op, held, more):
    return more if held is None else [op(a, b) for a, b in zip(held, more)]


def settle(reduce, values):
    return [reduce(value, axis=0, keepdims=True) for value in values]


def log_sum(top, total):
    return ONE_UNIT * top + ENTROPY * jnp.log(total)


def run_chunks(p_ref, chunk, chunks, col_ref, z_refs, emit):
    slabs = p_ref.shape[0] // SLAB
    tops = None
    for t in range(chunks + 1):
        q = chunk(t) if t < chunks else None
        later, totals, weights = None, None, []
        for s in range(slabs):
            if t < chunks:
                later = join(jnp.maximum, later, scores(p_ref, q, col_ref, z_refs[t % 2], s))
            if t > 0:
                weight, total = weigh(z_refs[(t - 1) % 2], tops, s)
                totals = join(jnp.add, totals, total)
                weights.append(weight)
        if t > 0:
            emit(t - 1, tops, settle(jnp.sum, totals), weights)
        if t < chunks:
            tops = settle(jnp.max, later)


def log_sums(p_ref, q_ref, col_ref, z_ref, row_ref, rows=2 * SLAB):
    slabs, chunks = p_ref.shape[0] // SLAB, q_ref.shape[0] // WIDTH
    totals = [None] * chunks
    for s in range(p_ref.shape[0] // rows):
        for t in range(chunks):
            parts = exponents(p_ref, q_ref[pl.ds(t * WIDTH, WIDTH), :], col_ref, s, rows)
            totals[t] = join(jnp.add, totals[t], [fold(jnp.sum, jnp.exp2(part)) for part in parts])
    for t in range(chunks):
        for h, total in enumerate(settle(jnp.sum, totals[t])):
            row_ref[pl.ds(t * HALVES + h, 1), :] = total
    sums = row_ref[...]
    row_ref[...] = ENTROPY * jnp.log(sums)
    safe = jnp.logical_and(jnp.min(sums) >= LOWEST, jnp.max(sums) <= HIGHEST)

    @pl.when(jnp.logical_not(safe))
    def _():
        @pl.loop(0, chunks)
        def _(t):
            q = q_ref[pl.ds(pl.multiple_of(t * WIDTH, WIDTH), WIDTH), :]
            tops, sums = None, None
            for s in range(slabs):
                tops = join(jnp.maximum, tops, scores(p_ref, q, col_ref, z_ref, s))
            tops = settle(jnp.max, tops)
            for s in range(slabs):
                sums = join(jnp.add, sums, weigh(z_ref, tops, s)[1])
            for h, pair in enumerate(zip(tops, settle(jnp.sum, sums))):
                row_ref[pl.ds(t * HALVES + h, 1), :] = log_sum(*pair)


def first_kernel(
    p_hbm, q_hbm, p_mass_hbm, q_mass_hbm, out_ref, p_ref, q_ref, p_log_ref, q_log_ref,
    p_sems, sems, col_ref, z_ref, row_ref,
):
    loads = []
    for s in range(p_ref.shape[0] // SLAB):
        slab = pl.ds(s * SLAB, SLAB)
        loads.append(pltpu.make_async_copy(p_hbm.at[slab, :], p_ref.at[slab, :], p_sems.at[s]))
    load_q = pltpu.make_async_copy(q_hbm, q_ref, sems.at[0])
    masses = [
        pltpu.make_async_copy(p_mass_hbm, p_log_ref, sems.at[1]),
        pltpu.make_async_copy(q_mass_hbm, q_log_ref, sems.at[2]),
    ]
    for copy in loads + [load_q] + masses:
        copy.start()
    for s, copy in enumerate(loads):
        copy.wait()
        slab = pl.ds(s * SLAB, SLAB)
        p = p_ref[slab, :].astype(jnp.float32)
        norms = jnp.sum(p * p, axis=1, keepdims=True)
        col_ref[slab, :] = jnp.broadcast_to(-ONE_SCALE * norms, (SLAB, LANES))
    load_q.wait()
    log_sums(p_ref, q_ref, col_ref, z_ref, row_ref)
    for copy in masses:
        copy.wait()
    p_log_ref[...] = ENTROPY * jnp.log(p_log_ref[...])
    q_log_ref[...] = ENTROPY * jnp.log(q_log_ref[...])
    out_ref[...] = jnp.broadcast_to(row_ref[...][None], out_ref.shape)


def next_kernel(parts_ref, log_ref, p_ref, q_ref, out_ref, col_ref, z_ref, row_ref):
    lanes_to_rows(ONE_SCALE * (log_ref[...] - merge(parts_ref[...])), col_ref)
    log_sums(p_ref, q_ref, col_ref, z_ref, row_ref)
    out_ref[...] = jnp.broadcast_to(row_ref[...][None], out_ref.shape)


def last_kernel(
    parts_ref, log_ref, p_ref, q_ref, feat_ref,
    sent_ref, keep_ref, own_ref, bias_ref, flip_ref, col_ref, even_ref, odd_ref,
):
    core = lax.rem(lax.axis_index("tgt"), 2)
    chips, _, share, depth = q_ref.shape
    half = chips * share
    width = feat_ref.shape[1]
    blocks = WIDTH // share
    bias = log_ref[...] - merge(parts_ref[...])
    bias_ref[...] = bias
    lanes_to_rows(ONE_SCALE * bias, col_ref)
    flip_ref[...] = feat_ref[...].astype(jnp.float32).T.astype(jnp.bfloat16)
    sent_ref[pl.ds(width, 8), :] = jnp.zeros((8, half), jnp.float32)
    own_ref[...] = jnp.zeros((8, half), jnp.float32)

    def chunk(t):
        own, first = divmod(t * WIDTH, half)
        q = q_ref[pl.ds(first // share, blocks), core if own else 1 - core]
        return q.reshape(WIDTH, depth)

    def emit(t, tops, totals, weights):
        own, first = divmod(t * WIDTH, half)
        slabs = [
            jnp.concatenate([weight.astype(jnp.bfloat16) for weight in slab], axis=1)
            for slab in weights
        ]
        lanes = pl.ds(first, WIDTH)
        lse = jnp.concatenate([log_sum(*pair) for pair in zip(tops, totals)], axis=1)
        scale = 1.0 / jnp.concatenate(totals, axis=1)
        sent_ref[pl.ds(width + own, 1), lanes] = lse
        own_ref[pl.ds(own, 1), lanes] = lse
        if own:
            for s, slab in enumerate(slabs):
                keep_ref[pl.ds(s * SLAB, SLAB), lanes] = slab
            own_ref[pl.ds(2, 1), lanes] = scale
        else:
            weight = jnp.concatenate(slabs, axis=0)
            numer = lax.dot_general(
                flip_ref[...], weight, NN, preferred_element_type=jnp.float32
            )
            sent_ref[pl.ds(0, width), lanes] = numer * scale

    run_chunks(p_ref, chunk, 2 * half // WIDTH, col_ref, (even_ref, odd_ref), emit)


def squares(ref, k):
    rows = ref[pl.ds(k * LANES, LANES), :].astype(jnp.float32)
    norms = jnp.sum(rows * rows, axis=1, keepdims=True)
    return jnp.broadcast_to(norms, (LANES, LANES)).T[:1, :]


def own_kernel(
    keep_ref, own_ref, flip_ref, bias_ref, p_ref, q_ref, log_ref, mean_ref, pot_ref, base_ref
):
    numer = lax.dot_general(
        flip_ref[...], keep_ref[...], NN, preferred_element_type=jnp.float32
    )
    mean_ref[...] = numer * own_ref[pl.ds(2, 1), :]
    for k in range(pot_ref.shape[0]):
        row = pl.ds(k, 1)
        pot_ref[row, :] = bias_ref[row, :] + squares(p_ref, k)
    for k in range(base_ref.shape[0]):
        row = pl.ds(k, 1)
        base_ref[row, :] = log_ref[row, :] + squares(q_ref, k)


def pair_kernel(far_chip, mean_ref, own_ref, came_ref, out_ref, row_ref):
    width, half = mean_ref.shape
    chips = out_ref.shape[0]
    share = half // chips
    rows = half // LANES
    for side in range(2):
        mine = own_ref[pl.ds(1 - side, 1), :]
        other = came_ref[pl.ds(width + side, 1), :]
        top = jnp.maximum(mine, other)
        mine_share = jnp.exp2((mine - top) * ONE_SCALE)
        other_share = jnp.exp2((other - top) * ONE_SCALE)
        total = mine_share + other_share
        lse = top + ENTROPY * jnp.log(total)
        for k in range(rows):
            row_ref[pl.ds(side * rows + k, 1), :] = lse[:, k * LANES : (k + 1) * LANES]
        if side == 0:
            scale = 1.0 / total
            mine_share, other_share = mine_share * scale, other_share * scale
            step = LANES // share
            for k in range(rows):
                lanes = slice(k * LANES, (k + 1) * LANES)
                block = (
                    mean_ref[:, lanes] * mine_share[:, lanes]
                    + came_ref[pl.ds(0, width), lanes] * other_share[:, lanes]
                )
                place = (k * step - far_chip) % chips
                out_ref[pl.ds(place, step), pl.ds(0, share), :] = block.T.reshape(
                    step, share, LANES
                )
    out_ref[:, pl.ds(share, 2 * rows), :] = jnp.broadcast_to(
        row_ref[...][None], (chips, 2 * rows, LANES)
    )


def final_kernel(landed_ref, base_ref, pot_ref, out_ref):
    index = lax.axis_index("tgt")
    core, chip = lax.rem(index, 2), lax.div(index, 2)
    share = out_ref.shape[0]
    chips = landed_ref.shape[0]
    mine = landed_ref[:, pl.ds(share + lax.div(chip, 2), 1), :].reshape(chips, LANES)
    mine = jnp.exp2((mine - jnp.max(mine, axis=0, keepdims=True)) * ONE_SCALE)
    mine = mine / jnp.sum(mine, axis=0, keepdims=True)
    mine = jnp.where(lax.rem(chip, 2) == 0, mine, pltpu.roll(mine, share, 1))
    mine = jnp.concatenate([mine, jnp.zeros((LANES - chips, LANES), jnp.float32)], axis=0).T
    total = jnp.zeros(out_ref.shape, jnp.float32)
    for b in range(chips):
        scale = jnp.broadcast_to(mine[:share, b : b + 1], out_ref.shape)
        total = total + landed_ref[b, pl.ds(0, share), :] * scale
    out_ref[...] = total
    whole = merge(landed_ref[:, pl.ds(share, landed_ref.shape[1] - share), :])
    rows = whole.shape[0] // 2
    even = jnp.where(core == 0, whole[:rows], whole[rows:])
    odd = jnp.where(core == 0, whole[rows:], whole[:rows])
    lane = lax.broadcasted_iota(jnp.int32, (rows, LANES), 1)
    first = jnp.where(lane < share, even, pltpu.roll(odd, share, 1))
    second = jnp.where(lane < share, pltpu.roll(even, share, 1), odd)
    for k in range(rows):
        for side, values in enumerate((first, second)):
            row = pl.ds(2 * k + side, 1)
            pot_ref[row, :] = base_ref[row, :] - values[k : k + 1]


def rotated(n, first):
    return [(first + place) % n for place in range(n)]


def near_first(n):
    return [n // 2] + sorted(set(range(n)) - {n // 2}, key=lambda place: min(place, n - place))


def scratch(p, q):
    return [
        pltpu.VMEM((p.shape[0], LANES), jnp.float32),
        pltpu.VMEM((p.shape[0], WIDTH), jnp.float32),
        pltpu.VMEM((q.shape[0] // LANES, LANES), jnp.float32),
    ]


def call(kernel, args, outs, scratch_shapes, spaces=None):
    whole = pl.BlockSpec(memory_space=pltpu.VMEM)
    return pl.pallas_call(
        kernel,
        out_shape=outs,
        in_specs=spaces or [whole] * len(args),
        out_specs=jax.tree.map(lambda _: whole, outs),
        scratch_shapes=scratch_shapes,
        compiler_params=pltpu.CompilerParams(vmem_limit_bytes=VMEM_LIMIT),
    )(*args)


def local(source_embed, target_embed, target_feat, source_mass, target_mass):
    f32 = jnp.float32
    shape = jax.ShapeDtypeStruct
    n_src, n_tgt = lax.axis_size("src"), lax.axis_size("tgt")
    rows, depth = source_embed.shape
    width = target_feat.shape[1]
    share, half, chips = rows // n_tgt, rows // 2, n_tgt // 2
    src_mass = source_mass.reshape(-1, LANES)
    tgt_mass = target_mass.reshape(-1, LANES)
    src_rows, tgt_rows = src_mass.shape[0], tgt_mass.shape[0]
    to_src = shape((n_src, tgt_rows, LANES), f32)
    to_tgt = shape((n_tgt, src_rows, LANES), f32)
    by_src = scratch(source_embed, target_embed)
    by_tgt = scratch(target_embed, source_embed)
    far_chip = chips // 2 + math.isqrt(chips) // 2
    same_core = [[2 * chip + core for chip in rotated(chips, far_chip)] for core in range(2)]
    swap = [(index, index ^ 1) for index in range(n_tgt)]

    sems = [pltpu.SemaphoreType.DMA((rows // SLAB,)), pltpu.SemaphoreType.DMA((3,))]
    inputs = [
        pltpu.with_memory_space_constraint(array, pltpu.HBM)
        for array in (source_embed, target_embed, src_mass, tgt_mass)
    ]
    held = [shape(array.shape, array.dtype) for array in inputs]
    sent, source_embed, target_embed, src_log, tgt_log = call(
        first_kernel,
        inputs,
        (to_src, *held),
        sems + by_src,
        [pl.BlockSpec(memory_space=pltpu.HBM)] * len(inputs),
    )
    parts = lax.all_to_all(sent, "src", 0, 0, axis_index_groups=[near_first(n_src)])
    sent = call(next_kernel, (parts, tgt_log, target_embed, source_embed), to_tgt, by_tgt)
    parts = lax.all_to_all(sent, "tgt", 0, 0, axis_index_groups=[rotated(n_tgt, 2 * far_chip + 1)])
    sent = call(next_kernel, (parts, src_log, source_embed, target_embed), to_src, by_src)
    parts = lax.all_to_all(sent, "src", 0, 0, axis_index_groups=[rotated(n_src, n_src // 2)])
    sent, keep, own, bias, turned = call(
        last_kernel,
        (parts, tgt_log, target_embed, source_embed.reshape(chips, 2, share, depth), target_feat),
        (
            shape((width + 8, half), f32),
            shape((target_embed.shape[0], half), jnp.bfloat16),
            shape((8, half), f32),
            shape((tgt_rows, LANES), f32),
            shape(target_feat.shape[::-1], jnp.bfloat16),
        ),
        by_tgt[:2] + by_tgt[1:2],
    )
    came = lax.ppermute(sent, "tgt", swap)
    mean, target_pot, base = call(
        own_kernel,
        (keep, own, turned, bias, target_embed, source_embed, src_log),
        (shape((width, half), f32), shape(bias.shape, f32), shape(src_log.shape, f32)),
        [],
    )
    sent = call(
        functools.partial(pair_kernel, far_chip),
        (mean, own, came),
        shape((chips, share + src_rows, LANES), f32),
        [pltpu.VMEM((src_rows, LANES), f32)],
    )
    landed = lax.all_to_all(sent, "tgt", 0, 0, axis_index_groups=same_core)
    source_pot, projected = call(
        final_kernel,
        (landed, base),
        (shape((src_rows, LANES), f32), shape((share, width), f32)),
        [],
    )
    return (source_pot.reshape(-1), target_pot.reshape(-1), projected)


def solution(mesh):
    placed = (P("src", None), P("tgt", None), P("tgt", None), P("src"), P("tgt"))
    return jax.shard_map(
        local,
        mesh=mesh,
        in_specs=placed,
        out_specs=(P("src"), P("tgt"), P(("src", "tgt"), None)),
        check_vma=False,
    )
```

```python
import functools
import math

import jax
import jax.numpy as jnp
from jax import lax
from jax.experimental import pallas as pl
from jax.experimental.pallas import tpu as pltpu
from jax.sharding import PartitionSpec as P

ENTROPY = 0.05
LANES = 128
WIDTH = 256
ONE_SCALE = 1.0 / ENTROPY * math.log2(math.e)
TWO_SCALE = 2.0 * ONE_SCALE
ONE_UNIT = ENTROPY * math.log(2.0)
LOWEST, HIGHEST = 2.0**-90, 2.0**110
NT = (((1,), (1,)), ((), ()))
NN = (((1,), (0,)), ((), ()))
HALVES = WIDTH // LANES
SLAB = 512
ACCUMULATE = 32
VMEM_LIMIT = 40 * 1024 * 1024


def merge(parts):
    top = jnp.max(parts, axis=0)
    total = jnp.sum(jnp.exp2((parts - top[None]) * ONE_SCALE), axis=0)
    return top + ENTROPY * jnp.log(total)


def lanes_to_rows(values, col_ref):
    for k in range(values.shape[0]):
        square = jnp.broadcast_to(values[k : k + 1, :], (LANES, LANES))
        col_ref[pl.ds(k * LANES, LANES), :] = square.T


def fold(reduce, part):
    return reduce(part.reshape(-1, ACCUMULATE, LANES), axis=0)


def exponents(p_ref, q, col_ref, s, rows=SLAB):
    slab = pl.ds(s * rows, rows)
    cross = lax.dot_general(p_ref[slab, :], q, NT, preferred_element_type=jnp.float32)
    col = col_ref[slab, :]
    return [cross[:, h * LANES : (h + 1) * LANES] * TWO_SCALE + col for h in range(HALVES)]


def scores(p_ref, q, col_ref, z_ref, s):
    slab = pl.ds(s * SLAB, SLAB)
    tops = []
    for h, part in enumerate(exponents(p_ref, q, col_ref, s)):
        z_ref[slab, pl.ds(h * LANES, LANES)] = part
        tops.append(fold(jnp.max, part))
    return tops


def weigh(z_ref, tops, s):
    slab = pl.ds(s * SLAB, SLAB)
    weights, totals = [], []
    for h, top in enumerate(tops):
        part = z_ref[slab, pl.ds(h * LANES, LANES)]
        weight = jnp.exp2(part - top)
        weights.append(weight)
        totals.append(fold(jnp.sum, weight))
    return weights, totals


def join(op, held, more):
    return more if held is None else [op(a, b) for a, b in zip(held, more)]


def settle(reduce, values):
    return [reduce(value, axis=0, keepdims=True) for value in values]


def log_sum(top, total):
    return ONE_UNIT * top + ENTROPY * jnp.log(total)


def run_chunks(p_ref, chunk, chunks, col_ref, z_refs, emit):
    slabs = p_ref.shape[0] // SLAB
    tops = None
    for t in range(chunks + 1):
        q = chunk(t) if t < chunks else None
        later, totals, weights = None, None, []
        for s in range(slabs):
            if t < chunks:
                later = join(jnp.maximum, later, scores(p_ref, q, col_ref, z_refs[t % 2], s))
            if t > 0:
                weight, total = weigh(z_refs[(t - 1) % 2], tops, s)
                totals = join(jnp.add, totals, total)
                weights.append(weight)
        if t > 0:
            emit(t - 1, tops, settle(jnp.sum, totals), weights)
        if t < chunks:
            tops = settle(jnp.max, later)


def log_sums(p_ref, q_ref, col_ref, z_ref, row_ref, rows=2 * SLAB):
    slabs, chunks = p_ref.shape[0] // SLAB, q_ref.shape[0] // WIDTH
    totals = [None] * chunks
    for s in range(p_ref.shape[0] // rows):
        for t in range(chunks):
            parts = exponents(p_ref, q_ref[pl.ds(t * WIDTH, WIDTH), :], col_ref, s, rows)
            totals[t] = join(jnp.add, totals[t], [fold(jnp.sum, jnp.exp2(part)) for part in parts])
    for t in range(chunks):
        for h, total in enumerate(settle(jnp.sum, totals[t])):
            row_ref[pl.ds(t * HALVES + h, 1), :] = total
    sums = row_ref[...]
    row_ref[...] = ENTROPY * jnp.log(sums)
    safe = jnp.logical_and(jnp.min(sums) >= LOWEST, jnp.max(sums) <= HIGHEST)

    @pl.when(jnp.logical_not(safe))
    def _():
        @pl.loop(0, chunks)
        def _(t):
            q = q_ref[pl.ds(pl.multiple_of(t * WIDTH, WIDTH), WIDTH), :]
            tops, sums = None, None
            for s in range(slabs):
                tops = join(jnp.maximum, tops, scores(p_ref, q, col_ref, z_ref, s))
            tops = settle(jnp.max, tops)
            for s in range(slabs):
                sums = join(jnp.add, sums, weigh(z_ref, tops, s)[1])
            for h, pair in enumerate(zip(tops, settle(jnp.sum, sums))):
                row_ref[pl.ds(t * HALVES + h, 1), :] = log_sum(*pair)


def first_kernel(
    p_hbm, q_hbm, p_mass_hbm, q_mass_hbm, out_ref, p_ref, q_ref, p_log_ref, q_log_ref,
    p_sems, sems, col_ref, z_ref, row_ref,
):
    loads = []
    for s in range(p_ref.shape[0] // SLAB):
        slab = pl.ds(s * SLAB, SLAB)
        loads.append(pltpu.make_async_copy(p_hbm.at[slab, :], p_ref.at[slab, :], p_sems.at[s]))
    load_q = pltpu.make_async_copy(q_hbm, q_ref, sems.at[0])
    masses = [
        pltpu.make_async_copy(p_mass_hbm, p_log_ref, sems.at[1]),
        pltpu.make_async_copy(q_mass_hbm, q_log_ref, sems.at[2]),
    ]
    for copy in loads + [load_q] + masses:
        copy.start()
    for s, copy in enumerate(loads):
        copy.wait()
        slab = pl.ds(s * SLAB, SLAB)
        p = p_ref[slab, :].astype(jnp.float32)
        norms = jnp.sum(p * p, axis=1, keepdims=True)
        col_ref[slab, :] = jnp.broadcast_to(-ONE_SCALE * norms, (SLAB, LANES))
    load_q.wait()
    log_sums(p_ref, q_ref, col_ref, z_ref, row_ref)
    for copy in masses:
        copy.wait()
    p_log_ref[...] = ENTROPY * jnp.log(p_log_ref[...])
    q_log_ref[...] = ENTROPY * jnp.log(q_log_ref[...])
    out_ref[...] = jnp.broadcast_to(row_ref[...][None], out_ref.shape)


def next_kernel(parts_ref, log_ref, p_ref, q_ref, out_ref, col_ref, z_ref, row_ref):
    lanes_to_rows(ONE_SCALE * (log_ref[...] - merge(parts_ref[...])), col_ref)
    log_sums(p_ref, q_ref, col_ref, z_ref, row_ref)
    out_ref[...] = jnp.broadcast_to(row_ref[...][None], out_ref.shape)


def last_kernel(
    parts_ref, log_ref, p_ref, q_ref, feat_ref,
    sent_ref, keep_ref, own_ref, bias_ref, flip_ref, col_ref, even_ref, odd_ref,
):
    core = lax.rem(lax.axis_index("tgt"), 2)
    chips, _, share, depth = q_ref.shape
    half = chips * share
    width = feat_ref.shape[1]
    blocks = WIDTH // share
    bias = log_ref[...] - merge(parts_ref[...])
    bias_ref[...] = bias
    lanes_to_rows(ONE_SCALE * bias, col_ref)
    flip_ref[...] = feat_ref[...].astype(jnp.float32).T.astype(jnp.bfloat16)
    sent_ref[pl.ds(width, 8), :] = jnp.zeros((8, half), jnp.float32)
    own_ref[...] = jnp.zeros((8, half), jnp.float32)

    def chunk(t):
        own, first = divmod(t * WIDTH, half)
        q = q_ref[pl.ds(first // share, blocks), core if own else 1 - core]
        return q.reshape(WIDTH, depth)

    def emit(t, tops, totals, weights):
        own, first = divmod(t * WIDTH, half)
        slabs = [
            jnp.concatenate([weight.astype(jnp.bfloat16) for weight in slab], axis=1)
            for slab in weights
        ]
        lanes = pl.ds(first, WIDTH)
        lse = jnp.concatenate([log_sum(*pair) for pair in zip(tops, totals)], axis=1)
        scale = 1.0 / jnp.concatenate(totals, axis=1)
        sent_ref[pl.ds(width + own, 1), lanes] = lse
        own_ref[pl.ds(own, 1), lanes] = lse
        if own:
            for s, slab in enumerate(slabs):
                keep_ref[pl.ds(s * SLAB, SLAB), lanes] = slab
            own_ref[pl.ds(2, 1), lanes] = scale
        else:
            weight = jnp.concatenate(slabs, axis=0)
            numer = lax.dot_general(
                flip_ref[...], weight, NN, preferred_element_type=jnp.float32
            )
            sent_ref[pl.ds(0, width), lanes] = numer * scale

    run_chunks(p_ref, chunk, 2 * half // WIDTH, col_ref, (even_ref, odd_ref), emit)


def squares(ref, k):
    rows = ref[pl.ds(k * LANES, LANES), :].astype(jnp.float32)
    norms = jnp.sum(rows * rows, axis=1, keepdims=True)
    return jnp.broadcast_to(norms, (LANES, LANES)).T[:1, :]


def own_kernel(
    keep_ref, own_ref, flip_ref, bias_ref, p_ref, q_ref, log_ref, mean_ref, pot_ref, base_ref
):
    numer = lax.dot_general(
        flip_ref[...], keep_ref[...], NN, preferred_element_type=jnp.float32
    )
    mean_ref[...] = numer * own_ref[pl.ds(2, 1), :]
    for k in range(pot_ref.shape[0]):
        row = pl.ds(k, 1)
        pot_ref[row, :] = bias_ref[row, :] + squares(p_ref, k)
    for k in range(base_ref.shape[0]):
        row = pl.ds(k, 1)
        base_ref[row, :] = log_ref[row, :] + squares(q_ref, k)


def pair_kernel(order, mean_ref, own_ref, came_ref, out_ref, row_ref):
    width, half = mean_ref.shape
    chips = out_ref.shape[0]
    share = half // chips
    rows = half // LANES
    for side in range(2):
        mine = own_ref[pl.ds(1 - side, 1), :]
        other = came_ref[pl.ds(width + side, 1), :]
        top = jnp.maximum(mine, other)
        mine_share = jnp.exp2((mine - top) * ONE_SCALE)
        other_share = jnp.exp2((other - top) * ONE_SCALE)
        total = mine_share + other_share
        lse = top + ENTROPY * jnp.log(total)
        for k in range(rows):
            row_ref[pl.ds(side * rows + k, 1), :] = lse[:, k * LANES : (k + 1) * LANES]
        if side == 0:
            scale = 1.0 / total
            mine_share, other_share = mine_share * scale, other_share * scale
            step = LANES // share
            for k in range(rows):
                lanes = slice(k * LANES, (k + 1) * LANES)
                block = (
                    mean_ref[:, lanes] * mine_share[:, lanes]
                    + came_ref[pl.ds(0, width), lanes] * other_share[:, lanes]
                )
                block = block.T.reshape(step, share, LANES)
                for place in range(step):
                    out_ref[order.index(k * step + place), pl.ds(0, share), :] = block[place]
    out_ref[:, pl.ds(share, 2 * rows), :] = jnp.broadcast_to(
        row_ref[...][None], (chips, 2 * rows, LANES)
    )


def final_kernel(landed_ref, base_ref, pot_ref, out_ref):
    index = lax.axis_index("tgt")
    core, chip = lax.rem(index, 2), lax.div(index, 2)
    share = out_ref.shape[0]
    chips = landed_ref.shape[0]
    mine = landed_ref[:, pl.ds(share + lax.div(chip, 2), 1), :].reshape(chips, LANES)
    mine = jnp.exp2((mine - jnp.max(mine, axis=0, keepdims=True)) * ONE_SCALE)
    mine = mine / jnp.sum(mine, axis=0, keepdims=True)
    mine = jnp.where(lax.rem(chip, 2) == 0, mine, pltpu.roll(mine, share, 1))
    mine = jnp.concatenate([mine, jnp.zeros((LANES - chips, LANES), jnp.float32)], axis=0).T
    total = jnp.zeros(out_ref.shape, jnp.float32)
    for b in range(chips):
        scale = jnp.broadcast_to(mine[:share, b : b + 1], out_ref.shape)
        total = total + landed_ref[b, pl.ds(0, share), :] * scale
    out_ref[...] = total
    whole = merge(landed_ref[:, pl.ds(share, landed_ref.shape[1] - share), :])
    rows = whole.shape[0] // 2
    even = jnp.where(core == 0, whole[:rows], whole[rows:])
    odd = jnp.where(core == 0, whole[rows:], whole[:rows])
    lane = lax.broadcasted_iota(jnp.int32, (rows, LANES), 1)
    first = jnp.where(lane < share, even, pltpu.roll(odd, share, 1))
    second = jnp.where(lane < share, pltpu.roll(even, share, 1), odd)
    for k in range(rows):
        for side, values in enumerate((first, second)):
            row = pl.ds(2 * k + side, 1)
            pot_ref[row, :] = base_ref[row, :] - values[k : k + 1]


def rotated(n, first, stride=1):
    return [(first + stride * place) % n for place in range(n)]


def near_first(chips, far_chip):
    side = math.isqrt(chips)

    def distance(chip):
        return sum(min(place, side - place) for place in divmod(chip, side))

    return [far_chip] + sorted(set(range(chips)) - {far_chip}, key=distance)


def scratch(p, q):
    return [
        pltpu.VMEM((p.shape[0], LANES), jnp.float32),
        pltpu.VMEM((p.shape[0], WIDTH), jnp.float32),
        pltpu.VMEM((q.shape[0] // LANES, LANES), jnp.float32),
    ]


def call(kernel, args, outs, scratch_shapes, spaces=None):
    whole = pl.BlockSpec(memory_space=pltpu.VMEM)
    return pl.pallas_call(
        kernel,
        out_shape=outs,
        in_specs=spaces or [whole] * len(args),
        out_specs=jax.tree.map(lambda _: whole, outs),
        scratch_shapes=scratch_shapes,
        compiler_params=pltpu.CompilerParams(vmem_limit_bytes=VMEM_LIMIT),
    )(*args)


def local(source_embed, target_embed, target_feat, source_mass, target_mass):
    f32 = jnp.float32
    shape = jax.ShapeDtypeStruct
    n_src, n_tgt = lax.axis_size("src"), lax.axis_size("tgt")
    rows, depth = source_embed.shape
    width = target_feat.shape[1]
    share, half, chips = rows // n_tgt, rows // 2, n_tgt // 2
    src_mass = source_mass.reshape(-1, LANES)
    tgt_mass = target_mass.reshape(-1, LANES)
    src_rows, tgt_rows = src_mass.shape[0], tgt_mass.shape[0]
    to_src = shape((n_src, tgt_rows, LANES), f32)
    to_tgt = shape((n_tgt, src_rows, LANES), f32)
    by_src = scratch(source_embed, target_embed)
    by_tgt = scratch(target_embed, source_embed)
    far_chip = chips // 2 + math.isqrt(chips) // 2
    order = near_first(chips, far_chip)
    same_core = [[2 * chip + core for chip in order] for core in range(2)]
    swap = [(index, index ^ 1) for index in range(n_tgt)]

    sems = [pltpu.SemaphoreType.DMA((rows // SLAB,)), pltpu.SemaphoreType.DMA((3,))]
    inputs = [
        pltpu.with_memory_space_constraint(array, pltpu.HBM)
        for array in (source_embed, target_embed, src_mass, tgt_mass)
    ]
    held = [shape(array.shape, array.dtype) for array in inputs]
    sent, source_embed, target_embed, src_log, tgt_log = call(
        first_kernel,
        inputs,
        (to_src, *held),
        sems + by_src,
        [pl.BlockSpec(memory_space=pltpu.HBM)] * len(inputs),
    )
    parts = lax.all_to_all(sent, "src", 0, 0, axis_index_groups=[rotated(n_src, n_src // 2)])
    sent = call(next_kernel, (parts, tgt_log, target_embed, source_embed), to_tgt, by_tgt)
    parts = lax.all_to_all(sent, "tgt", 0, 0, axis_index_groups=[rotated(n_tgt, 2 * far_chip + 1)])
    sent = call(next_kernel, (parts, src_log, source_embed, target_embed), to_src, by_src)
    parts = lax.all_to_all(sent, "src", 0, 0, axis_index_groups=[rotated(n_src, n_src // 2, n_src // 2 - 1)])
    sent, keep, own, bias, turned = call(
        last_kernel,
        (parts, tgt_log, target_embed, source_embed.reshape(chips, 2, share, depth), target_feat),
        (
            shape((width + 8, half), f32),
            shape((target_embed.shape[0], half), jnp.bfloat16),
            shape((8, half), f32),
            shape((tgt_rows, LANES), f32),
            shape(target_feat.shape[::-1], jnp.bfloat16),
        ),
        by_tgt[:2] + by_tgt[1:2],
    )
    came = lax.ppermute(sent, "tgt", swap)
    mean, target_pot, base = call(
        own_kernel,
        (keep, own, turned, bias, target_embed, source_embed, src_log),
        (shape((width, half), f32), shape(bias.shape, f32), shape(src_log.shape, f32)),
        [],
    )
    sent = call(
        functools.partial(pair_kernel, order),
        (mean, own, came),
        shape((chips, share + src_rows, LANES), f32),
        [pltpu.VMEM((src_rows, LANES), f32)],
    )
    landed = lax.all_to_all(sent, "tgt", 0, 0, axis_index_groups=same_core)
    source_pot, projected = call(
        final_kernel,
        (landed, base),
        (shape((src_rows, LANES), f32), shape((share, width), f32)),
        [],
    )
    return (source_pot.reshape(-1), target_pot.reshape(-1), projected)


def solution(mesh):
    placed = (P("src", None), P("tgt", None), P("tgt", None), P("src"), P("tgt"))
    return jax.shard_map(
        local,
        mesh=mesh,
        in_specs=placed,
        out_specs=(P("src"), P("tgt"), P(("src", "tgt"), None)),
        check_vma=False,
    )
```

```python
import functools
import math

import jax
import jax.numpy as jnp
from jax import lax
from jax.experimental import pallas as pl
from jax.experimental.pallas import tpu as pltpu
from jax.sharding import PartitionSpec as P

ENTROPY = 0.05
LANES = 128
WIDTH = 256
ONE_SCALE = 1.0 / ENTROPY * math.log2(math.e)
TWO_SCALE = 2.0 * ONE_SCALE
ONE_UNIT = ENTROPY * math.log(2.0)
LOWEST, HIGHEST = 2.0**-90, 2.0**110
NT = (((1,), (1,)), ((), ()))
NN = (((1,), (0,)), ((), ()))
HALVES = WIDTH // LANES
SLAB = 512
ACCUMULATE = 32
VMEM_LIMIT = 40 * 1024 * 1024


def merge(parts):
    top = jnp.max(parts, axis=0)
    total = jnp.sum(jnp.exp2((parts - top[None]) * ONE_SCALE), axis=0)
    return top + ENTROPY * jnp.log(total)


def lanes_to_rows(values, col_ref):
    for k in range(values.shape[0]):
        square = jnp.broadcast_to(values[k : k + 1, :], (LANES, LANES))
        col_ref[pl.ds(k * LANES, LANES), :] = square.T


def fold(reduce, part):
    return reduce(part.reshape(-1, ACCUMULATE, LANES), axis=0)


def exponents(p_ref, q, col_ref, s, rows=SLAB):
    slab = pl.ds(s * rows, rows)
    cross = lax.dot_general(p_ref[slab, :], q, NT, preferred_element_type=jnp.float32)
    col = col_ref[slab, :]
    return [cross[:, h * LANES : (h + 1) * LANES] * TWO_SCALE + col for h in range(HALVES)]


def scores(p_ref, q, col_ref, z_ref, s, rows=SLAB):
    slab = pl.ds(s * rows, rows)
    tops = []
    for h, part in enumerate(exponents(p_ref, q, col_ref, s, rows)):
        z_ref[slab, pl.ds(h * LANES, LANES)] = part
        tops.append(fold(jnp.max, part))
    return tops


def weigh(z_ref, tops, s, rows=SLAB):
    slab = pl.ds(s * rows, rows)
    weights, totals = [], []
    for h, top in enumerate(tops):
        part = z_ref[slab, pl.ds(h * LANES, LANES)]
        weight = jnp.exp2(part - top)
        weights.append(weight)
        totals.append(fold(jnp.sum, weight))
    return weights, totals


def join(op, held, more):
    return more if held is None else [op(a, b) for a, b in zip(held, more)]


def settle(reduce, values):
    return [reduce(value, axis=0, keepdims=True) for value in values]


def log_sum(top, total):
    return ONE_UNIT * top + ENTROPY * jnp.log(total)


def run_chunks(p_ref, chunk, chunks, col_ref, z_refs, emit, rows=2 * SLAB):
    slabs = p_ref.shape[0] // rows
    tops = None
    for t in range(chunks + 1):
        q = chunk(t) if t < chunks else None
        later, totals, weights = None, None, []
        for s in range(slabs):
            if t < chunks:
                later = join(jnp.maximum, later, scores(p_ref, q, col_ref, z_refs[t % 2], s, rows))
            if t > 0:
                weight, total = weigh(z_refs[(t - 1) % 2], tops, s, rows)
                totals = join(jnp.add, totals, total)
                weights.append(weight)
        if t > 0:
            emit(t - 1, tops, settle(jnp.sum, totals), weights)
        if t < chunks:
            tops = settle(jnp.max, later)


def log_sums(p_ref, q_ref, col_ref, z_ref, row_ref, rows=2 * SLAB):
    slabs, chunks = p_ref.shape[0] // SLAB, q_ref.shape[0] // WIDTH
    totals = [None] * chunks
    for s in range(p_ref.shape[0] // rows):
        for t in range(chunks):
            parts = exponents(p_ref, q_ref[pl.ds(t * WIDTH, WIDTH), :], col_ref, s, rows)
            totals[t] = join(jnp.add, totals[t], [fold(jnp.sum, jnp.exp2(part)) for part in parts])
    for t in range(chunks):
        for h, total in enumerate(settle(jnp.sum, totals[t])):
            row_ref[pl.ds(t * HALVES + h, 1), :] = total
    sums = row_ref[...]
    row_ref[...] = ENTROPY * jnp.log(sums)
    safe = jnp.logical_and(jnp.min(sums) >= LOWEST, jnp.max(sums) <= HIGHEST)

    @pl.when(jnp.logical_not(safe))
    def _():
        @pl.loop(0, chunks)
        def _(t):
            q = q_ref[pl.ds(pl.multiple_of(t * WIDTH, WIDTH), WIDTH), :]
            tops, sums = None, None
            for s in range(slabs):
                tops = join(jnp.maximum, tops, scores(p_ref, q, col_ref, z_ref, s))
            tops = settle(jnp.max, tops)
            for s in range(slabs):
                sums = join(jnp.add, sums, weigh(z_ref, tops, s)[1])
            for h, pair in enumerate(zip(tops, settle(jnp.sum, sums))):
                row_ref[pl.ds(t * HALVES + h, 1), :] = log_sum(*pair)


def first_kernel(
    p_hbm, q_hbm, p_mass_hbm, q_mass_hbm, out_ref, p_ref, q_ref, p_log_ref, q_log_ref,
    p_sems, sems, col_ref, z_ref, row_ref,
):
    loads = []
    for s in range(p_ref.shape[0] // SLAB):
        slab = pl.ds(s * SLAB, SLAB)
        loads.append(pltpu.make_async_copy(p_hbm.at[slab, :], p_ref.at[slab, :], p_sems.at[s]))
    load_q = pltpu.make_async_copy(q_hbm, q_ref, sems.at[0])
    masses = [
        pltpu.make_async_copy(p_mass_hbm, p_log_ref, sems.at[1]),
        pltpu.make_async_copy(q_mass_hbm, q_log_ref, sems.at[2]),
    ]
    for copy in loads + [load_q] + masses:
        copy.start()
    for s, copy in enumerate(loads):
        copy.wait()
        slab = pl.ds(s * SLAB, SLAB)
        p = p_ref[slab, :].astype(jnp.float32)
        norms = jnp.sum(p * p, axis=1, keepdims=True)
        col_ref[slab, :] = jnp.broadcast_to(-ONE_SCALE * norms, (SLAB, LANES))
    load_q.wait()
    log_sums(p_ref, q_ref, col_ref, z_ref, row_ref)
    for copy in masses:
        copy.wait()
    p_log_ref[...] = ENTROPY * jnp.log(p_log_ref[...])
    q_log_ref[...] = ENTROPY * jnp.log(q_log_ref[...])
    out_ref[...] = jnp.broadcast_to(row_ref[...][None], out_ref.shape)


def next_kernel(parts_ref, log_ref, p_ref, q_ref, out_ref, col_ref, z_ref, row_ref):
    lanes_to_rows(ONE_SCALE * (log_ref[...] - merge(parts_ref[...])), col_ref)
    log_sums(p_ref, q_ref, col_ref, z_ref, row_ref)
    out_ref[...] = jnp.broadcast_to(row_ref[...][None], out_ref.shape)


def last_kernel(
    parts_ref, log_ref, p_ref, q_ref, feat_ref,
    sent_ref, keep_ref, own_ref, bias_ref, flip_ref, col_ref, even_ref, odd_ref,
):
    core = lax.rem(lax.axis_index("tgt"), 2)
    chips, _, share, depth = q_ref.shape
    half = chips * share
    width = feat_ref.shape[1]
    blocks = WIDTH // share
    bias = log_ref[...] - merge(parts_ref[...])
    bias_ref[...] = bias
    lanes_to_rows(ONE_SCALE * bias, col_ref)
    flip_ref[...] = feat_ref[...].astype(jnp.float32).T.astype(jnp.bfloat16)
    sent_ref[pl.ds(width, 8), :] = jnp.zeros((8, half), jnp.float32)
    own_ref[...] = jnp.zeros((8, half), jnp.float32)

    def chunk(t):
        own, first = divmod(t * WIDTH, half)
        q = q_ref[pl.ds(first // share, blocks), core if own else 1 - core]
        return q.reshape(WIDTH, depth)

    def emit(t, tops, totals, weights):
        own, first = divmod(t * WIDTH, half)
        slabs = [
            jnp.concatenate([weight.astype(jnp.bfloat16) for weight in slab], axis=1)
            for slab in weights
        ]
        lanes = pl.ds(first, WIDTH)
        lse = jnp.concatenate([log_sum(*pair) for pair in zip(tops, totals)], axis=1)
        scale = 1.0 / jnp.concatenate(totals, axis=1)
        sent_ref[pl.ds(width + own, 1), lanes] = lse
        own_ref[pl.ds(own, 1), lanes] = lse
        if own:
            for s, slab in enumerate(slabs):
                keep_ref[pl.ds(s * slab.shape[0], slab.shape[0]), lanes] = slab
            own_ref[pl.ds(2, 1), lanes] = scale
        else:
            weight = jnp.concatenate(slabs, axis=0)
            numer = lax.dot_general(
                flip_ref[...], weight, NN, preferred_element_type=jnp.float32
            )
            sent_ref[pl.ds(0, width), lanes] = numer * scale

    run_chunks(p_ref, chunk, 2 * half // WIDTH, col_ref, (even_ref, odd_ref), emit)


def squares(ref, k):
    rows = ref[pl.ds(k * LANES, LANES), :].astype(jnp.float32)
    norms = jnp.sum(rows * rows, axis=1, keepdims=True)
    return jnp.broadcast_to(norms, (LANES, LANES)).T[:1, :]


def own_kernel(
    keep_ref, own_ref, flip_ref, bias_ref, p_ref, q_ref, log_ref, mean_ref, pot_ref, base_ref
):
    numer = lax.dot_general(
        flip_ref[...], keep_ref[...], NN, preferred_element_type=jnp.float32
    )
    mean_ref[...] = numer * own_ref[pl.ds(2, 1), :]
    for k in range(pot_ref.shape[0]):
        row = pl.ds(k, 1)
        pot_ref[row, :] = bias_ref[row, :] + squares(p_ref, k)
    for k in range(base_ref.shape[0]):
        row = pl.ds(k, 1)
        base_ref[row, :] = log_ref[row, :] + squares(q_ref, k)


def pair_kernel(far_chip, mean_ref, own_ref, came_ref, out_ref, row_ref):
    width, half = mean_ref.shape
    chips = out_ref.shape[0]
    share = half // chips
    rows = half // LANES
    for side in range(2):
        mine = own_ref[pl.ds(1 - side, 1), :]
        other = came_ref[pl.ds(width + side, 1), :]
        top = jnp.maximum(mine, other)
        mine_share = jnp.exp2((mine - top) * ONE_SCALE)
        other_share = jnp.exp2((other - top) * ONE_SCALE)
        total = mine_share + other_share
        lse = top + ENTROPY * jnp.log(total)
        for k in range(rows):
            row_ref[pl.ds(side * rows + k, 1), :] = lse[:, k * LANES : (k + 1) * LANES]
        if side == 0:
            scale = 1.0 / total
            mine_share, other_share = mine_share * scale, other_share * scale
            step = LANES // share
            for k in range(rows):
                lanes = slice(k * LANES, (k + 1) * LANES)
                block = (
                    mean_ref[:, lanes] * mine_share[:, lanes]
                    + came_ref[pl.ds(0, width), lanes] * other_share[:, lanes]
                )
                place = (k * step - far_chip) % chips
                out_ref[pl.ds(place, step), pl.ds(0, share), :] = block.T.reshape(
                    step, share, LANES
                )
    out_ref[:, pl.ds(share, 2 * rows), :] = jnp.broadcast_to(
        row_ref[...][None], (chips, 2 * rows, LANES)
    )


def final_kernel(landed_ref, base_ref, pot_ref, out_ref):
    index = lax.axis_index("tgt")
    core, chip = lax.rem(index, 2), lax.div(index, 2)
    share = out_ref.shape[0]
    chips = landed_ref.shape[0]
    mine = landed_ref[:, pl.ds(share + lax.div(chip, 2), 1), :].reshape(chips, LANES)
    mine = jnp.exp2((mine - jnp.max(mine, axis=0, keepdims=True)) * ONE_SCALE)
    mine = mine / jnp.sum(mine, axis=0, keepdims=True)
    mine = jnp.where(lax.rem(chip, 2) == 0, mine, pltpu.roll(mine, share, 1))
    mine = jnp.concatenate([mine, jnp.zeros((LANES - chips, LANES), jnp.float32)], axis=0).T
    total = jnp.zeros(out_ref.shape, jnp.float32)
    for b in range(chips):
        scale = jnp.broadcast_to(mine[:share, b : b + 1], out_ref.shape)
        total = total + landed_ref[b, pl.ds(0, share), :] * scale
    out_ref[...] = total
    whole = merge(landed_ref[:, pl.ds(share, landed_ref.shape[1] - share), :])
    rows = whole.shape[0] // 2
    even = jnp.where(core == 0, whole[:rows], whole[rows:])
    odd = jnp.where(core == 0, whole[rows:], whole[:rows])
    lane = lax.broadcasted_iota(jnp.int32, (rows, LANES), 1)
    first = jnp.where(lane < share, even, pltpu.roll(odd, share, 1))
    second = jnp.where(lane < share, pltpu.roll(even, share, 1), odd)
    for k in range(rows):
        for side, values in enumerate((first, second)):
            row = pl.ds(2 * k + side, 1)
            pot_ref[row, :] = base_ref[row, :] - values[k : k + 1]


def rotated(n, first):
    return [(first + place) % n for place in range(n)]


def near_first(n):
    return [n // 2] + sorted(set(range(n)) - {n // 2}, key=lambda place: min(place, n - place))


def scratch(p, q):
    return [
        pltpu.VMEM((p.shape[0], LANES), jnp.float32),
        pltpu.VMEM((p.shape[0], WIDTH), jnp.float32),
        pltpu.VMEM((q.shape[0] // LANES, LANES), jnp.float32),
    ]


def call(kernel, args, outs, scratch_shapes, spaces=None):
    whole = pl.BlockSpec(memory_space=pltpu.VMEM)
    return pl.pallas_call(
        kernel,
        out_shape=outs,
        in_specs=spaces or [whole] * len(args),
        out_specs=jax.tree.map(lambda _: whole, outs),
        scratch_shapes=scratch_shapes,
        compiler_params=pltpu.CompilerParams(vmem_limit_bytes=VMEM_LIMIT),
    )(*args)


def local(source_embed, target_embed, target_feat, source_mass, target_mass):
    f32 = jnp.float32
    shape = jax.ShapeDtypeStruct
    n_src, n_tgt = lax.axis_size("src"), lax.axis_size("tgt")
    rows, depth = source_embed.shape
    width = target_feat.shape[1]
    share, half, chips = rows // n_tgt, rows // 2, n_tgt // 2
    src_mass = source_mass.reshape(-1, LANES)
    tgt_mass = target_mass.reshape(-1, LANES)
    src_rows, tgt_rows = src_mass.shape[0], tgt_mass.shape[0]
    to_src = shape((n_src, tgt_rows, LANES), f32)
    to_tgt = shape((n_tgt, src_rows, LANES), f32)
    by_src = scratch(source_embed, target_embed)
    by_tgt = scratch(target_embed, source_embed)
    far_chip = chips // 2 + math.isqrt(chips) // 2
    same_core = [[2 * chip + core for chip in rotated(chips, far_chip)] for core in range(2)]
    swap = [(index, index ^ 1) for index in range(n_tgt)]

    sems = [pltpu.SemaphoreType.DMA((rows // SLAB,)), pltpu.SemaphoreType.DMA((3,))]
    inputs = [
        pltpu.with_memory_space_constraint(array, pltpu.HBM)
        for array in (source_embed, target_embed, src_mass, tgt_mass)
    ]
    held = [shape(array.shape, array.dtype) for array in inputs]
    sent, source_embed, target_embed, src_log, tgt_log = call(
        first_kernel,
        inputs,
        (to_src, *held),
        sems + by_src,
        [pl.BlockSpec(memory_space=pltpu.HBM)] * len(inputs),
    )
    parts = lax.all_to_all(sent, "src", 0, 0, axis_index_groups=[rotated(n_src, n_src // 2)])
    sent = call(next_kernel, (parts, tgt_log, target_embed, source_embed), to_tgt, by_tgt)
    parts = lax.all_to_all(sent, "tgt", 0, 0, axis_index_groups=[rotated(n_tgt, 2 * far_chip + 1)])
    sent = call(next_kernel, (parts, src_log, source_embed, target_embed), to_src, by_src)
    parts = lax.all_to_all(sent, "src", 0, 0, axis_index_groups=[near_first(n_src)])
    sent, keep, own, bias, turned = call(
        last_kernel,
        (parts, tgt_log, target_embed, source_embed.reshape(chips, 2, share, depth), target_feat),
        (
            shape((width + 8, half), f32),
            shape((target_embed.shape[0], half), jnp.bfloat16),
            shape((8, half), f32),
            shape((tgt_rows, LANES), f32),
            shape(target_feat.shape[::-1], jnp.bfloat16),
        ),
        by_tgt[:2] + by_tgt[1:2],
    )
    came = lax.ppermute(sent, "tgt", swap)
    mean, target_pot, base = call(
        own_kernel,
        (keep, own, turned, bias, target_embed, source_embed, src_log),
        (shape((width, half), f32), shape(bias.shape, f32), shape(src_log.shape, f32)),
        [],
    )
    sent = call(
        functools.partial(pair_kernel, far_chip),
        (mean, own, came),
        shape((chips, share + src_rows, LANES), f32),
        [pltpu.VMEM((src_rows, LANES), f32)],
    )
    landed = lax.all_to_all(sent, "tgt", 0, 0, axis_index_groups=same_core)
    source_pot, projected = call(
        final_kernel,
        (landed, base),
        (shape((src_rows, LANES), f32), shape((share, width), f32)),
        [],
    )
    return (source_pot.reshape(-1), target_pot.reshape(-1), projected)


def solution(mesh):
    placed = (P("src", None), P("tgt", None), P("tgt", None), P("src"), P("tgt"))
    return jax.shard_map(
        local,
        mesh=mesh,
        in_specs=placed,
        out_specs=(P("src"), P("tgt"), P(("src", "tgt"), None)),
        check_vma=False,
    )
```

```python
import functools
import math

import jax
import jax.numpy as jnp
from jax import lax
from jax.experimental import pallas as pl
from jax.experimental.pallas import tpu as pltpu
from jax.sharding import PartitionSpec as P

ENTROPY = 0.05
LANES = 128
WIDTH = 256
ONE_SCALE = 1.0 / ENTROPY * math.log2(math.e)
TWO_SCALE = 2.0 * ONE_SCALE
ONE_UNIT = ENTROPY * math.log(2.0)
LOWEST, HIGHEST = 2.0**-90, 2.0**110
NT = (((1,), (1,)), ((), ()))
NN = (((1,), (0,)), ((), ()))
HALVES = WIDTH // LANES
SLAB = 512
ACCUMULATE = 32
VMEM_LIMIT = 40 * 1024 * 1024


def merge(parts):
    top = jnp.max(parts, axis=0)
    total = jnp.sum(jnp.exp2((parts - top[None]) * ONE_SCALE), axis=0)
    return top + ENTROPY * jnp.log(total)


def lanes_to_rows(values, col_ref):
    for k in range(values.shape[0]):
        square = jnp.broadcast_to(values[k : k + 1, :], (LANES, LANES))
        col_ref[pl.ds(k * LANES, LANES), :] = square.T


def fold(reduce, part):
    return reduce(part.reshape(-1, ACCUMULATE, LANES), axis=0)


def exponents(p_ref, q, col_ref, s, rows=SLAB):
    slab = pl.ds(s * rows, rows)
    cross = lax.dot_general(p_ref[slab, :], q, NT, preferred_element_type=jnp.float32)
    col = col_ref[slab, :]
    return [cross[:, h * LANES : (h + 1) * LANES] * TWO_SCALE + col for h in range(HALVES)]


def scores(p_ref, q, col_ref, z_ref, s, rows=SLAB):
    slab = pl.ds(s * rows, rows)
    tops = []
    for h, part in enumerate(exponents(p_ref, q, col_ref, s, rows)):
        z_ref[slab, pl.ds(h * LANES, LANES)] = part
        tops.append(fold(jnp.max, part))
    return tops


def weigh(z_ref, tops, s, rows=SLAB):
    slab = pl.ds(s * rows, rows)
    weights, totals = [], []
    for h, top in enumerate(tops):
        part = z_ref[slab, pl.ds(h * LANES, LANES)]
        weight = jnp.exp2(part - top)
        weights.append(weight)
        totals.append(fold(jnp.sum, weight))
    return weights, totals


def join(op, held, more):
    return more if held is None else [op(a, b) for a, b in zip(held, more)]


def settle(reduce, values):
    return [reduce(value, axis=0, keepdims=True) for value in values]


def log_sum(top, total):
    return ONE_UNIT * top + ENTROPY * jnp.log(total)


def run_chunks(p_ref, chunk, chunks, col_ref, z_refs, emit, rows=SLAB):
    slabs = p_ref.shape[0] // rows
    tops = None
    for t in range(chunks + 1):
        q = chunk(t) if t < chunks else None
        later, totals, weights = None, None, []
        for s in range(slabs):
            if t < chunks:
                later = join(jnp.maximum, later, scores(p_ref, q, col_ref, z_refs[t % 2], s, rows))
            if t > 0:
                weight, total = weigh(z_refs[(t - 1) % 2], tops, s, rows)
                totals = join(jnp.add, totals, total)
                weights.append(weight)
        if t > 0:
            emit(t - 1, tops, settle(jnp.sum, totals), weights)
        if t < chunks:
            tops = settle(jnp.max, later)


def log_sums(p_ref, q_ref, col_ref, z_ref, row_ref, rows=2 * SLAB):
    slabs, chunks = p_ref.shape[0] // SLAB, q_ref.shape[0] // WIDTH
    totals = [None] * chunks
    for s in range(p_ref.shape[0] // rows):
        for t in range(chunks):
            parts = exponents(p_ref, q_ref[pl.ds(t * WIDTH, WIDTH), :], col_ref, s, rows)
            totals[t] = join(jnp.add, totals[t], [fold(jnp.sum, jnp.exp2(part)) for part in parts])
    for t in range(chunks):
        for h, total in enumerate(settle(jnp.sum, totals[t])):
            row_ref[pl.ds(t * HALVES + h, 1), :] = total
    sums = row_ref[...]
    row_ref[...] = ENTROPY * jnp.log(sums)
    safe = jnp.logical_and(jnp.min(sums) >= LOWEST, jnp.max(sums) <= HIGHEST)

    @pl.when(jnp.logical_not(safe))
    def _():
        @pl.loop(0, chunks)
        def _(t):
            q = q_ref[pl.ds(pl.multiple_of(t * WIDTH, WIDTH), WIDTH), :]
            tops, sums = None, None
            for s in range(slabs):
                tops = join(jnp.maximum, tops, scores(p_ref, q, col_ref, z_ref, s))
            tops = settle(jnp.max, tops)
            for s in range(slabs):
                sums = join(jnp.add, sums, weigh(z_ref, tops, s)[1])
            for h, pair in enumerate(zip(tops, settle(jnp.sum, sums))):
                row_ref[pl.ds(t * HALVES + h, 1), :] = log_sum(*pair)


def first_kernel(
    p_hbm, q_hbm, p_mass_hbm, q_mass_hbm, out_ref, p_ref, q_ref, p_log_ref, q_log_ref,
    p_sems, sems, col_ref, z_ref, row_ref,
):
    loads = []
    for s in range(p_ref.shape[0] // SLAB):
        slab = pl.ds(s * SLAB, SLAB)
        loads.append(pltpu.make_async_copy(p_hbm.at[slab, :], p_ref.at[slab, :], p_sems.at[s]))
    load_q = pltpu.make_async_copy(q_hbm, q_ref, sems.at[0])
    masses = [
        pltpu.make_async_copy(p_mass_hbm, p_log_ref, sems.at[1]),
        pltpu.make_async_copy(q_mass_hbm, q_log_ref, sems.at[2]),
    ]
    for copy in loads + [load_q] + masses:
        copy.start()
    for s, copy in enumerate(loads):
        copy.wait()
        slab = pl.ds(s * SLAB, SLAB)
        p = p_ref[slab, :].astype(jnp.float32)
        norms = jnp.sum(p * p, axis=1, keepdims=True)
        col_ref[slab, :] = jnp.broadcast_to(-ONE_SCALE * norms, (SLAB, LANES))
    load_q.wait()
    log_sums(p_ref, q_ref, col_ref, z_ref, row_ref)
    for copy in masses:
        copy.wait()
    p_log_ref[...] = ENTROPY * jnp.log(p_log_ref[...])
    q_log_ref[...] = ENTROPY * jnp.log(q_log_ref[...])
    out_ref[...] = jnp.broadcast_to(row_ref[...][None], out_ref.shape)


def next_kernel(parts_ref, log_ref, p_ref, q_ref, out_ref, col_ref, z_ref, row_ref):
    lanes_to_rows(ONE_SCALE * (log_ref[...] - merge(parts_ref[...])), col_ref)
    log_sums(p_ref, q_ref, col_ref, z_ref, row_ref)
    out_ref[...] = jnp.broadcast_to(row_ref[...][None], out_ref.shape)


def last_kernel(
    parts_ref, log_ref, p_ref, q_ref, feat_ref,
    sent_ref, keep_ref, own_ref, bias_ref, flip_ref, col_ref, even_ref, odd_ref,
):
    core = lax.rem(lax.axis_index("tgt"), 2)
    chips, _, share, depth = q_ref.shape
    half = chips * share
    width = feat_ref.shape[1]
    blocks = WIDTH // share
    bias = log_ref[...] - merge(parts_ref[...])
    bias_ref[...] = bias
    lanes_to_rows(ONE_SCALE * bias, col_ref)
    flip_ref[...] = feat_ref[...].astype(jnp.float32).T.astype(jnp.bfloat16)
    sent_ref[pl.ds(width, 8), :] = jnp.zeros((8, half), jnp.float32)
    own_ref[...] = jnp.zeros((8, half), jnp.float32)

    def chunk(t):
        own, first = divmod(t * WIDTH, half)
        q = q_ref[pl.ds(first // share, blocks), core if own else 1 - core]
        return q.reshape(WIDTH, depth)

    def emit(t, tops, totals, weights):
        own, first = divmod(t * WIDTH, half)
        slabs = [
            jnp.concatenate([weight.astype(jnp.bfloat16) for weight in slab], axis=1)
            for slab in weights
        ]
        lanes = pl.ds(first, WIDTH)
        lse = jnp.concatenate([log_sum(*pair) for pair in zip(tops, totals)], axis=1)
        scale = 1.0 / jnp.concatenate(totals, axis=1)
        sent_ref[pl.ds(width + own, 1), lanes] = lse
        own_ref[pl.ds(own, 1), lanes] = lse
        if own:
            for s, slab in enumerate(slabs):
                keep_ref[pl.ds(s * slab.shape[0], slab.shape[0]), lanes] = slab
            own_ref[pl.ds(2, 1), lanes] = scale
        else:
            weight = jnp.concatenate(slabs, axis=0)
            numer = lax.dot_general(
                flip_ref[...], weight, NN, preferred_element_type=jnp.float32
            )
            sent_ref[pl.ds(0, width), lanes] = numer * scale

    run_chunks(p_ref, chunk, 2 * half // WIDTH, col_ref, (even_ref, odd_ref), emit)


def squares(ref, k):
    rows = ref[pl.ds(k * LANES, LANES), :].astype(jnp.float32)
    norms = jnp.sum(rows * rows, axis=1, keepdims=True)
    return jnp.broadcast_to(norms, (LANES, LANES)).T[:1, :]


def own_kernel(
    keep_ref, own_ref, flip_ref, bias_ref, p_ref, q_ref, log_ref, mean_ref, pot_ref, base_ref
):
    numer = lax.dot_general(
        flip_ref[...], keep_ref[...], NN, preferred_element_type=jnp.float32
    )
    mean_ref[...] = numer * own_ref[pl.ds(2, 1), :]
    for k in range(pot_ref.shape[0]):
        row = pl.ds(k, 1)
        pot_ref[row, :] = bias_ref[row, :] + squares(p_ref, k)
    for k in range(base_ref.shape[0]):
        row = pl.ds(k, 1)
        base_ref[row, :] = log_ref[row, :] + squares(q_ref, k)


def pair_kernel(far_chip, mean_ref, own_ref, came_ref, out_ref, row_ref):
    width, half = mean_ref.shape
    chips = out_ref.shape[0]
    share = half // chips
    rows = half // LANES
    for side in range(2):
        mine = own_ref[pl.ds(1 - side, 1), :]
        other = came_ref[pl.ds(width + side, 1), :]
        top = jnp.maximum(mine, other)
        mine_share = jnp.exp2((mine - top) * ONE_SCALE)
        other_share = jnp.exp2((other - top) * ONE_SCALE)
        total = mine_share + other_share
        lse = top + ENTROPY * jnp.log(total)
        for k in range(rows):
            row_ref[pl.ds(side * rows + k, 1), :] = lse[:, k * LANES : (k + 1) * LANES]
        if side == 0:
            scale = 1.0 / total
            mine_share, other_share = mine_share * scale, other_share * scale
            step = LANES // share
            for k in range(rows):
                lanes = slice(k * LANES, (k + 1) * LANES)
                block = (
                    mean_ref[:, lanes] * mine_share[:, lanes]
                    + came_ref[pl.ds(0, width), lanes] * other_share[:, lanes]
                )
                place = (k * step - far_chip) % chips
                out_ref[pl.ds(place, step), pl.ds(0, share), :] = block.T.reshape(
                    step, share, LANES
                )
    out_ref[:, pl.ds(share, 2 * rows), :] = jnp.broadcast_to(
        row_ref[...][None], (chips, 2 * rows, LANES)
    )


def final_kernel(landed_ref, base_ref, pot_ref, out_ref):
    index = lax.axis_index("tgt")
    core, chip = lax.rem(index, 2), lax.div(index, 2)
    share = out_ref.shape[0]
    chips = landed_ref.shape[0]
    mine = landed_ref[:, pl.ds(share + lax.div(chip, 2), 1), :].reshape(chips, LANES)
    mine = jnp.exp2((mine - jnp.max(mine, axis=0, keepdims=True)) * ONE_SCALE)
    mine = mine / jnp.sum(mine, axis=0, keepdims=True)
    mine = jnp.where(lax.rem(chip, 2) == 0, mine, pltpu.roll(mine, share, 1))
    mine = jnp.concatenate([mine, jnp.zeros((LANES - chips, LANES), jnp.float32)], axis=0).T
    total = jnp.zeros(out_ref.shape, jnp.float32)
    for b in range(chips):
        scale = jnp.broadcast_to(mine[:share, b : b + 1], out_ref.shape)
        total = total + landed_ref[b, pl.ds(0, share), :] * scale
    out_ref[...] = total
    whole = merge(landed_ref[:, pl.ds(share, landed_ref.shape[1] - share), :])
    rows = whole.shape[0] // 2
    even = jnp.where(core == 0, whole[:rows], whole[rows:])
    odd = jnp.where(core == 0, whole[rows:], whole[:rows])
    lane = lax.broadcasted_iota(jnp.int32, (rows, LANES), 1)
    first = jnp.where(lane < share, even, pltpu.roll(odd, share, 1))
    second = jnp.where(lane < share, pltpu.roll(even, share, 1), odd)
    for k in range(rows):
        for side, values in enumerate((first, second)):
            row = pl.ds(2 * k + side, 1)
            pot_ref[row, :] = base_ref[row, :] - values[k : k + 1]


def rotated(n, first):
    return [(first + place) % n for place in range(n)]


def by_distance(n, place):
    far = n // 2
    return [far] + sorted(
        set(range(n)) - {far}, key=lambda other: min((other - place) % n, (place - other) % n)
    )


def scratch(p, q):
    return [
        pltpu.VMEM((p.shape[0], LANES), jnp.float32),
        pltpu.VMEM((p.shape[0], WIDTH), jnp.float32),
        pltpu.VMEM((q.shape[0] // LANES, LANES), jnp.float32),
    ]


def call(kernel, args, outs, scratch_shapes, spaces=None):
    whole = pl.BlockSpec(memory_space=pltpu.VMEM)
    return pl.pallas_call(
        kernel,
        out_shape=outs,
        in_specs=spaces or [whole] * len(args),
        out_specs=jax.tree.map(lambda _: whole, outs),
        scratch_shapes=scratch_shapes,
        compiler_params=pltpu.CompilerParams(vmem_limit_bytes=VMEM_LIMIT),
    )(*args)


def local(source_embed, target_embed, target_feat, source_mass, target_mass):
    f32 = jnp.float32
    shape = jax.ShapeDtypeStruct
    n_src, n_tgt = lax.axis_size("src"), lax.axis_size("tgt")
    rows, depth = source_embed.shape
    width = target_feat.shape[1]
    share, half, chips = rows // n_tgt, rows // 2, n_tgt // 2
    src_mass = source_mass.reshape(-1, LANES)
    tgt_mass = target_mass.reshape(-1, LANES)
    src_rows, tgt_rows = src_mass.shape[0], tgt_mass.shape[0]
    to_src = shape((n_src, tgt_rows, LANES), f32)
    to_tgt = shape((n_tgt, src_rows, LANES), f32)
    by_src = scratch(source_embed, target_embed)
    by_tgt = scratch(target_embed, source_embed)
    far_chip = chips // 2 + math.isqrt(chips) // 2
    same_core = [[2 * chip + core for chip in rotated(chips, far_chip)] for core in range(2)]
    swap = [(index, index ^ 1) for index in range(n_tgt)]

    sems = [pltpu.SemaphoreType.DMA((rows // SLAB,)), pltpu.SemaphoreType.DMA((3,))]
    inputs = [
        pltpu.with_memory_space_constraint(array, pltpu.HBM)
        for array in (source_embed, target_embed, src_mass, tgt_mass)
    ]
    held = [shape(array.shape, array.dtype) for array in inputs]
    sent, source_embed, target_embed, src_log, tgt_log = call(
        first_kernel,
        inputs,
        (to_src, *held),
        sems + by_src,
        [pl.BlockSpec(memory_space=pltpu.HBM)] * len(inputs),
    )
    parts = lax.all_to_all(sent, "src", 0, 0, axis_index_groups=[by_distance(n_src, n_src // 2)])
    sent = call(next_kernel, (parts, tgt_log, target_embed, source_embed), to_tgt, by_tgt)
    parts = lax.all_to_all(sent, "tgt", 0, 0, axis_index_groups=[rotated(n_tgt, 2 * far_chip + 1)])
    sent = call(next_kernel, (parts, src_log, source_embed, target_embed), to_src, by_src)
    parts = lax.all_to_all(sent, "src", 0, 0, axis_index_groups=[by_distance(n_src, 0)])
    sent, keep, own, bias, turned = call(
        last_kernel,
        (parts, tgt_log, target_embed, source_embed.reshape(chips, 2, share, depth), target_feat),
        (
            shape((width + 8, half), f32),
            shape((target_embed.shape[0], half), jnp.bfloat16),
            shape((8, half), f32),
            shape((tgt_rows, LANES), f32),
            shape(target_feat.shape[::-1], jnp.bfloat16),
        ),
        by_tgt[:2] + by_tgt[1:2],
    )
    came = lax.ppermute(sent, "tgt", swap)
    mean, target_pot, base = call(
        own_kernel,
        (keep, own, turned, bias, target_embed, source_embed, src_log),
        (shape((width, half), f32), shape(bias.shape, f32), shape(src_log.shape, f32)),
        [],
    )
    sent = call(
        functools.partial(pair_kernel, far_chip),
        (mean, own, came),
        shape((chips, share + src_rows, LANES), f32),
        [pltpu.VMEM((src_rows, LANES), f32)],
    )
    landed = lax.all_to_all(sent, "tgt", 0, 0, axis_index_groups=same_core)
    source_pot, projected = call(
        final_kernel,
        (landed, base),
        (shape((src_rows, LANES), f32), shape((share, width), f32)),
        [],
    )
    return (source_pot.reshape(-1), target_pot.reshape(-1), projected)


def solution(mesh):
    placed = (P("src", None), P("tgt", None), P("tgt", None), P("src"), P("tgt"))
    return jax.shard_map(
        local,
        mesh=mesh,
        in_specs=placed,
        out_specs=(P("src"), P("tgt"), P(("src", "tgt"), None)),
        check_vma=False,
    )
```

```python
import functools
import math

import jax
import jax.numpy as jnp
from jax import lax
from jax.experimental import pallas as pl
from jax.experimental.pallas import tpu as pltpu
from jax.sharding import PartitionSpec as P

ENTROPY = 0.05
LANES = 128
WIDTH = 256
ONE_SCALE = 1.0 / ENTROPY * math.log2(math.e)
TWO_SCALE = 2.0 * ONE_SCALE
ONE_UNIT = ENTROPY * math.log(2.0)
LOWEST, HIGHEST = 2.0**-90, 2.0**110
NT = (((1,), (1,)), ((), ()))
NN = (((1,), (0,)), ((), ()))
HALVES = WIDTH // LANES
SLAB = 512
ACCUMULATE = 32
VMEM_LIMIT = 40 * 1024 * 1024


def merge(parts):
    top = jnp.max(parts, axis=0)
    total = jnp.sum(jnp.exp2((parts - top[None]) * ONE_SCALE), axis=0)
    return top + ENTROPY * jnp.log(total)


def lanes_to_rows(values, col_ref):
    for k in range(values.shape[0]):
        square = jnp.broadcast_to(values[k : k + 1, :], (LANES, LANES))
        col_ref[pl.ds(k * LANES, LANES), :] = square.T


def fold(reduce, part):
    return reduce(part.reshape(-1, ACCUMULATE, LANES), axis=0)


def exponents(p_ref, q, col_ref, s, rows=SLAB):
    slab = pl.ds(s * rows, rows)
    cross = lax.dot_general(p_ref[slab, :], q, NT, preferred_element_type=jnp.float32)
    col = col_ref[slab, :]
    return [cross[:, h * LANES : (h + 1) * LANES] * TWO_SCALE + col for h in range(HALVES)]


def scores(p_ref, q, col_ref, z_ref, s, rows=SLAB):
    slab = pl.ds(s * rows, rows)
    tops = []
    for h, part in enumerate(exponents(p_ref, q, col_ref, s, rows)):
        z_ref[slab, pl.ds(h * LANES, LANES)] = part
        tops.append(fold(jnp.max, part))
    return tops


def weigh(z_ref, tops, s, rows=SLAB):
    slab = pl.ds(s * rows, rows)
    weights, totals = [], []
    for h, top in enumerate(tops):
        part = z_ref[slab, pl.ds(h * LANES, LANES)]
        weight = jnp.exp2(part - top)
        weights.append(weight)
        totals.append(fold(jnp.sum, weight))
    return weights, totals


def join(op, held, more):
    return more if held is None else [op(a, b) for a, b in zip(held, more)]


def settle(reduce, values):
    return [reduce(value, axis=0, keepdims=True) for value in values]


def log_sum(top, total):
    return ONE_UNIT * top + ENTROPY * jnp.log(total)


def run_chunks(p_ref, chunk, chunks, col_ref, z_refs, emit, rows=SLAB):
    slabs = p_ref.shape[0] // rows
    tops = None
    for t in range(chunks + 1):
        q = chunk(t) if t < chunks else None
        later, totals, weights = None, None, []
        for s in range(slabs):
            if t < chunks:
                later = join(jnp.maximum, later, scores(p_ref, q, col_ref, z_refs[t % 2], s, rows))
            if t > 0:
                weight, total = weigh(z_refs[(t - 1) % 2], tops, s, rows)
                totals = join(jnp.add, totals, total)
                weights.append(weight)
        if t > 0:
            emit(t - 1, tops, settle(jnp.sum, totals), weights)
        if t < chunks:
            tops = settle(jnp.max, later)


def log_sums(p_ref, q_ref, col_ref, z_ref, row_ref, out_ref, rows=2 * SLAB):
    slabs, chunks = p_ref.shape[0] // SLAB, q_ref.shape[0] // WIDTH
    totals = [None] * chunks
    for s in range(p_ref.shape[0] // rows):
        for t in range(chunks):
            parts = exponents(p_ref, q_ref[pl.ds(t * WIDTH, WIDTH), :], col_ref, s, rows)
            totals[t] = join(jnp.add, totals[t], [fold(jnp.sum, jnp.exp2(part)) for part in parts])
    for t in range(chunks):
        for h, total in enumerate(settle(jnp.sum, totals[t])):
            row_ref[pl.ds(t * HALVES + h, 1), :] = total
    sums = row_ref[...]
    out_ref[...] = jnp.broadcast_to((ENTROPY * jnp.log(sums))[None], out_ref.shape)
    safe = jnp.logical_and(jnp.min(sums) >= LOWEST, jnp.max(sums) <= HIGHEST)

    @pl.when(jnp.logical_not(safe))
    def _():
        @pl.loop(0, chunks)
        def _(t):
            q = q_ref[pl.ds(pl.multiple_of(t * WIDTH, WIDTH), WIDTH), :]
            tops, sums = None, None
            for s in range(slabs):
                tops = join(jnp.maximum, tops, scores(p_ref, q, col_ref, z_ref, s))
            tops = settle(jnp.max, tops)
            for s in range(slabs):
                sums = join(jnp.add, sums, weigh(z_ref, tops, s)[1])
            for h, pair in enumerate(zip(tops, settle(jnp.sum, sums))):
                row_ref[pl.ds(t * HALVES + h, 1), :] = log_sum(*pair)

        out_ref[...] = jnp.broadcast_to(row_ref[...][None], out_ref.shape)


def first_kernel(
    p_hbm, q_hbm, p_mass_hbm, q_mass_hbm, out_ref, p_ref, q_ref, p_log_ref, q_log_ref,
    p_sems, sems, col_ref, z_ref, row_ref,
):
    loads = []
    for s in range(p_ref.shape[0] // SLAB):
        slab = pl.ds(s * SLAB, SLAB)
        loads.append(pltpu.make_async_copy(p_hbm.at[slab, :], p_ref.at[slab, :], p_sems.at[s]))
    load_q = pltpu.make_async_copy(q_hbm, q_ref, sems.at[0])
    masses = [
        pltpu.make_async_copy(p_mass_hbm, p_log_ref, sems.at[1]),
        pltpu.make_async_copy(q_mass_hbm, q_log_ref, sems.at[2]),
    ]
    for copy in loads + [load_q] + masses:
        copy.start()
    for s, copy in enumerate(loads):
        copy.wait()
        slab = pl.ds(s * SLAB, SLAB)
        p = p_ref[slab, :].astype(jnp.float32)
        norms = jnp.sum(p * p, axis=1, keepdims=True)
        col_ref[slab, :] = jnp.broadcast_to(-ONE_SCALE * norms, (SLAB, LANES))
    for copy in masses + [load_q]:
        copy.wait()
    p_log_ref[...] = ENTROPY * jnp.log(p_log_ref[...])
    q_log_ref[...] = ENTROPY * jnp.log(q_log_ref[...])
    log_sums(p_ref, q_ref, col_ref, z_ref, row_ref, out_ref)


def next_kernel(parts_ref, log_ref, p_ref, q_ref, out_ref, col_ref, z_ref, row_ref):
    lanes_to_rows(ONE_SCALE * (log_ref[...] - merge(parts_ref[...])), col_ref)
    log_sums(p_ref, q_ref, col_ref, z_ref, row_ref, out_ref)


def last_kernel(
    parts_ref, log_ref, p_ref, q_ref, feat_ref,
    sent_ref, keep_ref, own_ref, bias_ref, flip_ref, col_ref, even_ref, odd_ref,
):
    core = lax.rem(lax.axis_index("tgt"), 2)
    chips, _, share, depth = q_ref.shape
    half = chips * share
    width = feat_ref.shape[1]
    blocks = WIDTH // share
    bias = log_ref[...] - merge(parts_ref[...])
    bias_ref[...] = bias
    lanes_to_rows(ONE_SCALE * bias, col_ref)
    flip_ref[...] = feat_ref[...].astype(jnp.float32).T.astype(jnp.bfloat16)
    sent_ref[pl.ds(width, 8), :] = jnp.zeros((8, half), jnp.float32)
    own_ref[...] = jnp.zeros((8, half), jnp.float32)

    def chunk(t):
        own, first = divmod(t * WIDTH, half)
        q = q_ref[pl.ds(first // share, blocks), core if own else 1 - core]
        return q.reshape(WIDTH, depth)

    def emit(t, tops, totals, weights):
        own, first = divmod(t * WIDTH, half)
        slabs = [
            jnp.concatenate([weight.astype(jnp.bfloat16) for weight in slab], axis=1)
            for slab in weights
        ]
        lanes = pl.ds(first, WIDTH)
        lse = jnp.concatenate([log_sum(*pair) for pair in zip(tops, totals)], axis=1)
        scale = 1.0 / jnp.concatenate(totals, axis=1)
        sent_ref[pl.ds(width + own, 1), lanes] = lse
        own_ref[pl.ds(own, 1), lanes] = lse
        if own:
            for s, slab in enumerate(slabs):
                keep_ref[pl.ds(s * slab.shape[0], slab.shape[0]), lanes] = slab
            own_ref[pl.ds(2, 1), lanes] = scale
        else:
            weight = jnp.concatenate(slabs, axis=0)
            numer = lax.dot_general(
                flip_ref[...], weight, NN, preferred_element_type=jnp.float32
            )
            sent_ref[pl.ds(0, width), lanes] = numer * scale

    run_chunks(p_ref, chunk, 2 * half // WIDTH, col_ref, (even_ref, odd_ref), emit)


def squares(ref, k):
    rows = ref[pl.ds(k * LANES, LANES), :].astype(jnp.float32)
    norms = jnp.sum(rows * rows, axis=1, keepdims=True)
    return jnp.broadcast_to(norms, (LANES, LANES)).T[:1, :]


def own_kernel(
    keep_ref, own_ref, flip_ref, bias_ref, p_ref, q_ref, log_ref, mean_ref, pot_ref, base_ref
):
    numer = lax.dot_general(
        flip_ref[...], keep_ref[...], NN, preferred_element_type=jnp.float32
    )
    mean_ref[...] = numer * own_ref[pl.ds(2, 1), :]
    for k in range(pot_ref.shape[0]):
        row = pl.ds(k, 1)
        pot_ref[row, :] = bias_ref[row, :] + squares(p_ref, k)
    for k in range(base_ref.shape[0]):
        row = pl.ds(k, 1)
        base_ref[row, :] = log_ref[row, :] + squares(q_ref, k)


def pair_kernel(far_chip, mean_ref, own_ref, came_ref, out_ref, row_ref):
    width, half = mean_ref.shape
    chips = out_ref.shape[0]
    share = half // chips
    rows = half // LANES
    for side in range(2):
        mine = own_ref[pl.ds(1 - side, 1), :]
        other = came_ref[pl.ds(width + side, 1), :]
        top = jnp.maximum(mine, other)
        mine_share = jnp.exp2((mine - top) * ONE_SCALE)
        other_share = jnp.exp2((other - top) * ONE_SCALE)
        total = mine_share + other_share
        lse = top + ENTROPY * jnp.log(total)
        for k in range(rows):
            row_ref[pl.ds(side * rows + k, 1), :] = lse[:, k * LANES : (k + 1) * LANES]
        if side == 0:
            scale = 1.0 / total
            mine_share, other_share = mine_share * scale, other_share * scale
            step = LANES // share
            for k in range(rows):
                lanes = slice(k * LANES, (k + 1) * LANES)
                block = (
                    mean_ref[:, lanes] * mine_share[:, lanes]
                    + came_ref[pl.ds(0, width), lanes] * other_share[:, lanes]
                )
                place = (k * step - far_chip) % chips
                out_ref[pl.ds(place, step), pl.ds(0, share), :] = block.T.reshape(
                    step, share, LANES
                )
    out_ref[:, pl.ds(share, 2 * rows), :] = jnp.broadcast_to(
        row_ref[...][None], (chips, 2 * rows, LANES)
    )


def final_kernel(landed_ref, base_ref, pot_ref, out_ref):
    index = lax.axis_index("tgt")
    core, chip = lax.rem(index, 2), lax.div(index, 2)
    share = out_ref.shape[0]
    chips = landed_ref.shape[0]
    mine = landed_ref[:, pl.ds(share + lax.div(chip, 2), 1), :].reshape(chips, LANES)
    mine = jnp.exp2((mine - jnp.max(mine, axis=0, keepdims=True)) * ONE_SCALE)
    mine = mine / jnp.sum(mine, axis=0, keepdims=True)
    mine = jnp.where(lax.rem(chip, 2) == 0, mine, pltpu.roll(mine, share, 1))
    mine = jnp.concatenate([mine, jnp.zeros((LANES - chips, LANES), jnp.float32)], axis=0).T
    total = jnp.zeros(out_ref.shape, jnp.float32)
    for b in range(chips):
        scale = jnp.broadcast_to(mine[:share, b : b + 1], out_ref.shape)
        total = total + landed_ref[b, pl.ds(0, share), :] * scale
    out_ref[...] = total
    whole = merge(landed_ref[:, pl.ds(share, landed_ref.shape[1] - share), :])
    rows = whole.shape[0] // 2
    even = jnp.where(core == 0, whole[:rows], whole[rows:])
    odd = jnp.where(core == 0, whole[rows:], whole[:rows])
    lane = lax.broadcasted_iota(jnp.int32, (rows, LANES), 1)
    first = jnp.where(lane < share, even, pltpu.roll(odd, share, 1))
    second = jnp.where(lane < share, pltpu.roll(even, share, 1), odd)
    for k in range(rows):
        for side, values in enumerate((first, second)):
            row = pl.ds(2 * k + side, 1)
            pot_ref[row, :] = base_ref[row, :] - values[k : k + 1]


def rotated(n, first):
    return [(first + place) % n for place in range(n)]


def near_first(n):
    return [n // 2] + sorted(set(range(n)) - {n // 2}, key=lambda place: min(place, n - place))


def scratch(p, q):
    return [
        pltpu.VMEM((p.shape[0], LANES), jnp.float32),
        pltpu.VMEM((p.shape[0], WIDTH), jnp.float32),
        pltpu.VMEM((q.shape[0] // LANES, LANES), jnp.float32),
    ]


def call(kernel, args, outs, scratch_shapes, spaces=None):
    whole = pl.BlockSpec(memory_space=pltpu.VMEM)
    return pl.pallas_call(
        kernel,
        out_shape=outs,
        in_specs=spaces or [whole] * len(args),
        out_specs=jax.tree.map(lambda _: whole, outs),
        scratch_shapes=scratch_shapes,
        compiler_params=pltpu.CompilerParams(vmem_limit_bytes=VMEM_LIMIT),
    )(*args)


def local(source_embed, target_embed, target_feat, source_mass, target_mass):
    f32 = jnp.float32
    shape = jax.ShapeDtypeStruct
    n_src, n_tgt = lax.axis_size("src"), lax.axis_size("tgt")
    rows, depth = source_embed.shape
    width = target_feat.shape[1]
    share, half, chips = rows // n_tgt, rows // 2, n_tgt // 2
    src_mass = source_mass.reshape(-1, LANES)
    tgt_mass = target_mass.reshape(-1, LANES)
    src_rows, tgt_rows = src_mass.shape[0], tgt_mass.shape[0]
    to_src = shape((n_src, tgt_rows, LANES), f32)
    to_tgt = shape((n_tgt, src_rows, LANES), f32)
    by_src = scratch(source_embed, target_embed)
    by_tgt = scratch(target_embed, source_embed)
    far_chip = chips // 2 + math.isqrt(chips) // 2
    same_core = [[2 * chip + core for chip in rotated(chips, far_chip)] for core in range(2)]
    swap = [(index, index ^ 1) for index in range(n_tgt)]

    sems = [pltpu.SemaphoreType.DMA((rows // SLAB,)), pltpu.SemaphoreType.DMA((3,))]
    inputs = [
        pltpu.with_memory_space_constraint(array, pltpu.HBM)
        for array in (source_embed, target_embed, src_mass, tgt_mass)
    ]
    held = [shape(array.shape, array.dtype) for array in inputs]
    sent, source_embed, target_embed, src_log, tgt_log = call(
        first_kernel,
        inputs,
        (to_src, *held),
        sems + by_src,
        [pl.BlockSpec(memory_space=pltpu.HBM)] * len(inputs),
    )
    parts = lax.all_to_all(sent, "src", 0, 0, axis_index_groups=[rotated(n_src, n_src // 2)])
    sent = call(next_kernel, (parts, tgt_log, target_embed, source_embed), to_tgt, by_tgt)
    parts = lax.all_to_all(sent, "tgt", 0, 0, axis_index_groups=[rotated(n_tgt, 2 * far_chip + 1)])
    sent = call(next_kernel, (parts, src_log, source_embed, target_embed), to_src, by_src)
    parts = lax.all_to_all(sent, "src", 0, 0, axis_index_groups=[near_first(n_src)])
    sent, keep, own, bias, turned = call(
        last_kernel,
        (parts, tgt_log, target_embed, source_embed.reshape(chips, 2, share, depth), target_feat),
        (
            shape((width + 8, half), f32),
            shape((target_embed.shape[0], half), jnp.bfloat16),
            shape((8, half), f32),
            shape((tgt_rows, LANES), f32),
            shape(target_feat.shape[::-1], jnp.bfloat16),
        ),
        by_tgt[:2] + by_tgt[1:2],
    )
    came = lax.ppermute(sent, "tgt", swap)
    mean, target_pot, base = call(
        own_kernel,
        (keep, own, turned, bias, target_embed, source_embed, src_log),
        (shape((width, half), f32), shape(bias.shape, f32), shape(src_log.shape, f32)),
        [],
    )
    sent = call(
        functools.partial(pair_kernel, far_chip),
        (mean, own, came),
        shape((chips, share + src_rows, LANES), f32),
        [pltpu.VMEM((src_rows, LANES), f32)],
    )
    landed = lax.all_to_all(sent, "tgt", 0, 0, axis_index_groups=same_core)
    source_pot, projected = call(
        final_kernel,
        (landed, base),
        (shape((src_rows, LANES), f32), shape((share, width), f32)),
        [],
    )
    return (source_pot.reshape(-1), target_pot.reshape(-1), projected)


def solution(mesh):
    placed = (P("src", None), P("tgt", None), P("tgt", None), P("src"), P("tgt"))
    return jax.shard_map(
        local,
        mesh=mesh,
        in_specs=placed,
        out_specs=(P("src"), P("tgt"), P(("src", "tgt"), None)),
        check_vma=False,
    )
```

```python
import functools
import math

import jax
import jax.numpy as jnp
from jax import lax
from jax.experimental import pallas as pl
from jax.experimental.pallas import tpu as pltpu
from jax.sharding import PartitionSpec as P

ENTROPY = 0.05
LANES = 128
WIDTH = 256
ONE_SCALE = 1.0 / ENTROPY * math.log2(math.e)
TWO_SCALE = 2.0 * ONE_SCALE
ONE_UNIT = ENTROPY * math.log(2.0)
LOWEST, HIGHEST = 2.0**-90, 2.0**110
NT = (((1,), (1,)), ((), ()))
NN = (((1,), (0,)), ((), ()))
HALVES = WIDTH // LANES
SLAB = 512
ACCUMULATE = 32
VMEM_LIMIT = 40 * 1024 * 1024


def merge(parts):
    top = jnp.max(parts, axis=0)
    total = jnp.sum(jnp.exp2((parts - top[None]) * ONE_SCALE), axis=0)
    return top + ENTROPY * jnp.log(total)


def lanes_to_rows(values, col_ref):
    for k in range(values.shape[0]):
        square = jnp.broadcast_to(values[k : k + 1, :], (LANES, LANES))
        col_ref[pl.ds(k * LANES, LANES), :] = square.T


def fold(reduce, part):
    return reduce(part.reshape(-1, ACCUMULATE, LANES), axis=0)


def exponents(p_ref, q, col_ref, s, rows=SLAB):
    slab = pl.ds(s * rows, rows)
    cross = lax.dot_general(p_ref[slab, :], q, NT, preferred_element_type=jnp.float32)
    col = col_ref[slab, :]
    return [cross[:, h * LANES : (h + 1) * LANES] * TWO_SCALE + col for h in range(HALVES)]


def scores(p_ref, q, col_ref, z_ref, s, rows=SLAB):
    slab = pl.ds(s * rows, rows)
    tops = []
    for h, part in enumerate(exponents(p_ref, q, col_ref, s, rows)):
        z_ref[slab, pl.ds(h * LANES, LANES)] = part
        tops.append(fold(jnp.max, part))
    return tops


def weigh(z_ref, tops, s, rows=SLAB):
    slab = pl.ds(s * rows, rows)
    weights, totals = [], []
    for h, top in enumerate(tops):
        part = z_ref[slab, pl.ds(h * LANES, LANES)]
        weight = jnp.exp2(part - top)
        weights.append(weight)
        totals.append(fold(jnp.sum, weight))
    return weights, totals


def join(op, held, more):
    return more if held is None else [op(a, b) for a, b in zip(held, more)]


def settle(reduce, values):
    return [reduce(value, axis=0, keepdims=True) for value in values]


def log_sum(top, total):
    return ONE_UNIT * top + ENTROPY * jnp.log(total)


def run_chunks(p_ref, chunk, chunks, col_ref, z_refs, emit, rows=SLAB):
    slabs = p_ref.shape[0] // rows
    tops = None
    for t in range(chunks + 1):
        q = chunk(t) if t < chunks else None
        later, totals, weights = None, None, []
        for s in range(slabs):
            if t < chunks:
                later = join(jnp.maximum, later, scores(p_ref, q, col_ref, z_refs[t % 2], s, rows))
            if t > 0:
                weight, total = weigh(z_refs[(t - 1) % 2], tops, s, rows)
                totals = join(jnp.add, totals, total)
                weights.append(weight)
        if t > 0:
            emit(t - 1, tops, settle(jnp.sum, totals), weights)
        if t < chunks:
            tops = settle(jnp.max, later)


def log_sums(p_ref, q_ref, col_ref, z_ref, row_ref, out_ref, rows=2 * SLAB):
    slabs, chunks = p_ref.shape[0] // SLAB, q_ref.shape[0] // WIDTH
    totals = [None] * chunks
    for s in range(p_ref.shape[0] // rows):
        for t in range(chunks):
            parts = exponents(p_ref, q_ref[pl.ds(t * WIDTH, WIDTH), :], col_ref, s, rows)
            totals[t] = join(jnp.add, totals[t], [fold(jnp.sum, jnp.exp2(part)) for part in parts])
    for t in range(chunks):
        for h, total in enumerate(settle(jnp.sum, totals[t])):
            row_ref[pl.ds(t * HALVES + h, 1), :] = total
    sums = row_ref[...]
    out_ref[...] = jnp.broadcast_to((ENTROPY * jnp.log(sums))[None], out_ref.shape)
    safe = jnp.logical_and(jnp.min(sums) >= LOWEST, jnp.max(sums) <= HIGHEST)

    @pl.when(jnp.logical_not(safe))
    def _():
        @pl.loop(0, chunks)
        def _(t):
            q = q_ref[pl.ds(pl.multiple_of(t * WIDTH, WIDTH), WIDTH), :]
            tops, sums = None, None
            for s in range(slabs):
                tops = join(jnp.maximum, tops, scores(p_ref, q, col_ref, z_ref, s))
            tops = settle(jnp.max, tops)
            for s in range(slabs):
                sums = join(jnp.add, sums, weigh(z_ref, tops, s)[1])
            for h, pair in enumerate(zip(tops, settle(jnp.sum, sums))):
                row_ref[pl.ds(t * HALVES + h, 1), :] = log_sum(*pair)

        out_ref[...] = jnp.broadcast_to(row_ref[...][None], out_ref.shape)


def first_kernel(
    p_hbm, q_hbm, p_mass_hbm, q_mass_hbm, out_ref, p_ref, q_ref, p_log_ref, q_log_ref,
    p_sems, sems, col_ref, z_ref, row_ref,
):
    loads = []
    for s in range(p_ref.shape[0] // SLAB):
        slab = pl.ds(s * SLAB, SLAB)
        loads.append(pltpu.make_async_copy(p_hbm.at[slab, :], p_ref.at[slab, :], p_sems.at[s]))
    load_q = pltpu.make_async_copy(q_hbm, q_ref, sems.at[0])
    masses = [
        pltpu.make_async_copy(p_mass_hbm, p_log_ref, sems.at[1]),
        pltpu.make_async_copy(q_mass_hbm, q_log_ref, sems.at[2]),
    ]
    for copy in loads + [load_q] + masses:
        copy.start()
    for s, copy in enumerate(loads):
        copy.wait()
        slab = pl.ds(s * SLAB, SLAB)
        p = p_ref[slab, :].astype(jnp.float32)
        norms = jnp.sum(p * p, axis=1, keepdims=True)
        col_ref[slab, :] = jnp.broadcast_to(-ONE_SCALE * norms, (SLAB, LANES))
    for copy in masses + [load_q]:
        copy.wait()
    p_log_ref[...] = ENTROPY * jnp.log(p_log_ref[...])
    q_log_ref[...] = ENTROPY * jnp.log(q_log_ref[...])
    log_sums(p_ref, q_ref, col_ref, z_ref, row_ref, out_ref)


def next_kernel(parts_ref, log_ref, p_ref, q_ref, out_ref, col_ref, z_ref, row_ref):
    lanes_to_rows(ONE_SCALE * (log_ref[...] - merge(parts_ref[...])), col_ref)
    log_sums(p_ref, q_ref, col_ref, z_ref, row_ref, out_ref)


def write_norms(ref, out_ref, first):
    for k in range(ref.shape[0] // LANES):
        rows = ref[pl.ds(k * LANES, LANES), :].astype(jnp.float32)
        norms = jnp.sum(rows * rows, axis=1, keepdims=True)
        out_ref[pl.ds(first + k, 1), :] = jnp.broadcast_to(norms, (LANES, LANES)).T[:1, :]


def norm_kernel(
    parts_ref, log_ref, p_ref, q_ref, out_ref, norms_ref, col_ref, z_ref, row_ref
):
    next_kernel(parts_ref, log_ref, p_ref, q_ref, out_ref, col_ref, z_ref, row_ref)

    @pl.when(lax.rem(lax.axis_index("tgt"), 2) == 1)
    def _():
        write_norms(p_ref, norms_ref, 0)
        write_norms(q_ref, norms_ref, p_ref.shape[0] // LANES)


def last_kernel(
    parts_ref, log_ref, p_ref, q_ref, feat_ref,
    sent_ref, keep_ref, own_ref, bias_ref, flip_ref, col_ref, even_ref, odd_ref,
):
    core = lax.rem(lax.axis_index("tgt"), 2)
    chips, _, share, depth = q_ref.shape
    half = chips * share
    width = feat_ref.shape[1]
    blocks = WIDTH // share
    bias = log_ref[...] - merge(parts_ref[...])
    bias_ref[...] = bias
    lanes_to_rows(ONE_SCALE * bias, col_ref)
    flip_ref[...] = feat_ref[...].astype(jnp.float32).T.astype(jnp.bfloat16)
    sent_ref[pl.ds(width, 8), :] = jnp.zeros((8, half), jnp.float32)
    own_ref[...] = jnp.zeros((8, half), jnp.float32)

    def chunk(t):
        own, first = divmod(t * WIDTH, half)
        q = q_ref[pl.ds(first // share, blocks), core if own else 1 - core]
        return q.reshape(WIDTH, depth)

    def emit(t, tops, totals, weights):
        own, first = divmod(t * WIDTH, half)
        slabs = [
            jnp.concatenate([weight.astype(jnp.bfloat16) for weight in slab], axis=1)
            for slab in weights
        ]
        lanes = pl.ds(first, WIDTH)
        lse = jnp.concatenate([log_sum(*pair) for pair in zip(tops, totals)], axis=1)
        scale = 1.0 / jnp.concatenate(totals, axis=1)
        sent_ref[pl.ds(width + own, 1), lanes] = lse
        own_ref[pl.ds(own, 1), lanes] = lse
        if own:
            for s, slab in enumerate(slabs):
                keep_ref[pl.ds(s * slab.shape[0], slab.shape[0]), lanes] = slab
            own_ref[pl.ds(2, 1), lanes] = scale
        else:
            weight = jnp.concatenate(slabs, axis=0)
            numer = lax.dot_general(
                flip_ref[...], weight, NN, preferred_element_type=jnp.float32
            )
            sent_ref[pl.ds(0, width), lanes] = numer * scale

    run_chunks(p_ref, chunk, 2 * half // WIDTH, col_ref, (even_ref, odd_ref), emit)


def own_kernel(
    keep_ref, own_ref, flip_ref, bias_ref, norms_ref, p_ref, q_ref, log_ref,
    mean_ref, pot_ref, base_ref,
):
    numer = lax.dot_general(
        flip_ref[...], keep_ref[...], NN, preferred_element_type=jnp.float32
    )
    mean_ref[...] = numer * own_ref[pl.ds(2, 1), :]
    core = lax.rem(lax.axis_index("tgt"), 2)
    split = base_ref.shape[0]

    @pl.when(core == 0)
    def _():
        write_norms(q_ref, base_ref, 0)
        write_norms(p_ref, pot_ref, 0)

    @pl.when(core == 1)
    def _():
        base_ref[...] = norms_ref[:split]
        pot_ref[...] = norms_ref[split:]

    base_ref[...] += log_ref[...]
    pot_ref[...] += bias_ref[...]


def pair_kernel(far_chip, mean_ref, own_ref, came_ref, out_ref, row_ref):
    width, half = mean_ref.shape
    chips = out_ref.shape[0]
    share = half // chips
    rows = half // LANES
    for side in range(2):
        mine = own_ref[pl.ds(1 - side, 1), :]
        other = came_ref[pl.ds(width + side, 1), :]
        top = jnp.maximum(mine, other)
        mine_share = jnp.exp2((mine - top) * ONE_SCALE)
        other_share = jnp.exp2((other - top) * ONE_SCALE)
        total = mine_share + other_share
        lse = top + ENTROPY * jnp.log(total)
        for k in range(rows):
            row_ref[pl.ds(side * rows + k, 1), :] = lse[:, k * LANES : (k + 1) * LANES]
        if side == 0:
            scale = 1.0 / total
            mine_share, other_share = mine_share * scale, other_share * scale
            step = LANES // share
            for k in range(rows):
                lanes = slice(k * LANES, (k + 1) * LANES)
                block = (
                    mean_ref[:, lanes] * mine_share[:, lanes]
                    + came_ref[pl.ds(0, width), lanes] * other_share[:, lanes]
                )
                place = (k * step - far_chip) % chips
                out_ref[pl.ds(place, step), pl.ds(0, share), :] = block.T.reshape(
                    step, share, LANES
                )
    out_ref[:, pl.ds(share, 2 * rows), :] = jnp.broadcast_to(
        row_ref[...][None], (chips, 2 * rows, LANES)
    )


def final_kernel(landed_ref, base_ref, pot_ref, out_ref):
    index = lax.axis_index("tgt")
    core, chip = lax.rem(index, 2), lax.div(index, 2)
    share = out_ref.shape[0]
    chips = landed_ref.shape[0]
    mine = landed_ref[:, pl.ds(share + lax.div(chip, 2), 1), :].reshape(chips, LANES)
    mine = jnp.exp2((mine - jnp.max(mine, axis=0, keepdims=True)) * ONE_SCALE)
    mine = mine / jnp.sum(mine, axis=0, keepdims=True)
    mine = jnp.where(lax.rem(chip, 2) == 0, mine, pltpu.roll(mine, share, 1))
    mine = jnp.concatenate([mine, jnp.zeros((LANES - chips, LANES), jnp.float32)], axis=0).T
    total = jnp.zeros(out_ref.shape, jnp.float32)
    for b in range(chips):
        scale = jnp.broadcast_to(mine[:share, b : b + 1], out_ref.shape)
        total = total + landed_ref[b, pl.ds(0, share), :] * scale
    out_ref[...] = total
    whole = merge(landed_ref[:, pl.ds(share, landed_ref.shape[1] - share), :])
    rows = whole.shape[0] // 2
    even = jnp.where(core == 0, whole[:rows], whole[rows:])
    odd = jnp.where(core == 0, whole[rows:], whole[:rows])
    lane = lax.broadcasted_iota(jnp.int32, (rows, LANES), 1)
    first = jnp.where(lane < share, even, pltpu.roll(odd, share, 1))
    second = jnp.where(lane < share, pltpu.roll(even, share, 1), odd)
    for k in range(rows):
        for side, values in enumerate((first, second)):
            row = pl.ds(2 * k + side, 1)
            pot_ref[row, :] = base_ref[row, :] - values[k : k + 1]


def rotated(n, first):
    return [(first + place) % n for place in range(n)]


def near_first(n):
    return [n // 2] + sorted(set(range(n)) - {n // 2}, key=lambda place: min(place, n - place))


def scratch(p, q):
    return [
        pltpu.VMEM((p.shape[0], LANES), jnp.float32),
        pltpu.VMEM((p.shape[0], WIDTH), jnp.float32),
        pltpu.VMEM((q.shape[0] // LANES, LANES), jnp.float32),
    ]


def call(kernel, args, outs, scratch_shapes, spaces=None):
    whole = pl.BlockSpec(memory_space=pltpu.VMEM)
    return pl.pallas_call(
        kernel,
        out_shape=outs,
        in_specs=spaces or [whole] * len(args),
        out_specs=jax.tree.map(lambda _: whole, outs),
        scratch_shapes=scratch_shapes,
        compiler_params=pltpu.CompilerParams(vmem_limit_bytes=VMEM_LIMIT),
    )(*args)


def local(source_embed, target_embed, target_feat, source_mass, target_mass):
    f32 = jnp.float32
    shape = jax.ShapeDtypeStruct
    n_src, n_tgt = lax.axis_size("src"), lax.axis_size("tgt")
    rows, depth = source_embed.shape
    width = target_feat.shape[1]
    share, half, chips = rows // n_tgt, rows // 2, n_tgt // 2
    src_mass = source_mass.reshape(-1, LANES)
    tgt_mass = target_mass.reshape(-1, LANES)
    src_rows, tgt_rows = src_mass.shape[0], tgt_mass.shape[0]
    to_src = shape((n_src, tgt_rows, LANES), f32)
    to_tgt = shape((n_tgt, src_rows, LANES), f32)
    by_src = scratch(source_embed, target_embed)
    by_tgt = scratch(target_embed, source_embed)
    far_chip = chips // 2 + math.isqrt(chips) // 2
    same_core = [[2 * chip + core for chip in rotated(chips, far_chip)] for core in range(2)]
    swap = [(index, index ^ 1) for index in range(n_tgt)]

    sems = [pltpu.SemaphoreType.DMA((rows // SLAB,)), pltpu.SemaphoreType.DMA((3,))]
    inputs = [
        pltpu.with_memory_space_constraint(array, pltpu.HBM)
        for array in (source_embed, target_embed, src_mass, tgt_mass)
    ]
    held = [shape(array.shape, array.dtype) for array in inputs]
    sent, source_embed, target_embed, src_log, tgt_log = call(
        first_kernel,
        inputs,
        (to_src, *held),
        sems + by_src,
        [pl.BlockSpec(memory_space=pltpu.HBM)] * len(inputs),
    )
    parts = lax.all_to_all(sent, "src", 0, 0, axis_index_groups=[rotated(n_src, n_src // 2)])
    sent = call(next_kernel, (parts, tgt_log, target_embed, source_embed), to_tgt, by_tgt)
    parts = lax.all_to_all(sent, "tgt", 0, 0, axis_index_groups=[rotated(n_tgt, 2 * far_chip + 1)])
    sent, norms = call(
        norm_kernel,
        (parts, src_log, source_embed, target_embed),
        (to_src, shape((src_rows + tgt_rows, LANES), f32)),
        by_src,
    )
    parts = lax.all_to_all(sent, "src", 0, 0, axis_index_groups=[near_first(n_src)])
    sent, keep, own, bias, turned = call(
        last_kernel,
        (parts, tgt_log, target_embed, source_embed.reshape(chips, 2, share, depth), target_feat),
        (
            shape((width + 8, half), f32),
            shape((target_embed.shape[0], half), jnp.bfloat16),
            shape((8, half), f32),
            shape((tgt_rows, LANES), f32),
            shape(target_feat.shape[::-1], jnp.bfloat16),
        ),
        by_tgt[:2] + by_tgt[1:2],
    )
    came = lax.ppermute(sent, "tgt", swap)
    mean, target_pot, base = call(
        own_kernel,
        (keep, own, turned, bias, norms, target_embed, source_embed, src_log),
        (shape((width, half), f32), shape(bias.shape, f32), shape(src_log.shape, f32)),
        [],
    )
    sent = call(
        functools.partial(pair_kernel, far_chip),
        (mean, own, came),
        shape((chips, share + src_rows, LANES), f32),
        [pltpu.VMEM((src_rows, LANES), f32)],
    )
    landed = lax.all_to_all(sent, "tgt", 0, 0, axis_index_groups=same_core)
    source_pot, projected = call(
        final_kernel,
        (landed, base),
        (shape((src_rows, LANES), f32), shape((share, width), f32)),
        [],
    )
    return (source_pot.reshape(-1), target_pot.reshape(-1), projected)


def solution(mesh):
    placed = (P("src", None), P("tgt", None), P("tgt", None), P("src"), P("tgt"))
    return jax.shard_map(
        local,
        mesh=mesh,
        in_specs=placed,
        out_specs=(P("src"), P("tgt"), P(("src", "tgt"), None)),
        check_vma=False,
    )
```

```python
import functools
import math

import jax
import jax.numpy as jnp
from jax import lax
from jax.experimental import pallas as pl
from jax.experimental.pallas import tpu as pltpu
from jax.sharding import PartitionSpec as P

ENTROPY = 0.05
LANES = 128
WIDTH = 512
ONE_SCALE = 1.0 / ENTROPY * math.log2(math.e)
TWO_SCALE = 2.0 * ONE_SCALE
ONE_UNIT = ENTROPY * math.log(2.0)
LOWEST, HIGHEST = 2.0**-90, 2.0**110
NT = (((1,), (1,)), ((), ()))
NN = (((1,), (0,)), ((), ()))
HALVES = WIDTH // LANES
SLAB = 512
ACCUMULATE = 32
VMEM_LIMIT = 40 * 1024 * 1024


def merge(parts):
    top = jnp.max(parts, axis=0)
    total = jnp.sum(jnp.exp2((parts - top[None]) * ONE_SCALE), axis=0)
    return top + ENTROPY * jnp.log(total)


def lanes_to_rows(values, col_ref):
    for k in range(values.shape[0]):
        square = jnp.broadcast_to(values[k : k + 1, :], (LANES, LANES))
        col_ref[pl.ds(k * LANES, LANES), :] = square.T


def fold(reduce, part):
    return reduce(part.reshape(-1, ACCUMULATE, LANES), axis=0)


def exponents(p_ref, q, col_ref, s, rows=SLAB):
    slab = pl.ds(s * rows, rows)
    cross = lax.dot_general(p_ref[slab, :], q, NT, preferred_element_type=jnp.float32)
    col = col_ref[slab, :]
    return [cross[:, h * LANES : (h + 1) * LANES] * TWO_SCALE + col for h in range(HALVES)]


def scores(p_ref, q, col_ref, z_ref, s, rows=SLAB):
    slab = pl.ds(s * rows, rows)
    tops = []
    for h, part in enumerate(exponents(p_ref, q, col_ref, s, rows)):
        z_ref[slab, pl.ds(h * LANES, LANES)] = part
        tops.append(fold(jnp.max, part))
    return tops


def weigh(z_ref, tops, s, rows=SLAB):
    slab = pl.ds(s * rows, rows)
    weights, totals = [], []
    for h, top in enumerate(tops):
        part = z_ref[slab, pl.ds(h * LANES, LANES)]
        weight = jnp.exp2(part - top)
        weights.append(weight)
        totals.append(fold(jnp.sum, weight))
    return weights, totals


def join(op, held, more):
    return more if held is None else [op(a, b) for a, b in zip(held, more)]


def settle(reduce, values):
    return [reduce(value, axis=0, keepdims=True) for value in values]


def log_sum(top, total):
    return ONE_UNIT * top + ENTROPY * jnp.log(total)


def run_chunks(p_ref, chunk, chunks, col_ref, z_refs, emit, rows=SLAB):
    slabs = p_ref.shape[0] // rows
    tops = None
    for t in range(chunks + 1):
        q = chunk(t) if t < chunks else None
        later, totals, weights = None, None, []
        for s in range(slabs):
            if t < chunks:
                later = join(jnp.maximum, later, scores(p_ref, q, col_ref, z_refs[t % 2], s, rows))
            if t > 0:
                weight, total = weigh(z_refs[(t - 1) % 2], tops, s, rows)
                totals = join(jnp.add, totals, total)
                weights.append(weight)
        if t > 0:
            emit(t - 1, tops, settle(jnp.sum, totals), weights)
        if t < chunks:
            tops = settle(jnp.max, later)


def log_sums(p_ref, q_ref, col_ref, z_ref, row_ref, out_ref, rows=2 * SLAB):
    slabs, chunks = p_ref.shape[0] // SLAB, q_ref.shape[0] // WIDTH
    totals = [None] * chunks
    for s in range(p_ref.shape[0] // rows):
        for t in range(chunks):
            parts = exponents(p_ref, q_ref[pl.ds(t * WIDTH, WIDTH), :], col_ref, s, rows)
            totals[t] = join(jnp.add, totals[t], [fold(jnp.sum, jnp.exp2(part)) for part in parts])
    for t in range(chunks):
        for h, total in enumerate(settle(jnp.sum, totals[t])):
            row_ref[pl.ds(t * HALVES + h, 1), :] = total
    sums = row_ref[...]
    out_ref[...] = jnp.broadcast_to((ENTROPY * jnp.log(sums))[None], out_ref.shape)
    safe = jnp.logical_and(jnp.min(sums) >= LOWEST, jnp.max(sums) <= HIGHEST)

    @pl.when(jnp.logical_not(safe))
    def _():
        @pl.loop(0, chunks)
        def _(t):
            q = q_ref[pl.ds(pl.multiple_of(t * WIDTH, WIDTH), WIDTH), :]
            tops, sums = None, None
            for s in range(slabs):
                tops = join(jnp.maximum, tops, scores(p_ref, q, col_ref, z_ref, s))
            tops = settle(jnp.max, tops)
            for s in range(slabs):
                sums = join(jnp.add, sums, weigh(z_ref, tops, s)[1])
            for h, pair in enumerate(zip(tops, settle(jnp.sum, sums))):
                row_ref[pl.ds(t * HALVES + h, 1), :] = log_sum(*pair)

        out_ref[...] = jnp.broadcast_to(row_ref[...][None], out_ref.shape)


def first_kernel(
    p_hbm, q_hbm, p_mass_hbm, q_mass_hbm, out_ref, p_ref, q_ref, p_log_ref, q_log_ref,
    p_sems, sems, col_ref, z_ref, row_ref,
):
    loads = []
    for s in range(p_ref.shape[0] // SLAB):
        slab = pl.ds(s * SLAB, SLAB)
        loads.append(pltpu.make_async_copy(p_hbm.at[slab, :], p_ref.at[slab, :], p_sems.at[s]))
    load_q = pltpu.make_async_copy(q_hbm, q_ref, sems.at[0])
    masses = [
        pltpu.make_async_copy(p_mass_hbm, p_log_ref, sems.at[1]),
        pltpu.make_async_copy(q_mass_hbm, q_log_ref, sems.at[2]),
    ]
    for copy in loads + [load_q] + masses:
        copy.start()
    for s, copy in enumerate(loads):
        copy.wait()
        slab = pl.ds(s * SLAB, SLAB)
        p = p_ref[slab, :].astype(jnp.float32)
        norms = jnp.sum(p * p, axis=1, keepdims=True)
        col_ref[slab, :] = jnp.broadcast_to(-ONE_SCALE * norms, (SLAB, LANES))
    for copy in masses + [load_q]:
        copy.wait()
    p_log_ref[...] = ENTROPY * jnp.log(p_log_ref[...])
    q_log_ref[...] = ENTROPY * jnp.log(q_log_ref[...])
    log_sums(p_ref, q_ref, col_ref, z_ref, row_ref, out_ref)


def next_kernel(parts_ref, log_ref, p_ref, q_ref, out_ref, col_ref, z_ref, row_ref):
    lanes_to_rows(ONE_SCALE * (log_ref[...] - merge(parts_ref[...])), col_ref)
    log_sums(p_ref, q_ref, col_ref, z_ref, row_ref, out_ref)


def last_kernel(
    parts_ref, log_ref, p_ref, q_ref, feat_ref,
    sent_ref, keep_ref, own_ref, bias_ref, flip_ref, col_ref, even_ref, odd_ref,
):
    core = lax.rem(lax.axis_index("tgt"), 2)
    chips, _, share, depth = q_ref.shape
    half = chips * share
    width = feat_ref.shape[1]
    blocks = WIDTH // share
    bias = log_ref[...] - merge(parts_ref[...])
    bias_ref[...] = bias
    lanes_to_rows(ONE_SCALE * bias, col_ref)
    flip_ref[...] = feat_ref[...].astype(jnp.float32).T.astype(jnp.bfloat16)
    sent_ref[pl.ds(width, 8), :] = jnp.zeros((8, half), jnp.float32)
    own_ref[...] = jnp.zeros((8, half), jnp.float32)

    def chunk(t):
        own, first = divmod(t * WIDTH, half)
        q = q_ref[pl.ds(first // share, blocks), core if own else 1 - core]
        return q.reshape(WIDTH, depth)

    def emit(t, tops, totals, weights):
        own, first = divmod(t * WIDTH, half)
        slabs = [
            jnp.concatenate([weight.astype(jnp.bfloat16) for weight in slab], axis=1)
            for slab in weights
        ]
        lanes = pl.ds(first, WIDTH)
        lse = jnp.concatenate([log_sum(*pair) for pair in zip(tops, totals)], axis=1)
        scale = 1.0 / jnp.concatenate(totals, axis=1)
        sent_ref[pl.ds(width + own, 1), lanes] = lse
        own_ref[pl.ds(own, 1), lanes] = lse
        if own:
            for s, slab in enumerate(slabs):
                keep_ref[pl.ds(s * slab.shape[0], slab.shape[0]), lanes] = slab
            own_ref[pl.ds(2, 1), lanes] = scale
        else:
            weight = jnp.concatenate(slabs, axis=0)
            numer = lax.dot_general(
                flip_ref[...], weight, NN, preferred_element_type=jnp.float32
            )
            sent_ref[pl.ds(0, width), lanes] = numer * scale

    run_chunks(p_ref, chunk, 2 * half // WIDTH, col_ref, (even_ref, odd_ref), emit)


def squares(ref, k):
    rows = ref[pl.ds(k * LANES, LANES), :].astype(jnp.float32)
    norms = jnp.sum(rows * rows, axis=1, keepdims=True)
    return jnp.broadcast_to(norms, (LANES, LANES)).T[:1, :]


def own_kernel(
    keep_ref, own_ref, flip_ref, bias_ref, p_ref, q_ref, log_ref, mean_ref, pot_ref, base_ref
):
    numer = lax.dot_general(
        flip_ref[...], keep_ref[...], NN, preferred_element_type=jnp.float32
    )
    mean_ref[...] = numer * own_ref[pl.ds(2, 1), :]
    for k in range(pot_ref.shape[0]):
        row = pl.ds(k, 1)
        pot_ref[row, :] = bias_ref[row, :] + squares(p_ref, k)
    for k in range(base_ref.shape[0]):
        row = pl.ds(k, 1)
        base_ref[row, :] = log_ref[row, :] + squares(q_ref, k)


def pair_kernel(far_chip, mean_ref, own_ref, came_ref, out_ref, row_ref):
    width, half = mean_ref.shape
    chips = out_ref.shape[0]
    share = half // chips
    rows = half // LANES
    for side in range(2):
        mine = own_ref[pl.ds(1 - side, 1), :]
        other = came_ref[pl.ds(width + side, 1), :]
        top = jnp.maximum(mine, other)
        mine_share = jnp.exp2((mine - top) * ONE_SCALE)
        other_share = jnp.exp2((other - top) * ONE_SCALE)
        total = mine_share + other_share
        lse = top + ENTROPY * jnp.log(total)
        for k in range(rows):
            row_ref[pl.ds(side * rows + k, 1), :] = lse[:, k * LANES : (k + 1) * LANES]
        if side == 0:
            scale = 1.0 / total
            mine_share, other_share = mine_share * scale, other_share * scale
            step = LANES // share
            for k in range(rows):
                lanes = slice(k * LANES, (k + 1) * LANES)
                block = (
                    mean_ref[:, lanes] * mine_share[:, lanes]
                    + came_ref[pl.ds(0, width), lanes] * other_share[:, lanes]
                )
                place = (k * step - far_chip) % chips
                out_ref[pl.ds(place, step), pl.ds(0, share), :] = block.T.reshape(
                    step, share, LANES
                )
    out_ref[:, pl.ds(share, 2 * rows), :] = jnp.broadcast_to(
        row_ref[...][None], (chips, 2 * rows, LANES)
    )


def final_kernel(landed_ref, base_ref, pot_ref, out_ref):
    index = lax.axis_index("tgt")
    core, chip = lax.rem(index, 2), lax.div(index, 2)
    share = out_ref.shape[0]
    chips = landed_ref.shape[0]
    mine = landed_ref[:, pl.ds(share + lax.div(chip, 2), 1), :].reshape(chips, LANES)
    mine = jnp.exp2((mine - jnp.max(mine, axis=0, keepdims=True)) * ONE_SCALE)
    mine = mine / jnp.sum(mine, axis=0, keepdims=True)
    mine = jnp.where(lax.rem(chip, 2) == 0, mine, pltpu.roll(mine, share, 1))
    mine = jnp.concatenate([mine, jnp.zeros((LANES - chips, LANES), jnp.float32)], axis=0).T
    total = jnp.zeros(out_ref.shape, jnp.float32)
    for b in range(chips):
        scale = jnp.broadcast_to(mine[:share, b : b + 1], out_ref.shape)
        total = total + landed_ref[b, pl.ds(0, share), :] * scale
    out_ref[...] = total
    whole = merge(landed_ref[:, pl.ds(share, landed_ref.shape[1] - share), :])
    rows = whole.shape[0] // 2
    even = jnp.where(core == 0, whole[:rows], whole[rows:])
    odd = jnp.where(core == 0, whole[rows:], whole[:rows])
    lane = lax.broadcasted_iota(jnp.int32, (rows, LANES), 1)
    first = jnp.where(lane < share, even, pltpu.roll(odd, share, 1))
    second = jnp.where(lane < share, pltpu.roll(even, share, 1), odd)
    for k in range(rows):
        for side, values in enumerate((first, second)):
            row = pl.ds(2 * k + side, 1)
            pot_ref[row, :] = base_ref[row, :] - values[k : k + 1]


def rotated(n, first):
    return [(first + place) % n for place in range(n)]


def near_first(n):
    return [n // 2] + sorted(set(range(n)) - {n // 2}, key=lambda place: min(place, n - place))


def scratch(p, q):
    return [
        pltpu.VMEM((p.shape[0], LANES), jnp.float32),
        pltpu.VMEM((p.shape[0], WIDTH), jnp.float32),
        pltpu.VMEM((q.shape[0] // LANES, LANES), jnp.float32),
    ]


def call(kernel, args, outs, scratch_shapes, spaces=None):
    whole = pl.BlockSpec(memory_space=pltpu.VMEM)
    return pl.pallas_call(
        kernel,
        out_shape=outs,
        in_specs=spaces or [whole] * len(args),
        out_specs=jax.tree.map(lambda _: whole, outs),
        scratch_shapes=scratch_shapes,
        compiler_params=pltpu.CompilerParams(vmem_limit_bytes=VMEM_LIMIT),
    )(*args)


def local(source_embed, target_embed, target_feat, source_mass, target_mass):
    f32 = jnp.float32
    shape = jax.ShapeDtypeStruct
    n_src, n_tgt = lax.axis_size("src"), lax.axis_size("tgt")
    rows, depth = source_embed.shape
    width = target_feat.shape[1]
    share, half, chips = rows // n_tgt, rows // 2, n_tgt // 2
    src_mass = source_mass.reshape(-1, LANES)
    tgt_mass = target_mass.reshape(-1, LANES)
    src_rows, tgt_rows = src_mass.shape[0], tgt_mass.shape[0]
    to_src = shape((n_src, tgt_rows, LANES), f32)
    to_tgt = shape((n_tgt, src_rows, LANES), f32)
    by_src = scratch(source_embed, target_embed)
    by_tgt = scratch(target_embed, source_embed)
    far_chip = chips // 2 + math.isqrt(chips) // 2
    same_core = [[2 * chip + core for chip in rotated(chips, far_chip)] for core in range(2)]
    swap = [(index, index ^ 1) for index in range(n_tgt)]

    sems = [pltpu.SemaphoreType.DMA((rows // SLAB,)), pltpu.SemaphoreType.DMA((3,))]
    inputs = [
        pltpu.with_memory_space_constraint(array, pltpu.HBM)
        for array in (source_embed, target_embed, src_mass, tgt_mass)
    ]
    held = [shape(array.shape, array.dtype) for array in inputs]
    sent, source_embed, target_embed, src_log, tgt_log = call(
        first_kernel,
        inputs,
        (to_src, *held),
        sems + by_src,
        [pl.BlockSpec(memory_space=pltpu.HBM)] * len(inputs),
    )
    parts = lax.all_to_all(sent, "src", 0, 0, axis_index_groups=[rotated(n_src, n_src // 2)])
    sent = call(next_kernel, (parts, tgt_log, target_embed, source_embed), to_tgt, by_tgt)
    parts = lax.all_to_all(sent, "tgt", 0, 0, axis_index_groups=[rotated(n_tgt, 2 * far_chip + 1)])
    sent = call(next_kernel, (parts, src_log, source_embed, target_embed), to_src, by_src)
    parts = lax.all_to_all(sent, "src", 0, 0, axis_index_groups=[near_first(n_src)])
    sent, keep, own, bias, turned = call(
        last_kernel,
        (parts, tgt_log, target_embed, source_embed.reshape(chips, 2, share, depth), target_feat),
        (
            shape((width + 8, half), f32),
            shape((target_embed.shape[0], half), jnp.bfloat16),
            shape((8, half), f32),
            shape((tgt_rows, LANES), f32),
            shape(target_feat.shape[::-1], jnp.bfloat16),
        ),
        by_tgt[:2] + by_tgt[1:2],
    )
    came = lax.ppermute(sent, "tgt", swap)
    mean, target_pot, base = call(
        own_kernel,
        (keep, own, turned, bias, target_embed, source_embed, src_log),
        (shape((width, half), f32), shape(bias.shape, f32), shape(src_log.shape, f32)),
        [],
    )
    sent = call(
        functools.partial(pair_kernel, far_chip),
        (mean, own, came),
        shape((chips, share + src_rows, LANES), f32),
        [pltpu.VMEM((src_rows, LANES), f32)],
    )
    landed = lax.all_to_all(sent, "tgt", 0, 0, axis_index_groups=same_core)
    source_pot, projected = call(
        final_kernel,
        (landed, base),
        (shape((src_rows, LANES), f32), shape((share, width), f32)),
        [],
    )
    return (source_pot.reshape(-1), target_pot.reshape(-1), projected)


def solution(mesh):
    placed = (P("src", None), P("tgt", None), P("tgt", None), P("src"), P("tgt"))
    return jax.shard_map(
        local,
        mesh=mesh,
        in_specs=placed,
        out_specs=(P("src"), P("tgt"), P(("src", "tgt"), None)),
        check_vma=False,
    )
```
